32 devices in a mesh: feat: 4 (over x, core), batch: 8 (over z, y).
Axes of the slice: x: 2, y: 2, z: 4, core: 2. Of those that a mesh axis runs over, the one named last changes fastest.
Arguments:
- node_feats: bfloat16 [32768, 1024], P('batch', 'feat'), may hold values from -96 to 96
- seed_ids: int32 [2048], P('batch'), may hold values from 0 to 4095
- first_hop: int32 [2048, 10], P('batch'), may hold values from 0 to 4095
- second_hop: int32 [2048, 10, 15], P('batch'), may hold values from 0 to 4095
- lower_self: bfloat16 [1024, 256], P('feat'), may hold values from -0.1875 to 0.1875
- lower_neighbour: bfloat16 [1024, 256], P('feat'), may hold values from -0.1875 to 0.1875
- norm_gain: float32 [256], replicated, may hold values from 0.1 to 1.9
- norm_shift: float32 [256], replicated, may hold values from -3 to 3
- upper_self: bfloat16 [256, 256], replicated, may hold values from -0.375 to 0.375
- upper_neighbour: bfloat16 [256, 256], replicated, may hold values from -0.375 to 0.375
- embed_grad: bfloat16 [2048, 256], P(('batch', 'feat')), may hold values from -0.125 to 0.125
Outputs:
- embedding: bfloat16 [2048, 256], P(('batch', 'feat'))
- grad_lower_self: float32 [1024, 256], P('feat')
- grad_lower_neighbour: float32 [1024, 256], P('feat')
- grad_upper_self: float32 [256, 256], replicated
- grad_upper_neighbour: float32 [256, 256], replicated
- grad_gain: float32 [256], replicated
- grad_shift: float32 [256], replicated
The draws below stay inside these ranges and needn't reach their ends.
All inputs are finite; a program needn't handle non-finite values.
Results may differ from the reference program's by a relative error of at most 0.007.
Values may be sent and summed in bfloat16 or wider, within the bound.
No kernel may reach another device: no remote copies, remote signals or barrier semaphores. Data moves between devices by JAX's collectives and lax.ppermute only.
A program may use at most 64 MiB of HBM per device.

```python
import math
import jax
import jax.numpy as jnp
from jax import lax

D = 1024
H = 256
FAN1 = 10
FAN2 = 15
NODE_GRP = 4096
SEEDS = 2048
NODES = 32768
N_BATCH = 8


def draw_node_feats(key, part):
    key = jax.random.fold_in(key, 11)
    base_key, row_key, column_key = jax.random.split(key, 3)
    groups = NODES // NODE_GRP
    position = (jnp.arange(NODES) // NODE_GRP).astype(jnp.float32) / max(groups - 1, 1)
    base = jnp.clip(jax.random.normal(base_key, (NODES, D), jnp.float32), -4.0, 4.0)
    growth = math.log(3.0)
    row_span = math.log(4.0)
    row_scale = jnp.exp(jax.random.uniform(row_key, (NODES, 1), jnp.float32) * row_span)
    column_scale = jnp.exp(jax.random.uniform(column_key, (1, D), jnp.float32) * math.log(3.0))
    values = base * jnp.exp(position * growth)[:, None] * row_scale * column_scale / 3.0
    return values.astype(jnp.bfloat16)


def set_ends(values, stream_key, least, high):
    extent = values.shape
    spot = [jax.random.randint(jax.random.fold_in(stream_key, axis), (), 0, extent[axis]) for axis in range(len(extent))]
    values = values.at[tuple(spot)].set(least)
    longest = extent.index(max(extent))
    spot[longest] = (spot[longest] + 1) % extent[longest]
    return values.at[tuple(spot)].set(high)


def block_scale(stream_key, shape, shards, low, largest):
    level, own = 1.0, jax.random.fold_in(stream_key, 6)
    for dim, shards_of in shards:
        draws = jnp.exp(jax.random.uniform(jax.random.fold_in(own, dim), (shards_of,), jnp.float32, low / len(shards), largest / len(shards)))
        level = level * jnp.repeat(draws, shape[dim] // shards_of).reshape([-1 if axis == dim else 1 for axis in range(len(shape))])
    return level


def normal_values(key, extent, deviation, most, pieces=(), held_as=jnp.bfloat16):
    result = jax.random.normal(key, extent, jnp.float32) * deviation
    if len(pieces) > 0:
        result = block_scale(key, extent, pieces, -0.22, 0.18) * result
    return jnp.clip(result, min=-most, max=most).astype(held_as)


def setup_inputs(seed: int = 0) -> dict:
    keys = jax.random.split(jax.random.key(seed), 12)
    node_feats = draw_node_feats(jax.random.fold_in(keys[11], 71), 0)
    seed_ids = set_ends(jax.random.randint(keys[1], (SEEDS,), 0, NODE_GRP), jax.random.fold_in(keys[1], 1), 0, NODE_GRP - 1).astype(jnp.int32)
    first_hop = set_ends(jax.random.randint(keys[2], (SEEDS, FAN1), 0, NODE_GRP), jax.random.fold_in(keys[2], 1), 0, NODE_GRP - 1).astype(jnp.int32)
    second_hop = set_ends(jax.random.randint(keys[3], (SEEDS, FAN1, FAN2), 0, NODE_GRP), jax.random.fold_in(keys[3], 1), 0, NODE_GRP - 1).astype(jnp.int32)
    lower_self = normal_values(keys[4], (D, H), D ** -0.5, 0.1875, ((0, 4),))
    lower_neighbour = normal_values(keys[5], (D, H), D ** -0.5, 0.1875, ((0, 4),))
    norm_gain = jnp.clip(1.0 + 0.18 * jax.random.normal(keys[6], (H,), jnp.float32), 0.1, 1.9)
    norm_shift = normal_values(keys[7], (H,), 0.5, 3.0, (), jnp.float32)
    upper_self = normal_values(keys[8], (H, H), H ** -0.5, 0.375)
    upper_neighbour = normal_values(keys[9], (H, H), H ** -0.5, 0.375)
    embed_grad = normal_values(keys[10], (SEEDS, H), SEEDS ** -0.5, 0.125, ((0, 32),))
    return dict(node_feats=node_feats, seed_ids=seed_ids, first_hop=first_hop, second_hop=second_hop, lower_self=lower_self, lower_neighbour=lower_neighbour, norm_gain=norm_gain, norm_shift=norm_shift, upper_self=upper_self, upper_neighbour=upper_neighbour, embed_grad=embed_grad)


def reference(node_feats, seed_ids, first_hop, second_hop, lower_self, lower_neighbour, norm_gain, norm_shift, upper_self, upper_neighbour, embed_grad):
    groups = N_BATCH
    group_size = SEEDS // groups
    tables = node_feats.reshape(groups, NODE_GRP, D)

    def one_group(group_items):
        node_table, seed_local, hop_one, hop_two = group_items
        seed_rows = jnp.take(node_table, seed_local, axis=0)
        hop_rows = jnp.take(node_table, hop_one, axis=0)
        self_x = jnp.concatenate([seed_rows[:, None, :], hop_rows], axis=1).reshape(-1, D)
        near_mean = (lax.optimization_barrier(jnp.sum(hop_rows.astype(jnp.float32), axis=1)) / FAN1).astype(jnp.bfloat16)
        far_rows = jnp.take(node_table, hop_two, axis=0)
        far_mean = (lax.optimization_barrier(jnp.sum(far_rows.astype(jnp.float32), axis=2)) / FAN2).astype(jnp.bfloat16)
        neigh_x = jnp.concatenate([near_mean[:, None, :], far_mean], axis=1).reshape(-1, D)
        pre_act = jnp.dot(self_x, lower_self, preferred_element_type=jnp.float32) + jnp.dot(neigh_x, lower_neighbour, preferred_element_type=jnp.float32)
        return (pre_act, self_x, neigh_x)
    pre_act, self_x, neigh_x = lax.map(one_group, (tables, seed_ids.reshape(groups, group_size), first_hop.reshape(groups, group_size, FAN1), second_hop.reshape(groups, group_size, FAN1, FAN2)))
    pre_act = pre_act.reshape(-1, H)
    self_x = self_x.reshape(-1, D)
    neigh_x = neigh_x.reshape(-1, D)
    row_total = pre_act.shape[0]
    row_mean = lax.optimization_barrier(jnp.sum(pre_act, axis=0)) / row_total
    centred = pre_act - row_mean
    spread = lax.optimization_barrier(jnp.sum(centred * centred, axis=0)) / row_total
    inv_std = lax.rsqrt(spread + 1e-05)
    normed = centred * inv_std
    shifted = norm_gain * normed + norm_shift
    hidden = jax.nn.silu(shifted).astype(jnp.bfloat16)
    hidden_slots = hidden.reshape(SEEDS, 1 + FAN1, H)
    own_rows = hidden_slots[:, 0, :]
    hidden_mean = (lax.optimization_barrier(jnp.sum(hidden_slots[:, 1:, :].astype(jnp.float32), axis=1)) / FAN1).astype(jnp.bfloat16)
    embedding = (jnp.dot(own_rows, upper_self, preferred_element_type=jnp.float32) + jnp.dot(hidden_mean, upper_neighbour, preferred_element_type=jnp.float32)).astype(jnp.bfloat16)
    grad_upper_self = jnp.dot(own_rows.T, embed_grad, preferred_element_type=jnp.float32)
    grad_upper_neighbour = jnp.dot(hidden_mean.T, embed_grad, preferred_element_type=jnp.float32)
    d_self = jnp.dot(embed_grad, upper_self.T, preferred_element_type=jnp.float32)
    d_mean = jnp.dot(embed_grad, upper_neighbour.T, preferred_element_type=jnp.float32) / FAN1
    grad_hidden = jnp.concatenate([d_self[:, None, :], jnp.broadcast_to(d_mean[:, None, :], (SEEDS, FAN1, H))], axis=1).reshape(-1, H)
    sigmoid_v = jax.nn.sigmoid(shifted)
    grad_shifted = grad_hidden * sigmoid_v * (1.0 + shifted * (1.0 - sigmoid_v))
    grad_gain = lax.optimization_barrier(jnp.sum(grad_shifted * normed, axis=0))
    grad_shift = lax.optimization_barrier(jnp.sum(grad_shifted, axis=0))
    grad_pre = (norm_gain * inv_std * (grad_shifted - grad_shift / row_total - normed * grad_gain / row_total)).astype(jnp.bfloat16)
    grad_lower_self = jnp.dot(self_x.T, grad_pre, preferred_element_type=jnp.float32)
    grad_lower_neighbour = jnp.dot(neigh_x.T, grad_pre, preferred_element_type=jnp.float32)
    return (embedding, grad_lower_self, grad_lower_neighbour, grad_upper_self, grad_upper_neighbour, grad_gain, grad_shift)
```

```python
import functools

import jax
import jax.numpy as jnp
from jax import lax
from jax.experimental import pallas as pl
from jax.experimental.pallas import tpu as pltpu
from jax.sharding import PartitionSpec as P

BF = jnp.bfloat16
F32 = jnp.float32
LANES = 128
LOW = 256
SLOT = 16
GROUP = LOW // SLOT
MIB = 2**20


def dot(left, right, dims=((1,), (0,)), precision=None):
    return lax.dot_general(
        left, right, (dims, ((), ())), preferred_element_type=F32, precision=precision
    )


def params(mib):
    return pltpu.CompilerParams(vmem_limit_bytes=mib * MIB)


def whole(shape):
    return pl.BlockSpec(shape, lambda *_: (0,) * len(shape))


def halves(value):
    high = value.astype(BF)
    return high, (value - high.astype(F32)).astype(BF)


def count_kernel(high_ref, low_ref, count_ref):
    index = lax.broadcasted_iota(jnp.int32, (LOW, LOW), 0).astype(BF)
    one = jnp.ones((LOW, LOW), BF)
    zero = jnp.zeros((LOW, LOW), BF)
    for g in range(high_ref.shape[1]):
        left = jnp.where(index == high_ref[0, g : g + 1, :].astype(BF), one, zero)
        right = jnp.where(index == low_ref[0, g : g + 1, :].astype(BF), one, zero)
        counts = dot(left, right, ((1,), (1,))).astype(BF)
        for h in range(LOW // GROUP):
            count_ref[g * GROUP : (g + 1) * GROUP, h * LOW : (h + 1) * LOW] = counts[
                h * GROUP : (h + 1) * GROUP, :
            ]


def count_rows(high, low, table_rows):
    steps, groups, _ = high.shape
    rows = groups * GROUP
    spec = pl.BlockSpec((1, groups, LOW), lambda i: (i, 0, 0))
    return pl.pallas_call(
        count_kernel,
        grid=(steps,),
        in_specs=[spec, spec],
        out_specs=pl.BlockSpec((rows, table_rows), lambda i: (i, 0)),
        out_shape=jax.ShapeDtypeStruct((steps * rows, table_rows), BF),
        compiler_params=params(24),
        cost_estimate=pl.CostEstimate(
            flops=2 * steps * groups * LOW**3,
            bytes_accessed=2 * steps * rows * table_rows,
            transcendentals=0,
        ),
        name="count_rows",
    )(high, low)


def pick_kernel(
    first_block,
    per_slot,
    fans,
    ids_ref,
    count_ref,
    own_ref,
    peer_ref,
    self_own_ref,
    self_peer_ref,
    neigh_own_ref,
    neigh_peer_ref,
    across_ref,
    pre_ref,
    hot,
):
    blocks = ids_ref.shape[1]
    table_rows, width = own_ref.shape
    lanes = lax.broadcasted_iota(jnp.int32, (LANES, LANES), 1)
    for b in range(blocks):
        ids = jnp.broadcast_to(ids_ref[0, b : b + 1, :], (LANES, LANES)).T
        low = jnp.bitwise_and(ids, LOW - 1)
        high = lax.shift_right_logical(ids, 8).astype(BF)
        for part in range(LOW // LANES):
            base = jnp.where(lanes + LANES * part == low, 1.0, 0.0).astype(BF)
            for h in range(table_rows // LOW):
                start = h * LOW + part * LANES
                hot[b * LANES : (b + 1) * LANES, start : start + LANES] = jnp.where(
                    high == BF(h), base, jnp.zeros_like(base)
                )
    slot = (first_block + pl.program_id(0) * blocks) // per_slot
    fan = jnp.where(slot == 0, fans[0], fans[1]).astype(F32)
    total = None
    for i, (table, weight_self, weight_neigh) in enumerate(
        ((own_ref, self_own_ref, neigh_own_ref), (peer_ref, self_peer_ref, neigh_peer_ref))
    ):
        self_x = dot(hot[...], table[...]).astype(BF)
        neigh_x = (dot(count_ref[...], table[...]) / fan).astype(BF)
        across_ref[2 * i * width : (2 * i + 1) * width, :] = self_x.T
        across_ref[(2 * i + 1) * width : (2 * i + 2) * width, :] = neigh_x.T
        part = dot(self_x, weight_self[...]) + dot(neigh_x, weight_neigh[...])
        total = part if total is None else total + part
    pre_ref[...] = total.astype(BF)


def pick_rows(first_block, count, ids, counts, own, peer, weights, per_slot, fans):
    blocks = 1
    table_rows, width = own.shape
    rows = blocks * LANES
    steps = count // blocks
    skip = first_block // blocks
    hidden_width = weights[0].shape[1]
    total = count * LANES
    return pl.pallas_call(
        functools.partial(pick_kernel, first_block, per_slot, fans),
        grid=(steps,),
        in_specs=[
            pl.BlockSpec((1, blocks, LANES), lambda i: (i + skip, 0, 0)),
            pl.BlockSpec((rows, table_rows), lambda i: (i + skip, 0)),
            whole(own.shape),
            whole(peer.shape),
        ]
        + [whole(weights[0].shape)] * 4,
        out_specs=[
            pl.BlockSpec((4 * width, rows), lambda i: (0, i)),
            pl.BlockSpec((rows, hidden_width), lambda i: (i, 0)),
        ],
        out_shape=[
            jax.ShapeDtypeStruct((4 * width, total), BF),
            jax.ShapeDtypeStruct((total, hidden_width), BF),
        ],
        scratch_shapes=[pltpu.VMEM((rows, table_rows), BF)],
        compiler_params=params(32),
        cost_estimate=pl.CostEstimate(
            flops=8 * total * table_rows * width,
            bytes_accessed=2 * total * table_rows + 4 * table_rows * width,
            transcendentals=0,
        ),
        name="pick_rows",
    )(ids, counts, own, peer, *weights)


def stats_kernel(chunks, *refs):
    pairs, acrosses = refs[: 2 * chunks], refs[2 * chunks : 3 * chunks]
    keep_ref, send_ref = refs[3 * chunks :]
    width = acrosses[0].shape[0] // 4
    rows = sum(pairs[2 * i].shape[0] for i in range(chunks))
    values = [
        pairs[2 * i][...].astype(F32) + pairs[2 * i + 1][...].astype(F32) for i in range(chunks)
    ]
    mean = sum(jnp.sum(v, axis=0, keepdims=True) for v in values) / rows
    square = sum(jnp.sum((v - mean) * (v - mean), axis=0, keepdims=True) for v in values)
    column = sum(
        dot(jnp.ones((8, a.shape[1]), BF), a[...], ((1,), (1,))) for a in acrosses
    )
    pad = jnp.zeros((4, mean.shape[1]), F32)
    lanes = mean.shape[1] - width
    for ref, first in ((keep_ref, 0), (send_ref, 2)):
        parts = [column[:1, (first + j) * width : (first + j + 1) * width] for j in range(2)]
        if lanes:
            parts = [jnp.concatenate([p, jnp.zeros((1, lanes), F32)], axis=1) for p in parts]
        ref[...] = jnp.concatenate([mean, square, *parts, pad], axis=0)


def middle_kernel(
    chunks,
    slots,
    row_total,
    batches,
    place_ref,
    *refs,
):
    pairs, acrosses = refs[: 2 * chunks], refs[2 * chunks : 3 * chunks]
    (
        stats_ref,
        gain_ref,
        shift_ref,
        upper_self_ref,
        upper_neigh_ref,
        grad_ref,
        embed_ref,
        keep_ref,
        send_ref,
        sums_ref,
        both,
        embed_all,
    ) = refs[3 * chunks :]
    seeds, hidden_width = grad_ref.shape
    width = acrosses[0].shape[0] // 4
    fan_one = slots - 1
    mean = stats_ref[0:1, :]
    inv_std = lax.rsqrt(stats_ref[1:2, :] / row_total + 1e-05)
    gain, shift = gain_ref[...], shift_ref[...]
    grad = grad_ref[...]
    d_self = dot(grad, upper_self_ref[...], ((1,), (1,)))
    d_mean = dot(grad, upper_neigh_ref[...], ((1,), (1,))) / fan_one
    gain_sum = shift_sum = hidden_sum = own_rows = None
    slot = 0
    for i in range(chunks):
        for k in range(pairs[2 * i].shape[0] // seeds):
            span = slice(k * seeds, (k + 1) * seeds)
            pre_act = pairs[2 * i][span, :].astype(F32) + pairs[2 * i + 1][span, :].astype(F32)
            normed = (pre_act - mean) * inv_std
            shifted = gain * normed + shift
            sigmoid_v = 1.0 / (1.0 + jnp.exp(-shifted))
            hidden = (shifted * sigmoid_v).astype(BF)
            if slot == 0:
                own_rows = hidden
            else:
                hidden_sum = hidden.astype(F32) + (0.0 if hidden_sum is None else hidden_sum)
            grad_hidden = d_self if slot == 0 else d_mean
            grad_shifted = grad_hidden * sigmoid_v * (1.0 + shifted * (1.0 - sigmoid_v))
            gain_part = grad_shifted * normed
            gain_sum = gain_part if gain_sum is None else gain_sum + gain_part
            shift_sum = grad_shifted if shift_sum is None else shift_sum + grad_shifted
            both[slot * seeds : (slot + 1) * seeds, :hidden_width] = grad_shifted.astype(BF)
            both[slot * seeds : (slot + 1) * seeds, hidden_width:] = normed.astype(BF)
            slot += 1
    hidden_mean = (hidden_sum / fan_one).astype(BF)
    embed_all[...] = dot(own_rows, upper_self_ref[...]) + dot(hidden_mean, upper_neigh_ref[...])
    own_seeds = embed_ref.shape[0]
    start = pl.multiple_of(place_ref[0] * own_seeds, own_seeds)
    embed_ref[...] = embed_all[pl.ds(start, own_seeds), :].astype(BF)
    upper_self_part = dot(own_rows, grad, ((0,), (0,)))
    upper_neigh_part = dot(hidden_mean, grad, ((0,), (0,)))
    first_core = place_ref[1] == 0
    upper_keep = jnp.where(first_core, upper_self_part, upper_neigh_part)
    upper_send = jnp.where(first_core, upper_neigh_part, upper_self_part)
    gain_high, gain_low = halves(jnp.sum(gain_sum, axis=0, keepdims=True))
    shift_high, shift_low = halves(jnp.sum(shift_sum, axis=0, keepdims=True))
    sums = [gain_high, gain_low, shift_high, shift_low]
    sums_ref[...] = jnp.concatenate(
        [s.astype(F32) for s in sums] + [jnp.zeros((12, hidden_width), F32)], axis=0
    ).astype(BF)
    lower = None
    first = 0
    for a in acrosses:
        part = dot(a[...], both[first : first + a.shape[1], :])
        lower = part if lower is None else lower + part
        first += a.shape[1]
    piece, upper_piece = width // batches, hidden_width // batches
    for block, upper, ref in ((0, upper_keep, keep_ref), (2, upper_send, send_ref)):
        for d in range(batches):
            parts = []
            for lane in (0, hidden_width):
                for j in (0, 1):
                    row = (block + j) * width + d * piece
                    parts.append(lower[row : row + piece, lane : lane + hidden_width])
            parts.append(upper[d * upper_piece : (d + 1) * upper_piece, :])
            ref[d, :, :] = jnp.concatenate(parts, axis=0).astype(ref.dtype)


def merge_kernel(keep_ref, got_ref, sums_ref, got_sums_ref, out_ref):
    batches, rows, _ = keep_ref.shape
    mine, theirs = sums_ref[...].astype(F32), got_sums_ref[...].astype(F32)
    sums = []
    for j in (0, 2):
        sums += halves(
            (mine[j : j + 1] + mine[j + 1 : j + 2]) + (theirs[j : j + 1] + theirs[j + 1 : j + 2])
        )
    tail = jnp.concatenate(
        [s.astype(F32) for s in sums] + [jnp.zeros((12, mine.shape[1]), F32)], axis=0
    ).astype(BF)
    for d in range(batches):
        out_ref[d, :rows, :] = (keep_ref[d, :, :] + got_ref[d, :, :].astype(F32)).astype(BF)
        out_ref[d, rows:, :] = tail


def finish_kernel(row_total, parts_ref, stats_ref, gain_ref, column_ref, out_ref, gain_out, shift_out):
    batches, all_rows, _ = parts_ref.shape
    total = parts_ref[0, :, :].astype(F32)
    for d in range(1, batches):
        total = total + parts_ref[d, :, :].astype(F32)
    rows = all_rows - 16
    pieces = column_ref.shape[1]
    grad_gain = total[rows : rows + 1] + total[rows + 1 : rows + 2]
    grad_shift = total[rows + 2 : rows + 3] + total[rows + 3 : rows + 4]
    inv_std = lax.rsqrt(stats_ref[1:2, :] / row_total + 1e-05)
    outer = dot(
        column_ref[...],
        jnp.broadcast_to(grad_shift / row_total, (8, grad_shift.shape[1])),
        ((0,), (0,)),
        lax.Precision.HIGHEST,
    )
    lower = (gain_ref[...] * inv_std) * (
        total[:pieces] - outer - total[pieces : 2 * pieces] * (grad_gain / row_total)
    )
    out_ref[...] = jnp.concatenate([lower, total[2 * pieces : rows]], axis=0).astype(BF)
    gain_out[...] = grad_gain
    shift_out[...] = grad_shift


def place_kernel(masks, group_ref, parts_ref, self_ref, neigh_ref, upper_ref):
    piece = self_ref.shape[0] // len(masks)
    upper_piece = upper_ref.shape[0] // len(masks)
    for i, mask in enumerate(masks):
        d = group_ref[0] ^ mask
        rows = parts_ref[i, :, :].astype(F32)
        self_ref[pl.ds(pl.multiple_of(d * piece, piece), piece), :] = rows[:piece]
        neigh_ref[pl.ds(pl.multiple_of(d * piece, piece), piece), :] = rows[piece : 2 * piece]
        upper_ref[pl.ds(pl.multiple_of(d * upper_piece, upper_piece), upper_piece), :] = rows[
            2 * piece :
        ]


def swap(value, axis, mask):
    return lax.ppermute(value, axis, [(i, i ^ mask) for i in range(lax.axis_size(axis))])


SMEM = pl.BlockSpec(memory_space=pltpu.SMEM)


def on_device(
    node_feats,
    seed_ids,
    first_hop,
    second_hop,
    lower_self,
    lower_neighbour,
    norm_gain,
    norm_shift,
    upper_self,
    upper_neighbour,
    embed_grad,
):
    feats, batches = lax.axis_size("feat"), lax.axis_size("batch")
    chips = feats // 2
    feat, batch = lax.axis_index("feat"), lax.axis_index("batch")
    core, chip = feat % 2, feat // 2
    table_rows, width = node_feats.shape
    hidden_width = lower_self.shape[1]
    fan_one, fan_two = first_hop.shape[1], second_hop.shape[2]
    slots = fan_one + 1
    own_seeds = embed_grad.shape[0]
    seeds = own_seeds * chips
    row_total = own_seeds * slots * feats * batches
    rows = seeds * slots

    peer_feats = swap(node_feats, "feat", 1)
    peer_self = swap(lower_self, "feat", 1)
    peer_neigh = swap(lower_neighbour, "feat", 1)
    grads = jnp.zeros((seeds, hidden_width), BF)
    for mask in range(chips):
        part = embed_grad if mask == 0 else swap(embed_grad, "feat", 2 * mask)
        grads = lax.dynamic_update_slice(grads, part, ((chip ^ mask) * own_seeds, 0))

    def mine(ids):
        split = ids.reshape(chips, 2, own_seeds, *ids.shape[1:])
        part = lax.dynamic_index_in_dim(split, core, 1, keepdims=False)
        return part.reshape(seeds, *ids.shape[1:])

    near = mine(first_hop)
    self_ids = jnp.concatenate([mine(seed_ids)[:, None], near], axis=1).T
    self_ids = self_ids.reshape(-1, 1, LANES)

    def padded(ids, fan):
        return jnp.pad(ids, ((0, 0), (0, 0), (0, SLOT - fan)), constant_values=-1)

    neigh_ids = jnp.concatenate(
        [padded(near[None], fan_one), padded(mine(second_hop).transpose(1, 0, 2), fan_two)], axis=0
    )
    in_group = (jnp.arange(seeds, dtype=jnp.int32) % GROUP)[None, :, None]
    high = jnp.where(neigh_ids < 0, -1, (neigh_ids >> 8) * GROUP + in_group)
    shape = (slots, seeds // GROUP, LOW)
    counts = count_rows(high.reshape(shape), (neigh_ids & (LOW - 1)).reshape(shape), table_rows)

    weights = (lower_self, peer_self, lower_neighbour, peer_neigh)
    per_slot = seeds // LANES
    pairs, acrosses = [], []
    first = 0
    for share in CHUNKS:
        across, pre_act = pick_rows(
            first * per_slot,
            share * per_slot,
            self_ids,
            counts,
            node_feats,
            peer_feats,
            weights,
            per_slot,
            (fan_one, fan_two),
        )
        acrosses.append(across)
        mask = 2
        other = swap(pre_act, "feat", mask)
        while 2 * mask < feats:
            mask *= 2
            pre_act = (pre_act.astype(F32) + other.astype(F32)).astype(BF)
            other = swap(pre_act, "feat", mask)
        pairs += [pre_act, other]
        first += share

    tile = jax.ShapeDtypeStruct((8, hidden_width), F32)
    keep, send = pl.pallas_call(
        functools.partial(stats_kernel, len(CHUNKS)),
        out_shape=[tile, tile],
        compiler_params=params(40),
        name="stats",
    )(*pairs, *acrosses)

    def joined(mine, other, count):
        gap = mine[0:1] - other[0:1]
        return jnp.concatenate(
            [
                (mine[0:1] + other[0:1]) * 0.5,
                mine[1:2] + other[1:2] + gap * gap * (count * 0.5),
                mine[2:] + other[2:],
            ],
            axis=0,
        )

    count = float(rows)
    stats = joined(keep, swap(send, "feat", 1), count)
    mask = 1
    while mask < batches:
        count *= 2
        stats = joined(stats, swap(stats, "batch", mask), count)
        mask *= 2

    gain_row, shift_row = norm_gain[None, :], norm_shift[None, :]
    place = jnp.stack([chip, core]).astype(jnp.int32)
    per_group = 4 * width // batches + hidden_width // batches
    operands = [
        *pairs,
        *acrosses,
        stats,
        gain_row,
        shift_row,
        upper_self,
        upper_neighbour,
        grads,
    ]
    vmem = pl.BlockSpec(memory_space=pltpu.VMEM)
    embedding, keep, send, sums = pl.pallas_call(
        functools.partial(middle_kernel, len(CHUNKS), slots, row_total, batches),
        in_specs=[SMEM] + [vmem] * len(operands),
        out_shape=[
            jax.ShapeDtypeStruct((own_seeds, hidden_width), BF),
            jax.ShapeDtypeStruct((batches, per_group, hidden_width), F32),
            jax.ShapeDtypeStruct((batches, per_group, hidden_width), BF),
            jax.ShapeDtypeStruct((16, hidden_width), BF),
        ],
        scratch_shapes=[
            pltpu.VMEM((rows, 2 * hidden_width), BF),
            pltpu.VMEM((seeds, hidden_width), F32),
        ],
        compiler_params=params(40),
        name="middle",
    )(place, *operands)

    parts = pl.pallas_call(
        merge_kernel,
        out_shape=jax.ShapeDtypeStruct((batches, per_group + 16, hidden_width), BF),
        compiler_params=params(16),
        name="merge",
    )(keep, swap(send, "feat", 1), sums, swap(sums, "feat", 1))
    parts = lax.all_to_all(parts, "batch", 0, 0)

    piece = width // batches
    column = lax.dynamic_slice(stats[2:4], (0, batch * piece), (2, piece)).reshape(1, 2 * piece)
    column = jnp.pad(column, ((0, 7), (0, 0)))
    out_rows = 2 * piece + hidden_width // batches
    line = jax.ShapeDtypeStruct((1, hidden_width), F32)
    done, grad_gain, grad_shift = pl.pallas_call(
        functools.partial(finish_kernel, row_total),
        out_shape=[jax.ShapeDtypeStruct((out_rows, hidden_width), BF), line, line],
        compiler_params=params(16),
        name="finish",
    )(parts, stats, gain_row, column)

    gathered, masks = done[None], [0]
    mask = batches // 2
    while mask:
        gathered = jnp.concatenate([gathered, swap(gathered, "batch", mask)], axis=0)
        masks += [m ^ mask for m in masks]
        mask //= 2
    grad_self, grad_neigh, upper = pl.pallas_call(
        functools.partial(place_kernel, tuple(masks)),
        in_specs=[SMEM, vmem],
        out_shape=[
            jax.ShapeDtypeStruct((width, hidden_width), F32),
            jax.ShapeDtypeStruct((width, hidden_width), F32),
            jax.ShapeDtypeStruct((hidden_width, hidden_width), F32),
        ],
        compiler_params=params(16),
        name="place",
    )(batch.astype(jnp.int32)[None], gathered)
    upper_other = swap(upper, "feat", 1)
    return (
        embedding,
        grad_self,
        grad_neigh,
        jnp.where(core == 0, upper, upper_other),
        jnp.where(core == 0, upper_other, upper),
        grad_gain[0],
        grad_shift[0],
    )


CHUNKS = (4, 4, 3)


def solution(mesh):
    return jax.shard_map(
        on_device,
        mesh=mesh,
        in_specs=(
            P("batch", "feat"),
            P("batch"),
            P("batch", None),
            P("batch", None, None),
            P("feat", None),
            P("feat", None),
            P(),
            P(),
            P(),
            P(),
            P(("batch", "feat"), None),
        ),
        out_specs=(
            P(("batch", "feat"), None),
            P("feat", None),
            P("feat", None),
            P(),
            P(),
            P(),
            P(),
        ),
        check_vma=False,
    )
```

```python
import functools

import jax
import jax.numpy as jnp
from jax import lax
from jax.experimental import pallas as pl
from jax.experimental.pallas import tpu as pltpu
from jax.sharding import PartitionSpec as P

BF = jnp.bfloat16
F32 = jnp.float32
LANES = 128
LOW = 256
SLOT = 16
GROUP = LOW // SLOT
MIB = 2**20


def dot(left, right, dims=((1,), (0,)), precision=None):
    return lax.dot_general(
        left, right, (dims, ((), ())), preferred_element_type=F32, precision=precision
    )


def params(mib):
    return pltpu.CompilerParams(vmem_limit_bytes=mib * MIB)


VMEM = pl.BlockSpec(memory_space=pltpu.VMEM)
SMEM = pl.BlockSpec(memory_space=pltpu.SMEM)
HBM = pl.BlockSpec(memory_space=pltpu.HBM)


def halves(value):
    high = value.astype(BF)
    return high, (value - high.astype(F32)).astype(BF)


def build_kernel(
    place_ref,
    seed_in,
    near_in,
    far_in,
    out_ref,
    seed_ref,
    near_ref,
    far_ref,
    keys,
    own_group,
    spread,
    own_slot,
    sems,
):
    groups = LANES // GROUP
    per_slot = seed_ref.shape[1] // (2 * LANES)
    step, steps = pl.program_id(0), pl.num_programs(0)
    first_core = place_ref[1] == 0

    def mine(ids, p):
        parts = []
        for q in range(per_slot):
            left = ids[:, 2 * q * LANES : (2 * q + 1) * LANES]
            right = ids[:, (2 * q + 1) * LANES : (2 * q + 2) * LANES]
            low_half = lax.broadcasted_iota(jnp.int32, left.shape, 1) < LANES // 2
            even = jnp.where(low_half, left, pltpu.roll(right, LANES // 2, 1))
            odd = jnp.where(low_half, pltpu.roll(left, LANES // 2, 1), right)
            parts.append(jnp.where(first_core, even, odd))
        part = parts[0]
        for q in range(1, per_slot):
            part = jnp.where(p == q, parts[q], part)
        return part

    def flag(shape, test):
        row = lax.broadcasted_iota(jnp.int32, shape, 0)
        lane = lax.broadcasted_iota(jnp.int32, shape, 1)
        return jnp.where(test(row, lane), 1.0, 0.0).astype(BF)

    def widen(part):
        tiled = jnp.concatenate([part.astype(F32).astype(BF)] * groups, axis=0) * own_group[...]
        return dot(tiled, spread[...]).astype(BF) * own_slot[...]

    def wide_of(ids, self_row, p):
        part = mine(ids, p)
        gap = SLOT - part.shape[0]
        part = jnp.concatenate([part, jnp.full((gap, LANES), -1, jnp.int32)], axis=0)
        own = mine(jnp.broadcast_to(self_row, (8, self_row.shape[1])), p).astype(F32)
        high = widen(lax.shift_right_arithmetic(part, 8))
        return high, widen(jnp.bitwise_and(part, LOW - 1)), jnp.concatenate([own, own], axis=1)

    def keys_of(high, low, own):
        gather = flag((groups, LANES), lambda r, c: r == c // SLOT)
        in_group = (lax.broadcasted_iota(jnp.int32, (groups, LOW), 1) % GROUP).astype(F32)
        return dot(gather, high) * GROUP + in_group, dot(gather, low), own

    def keep(values, at):
        for j, value in enumerate(values):
            keys[at, j, :, :] = value

    @pl.when(step == 0)
    def _():
        copies = [
            pltpu.make_async_copy(a, b, sems.at[i])
            for i, (a, b) in enumerate(((seed_in, seed_ref), (near_in, near_ref), (far_in, far_ref)))
        ]
        for copy in copies:
            copy.start()
        own_group[...] = flag((LANES, LANES), lambda r, c: r // SLOT == c // GROUP)
        spread[...] = flag((LANES, LOW), lambda r, c: r % GROUP == c % GROUP)
        own_slot[...] = flag((LANES, LOW), lambda r, c: r % SLOT == c // GROUP)
        for copy in copies:
            copy.wait()
        keep(keys_of(*wide_of(near_ref[...], seed_ref[...], 0)), 0)

    now = step % 2
    later = jnp.minimum(step + 1, steps - 1)
    slot = later // per_slot
    back = jnp.maximum(slot - 1, 0)
    ids = far_ref[back, :, :]
    self_row = near_ref[pl.ds(back, 1), :]
    if per_slot > 1:
        padded = jnp.concatenate(
            [near_ref[...], jnp.full((ids.shape[0] - near_ref.shape[0], ids.shape[1]), -1, jnp.int32)]
        )
        ids = jnp.where(slot == 0, padded, ids)
        self_row = jnp.where(slot == 0, seed_ref[...], self_row)
    later_wide = wide_of(ids, self_row, later % per_slot)

    index = lax.broadcasted_iota(jnp.int32, (LOW, LOW), 0).astype(BF)
    one = jnp.ones((LOW, LOW), BF)
    zero = jnp.zeros((LOW, LOW), BF)
    def store(g, counts):
        counts = counts.astype(BF)
        for h in range(LOW // GROUP):
            out_ref[g * GROUP : (g + 1) * GROUP, h * LOW : (h + 1) * LOW] = counts[
                h * GROUP : (h + 1) * GROUP, :
            ]

    lanes = lax.broadcasted_iota(jnp.int32, (LANES, LANES), 1)
    ids = jnp.broadcast_to(keys[now, 2, 0:1, :LANES], (LANES, LANES)).T.astype(jnp.int32)
    low = jnp.bitwise_and(ids, LOW - 1)
    high = lax.shift_right_logical(ids, 8).astype(BF)
    bases = [
        jnp.where(lanes + LANES * part == low, 1.0, 0.0).astype(BF) for part in range(LOW // LANES)
    ]
    tiles = [(h, part) for h in range(out_ref.shape[1] // LOW) for part in range(LOW // LANES)]
    share = -(-len(tiles) // groups)
    waiting = []
    later_keys = None
    for g in range(groups):
        left = jnp.where(index == keys[now, 0, g : g + 1, :].astype(BF), one, zero)
        right = jnp.where(index == keys[now, 1, g : g + 1, :].astype(BF), one, zero)
        waiting.append((g, dot(left, right, ((1,), (1,)))))
        if g == 6:
            later_keys = keys_of(*later_wide)
        for h, part in tiles[g * share : (g + 1) * share]:
            at = h * LOW + part * LANES
            out_ref[LANES:, at : at + LANES] = jnp.where(
                high == BF(h), bases[part], jnp.zeros_like(bases[part])
            )
        if len(waiting) > 1:
            store(*waiting.pop(0))
    for item in waiting:
        store(*item)
    keep(later_keys, 1 - now)


def build_rows(place, seeds, near, far, table_rows):
    steps = (near.shape[0] + 1) * seeds.shape[1] // (2 * LANES)
    groups = LANES // GROUP
    return pl.pallas_call(
        build_kernel,
        grid=(steps,),
        in_specs=[SMEM, HBM, HBM, HBM],
        out_specs=pl.BlockSpec((2 * LANES, table_rows), lambda i: (i, 0)),
        out_shape=jax.ShapeDtypeStruct((steps * 2 * LANES, table_rows), BF),
        scratch_shapes=[
            pltpu.VMEM(seeds.shape, jnp.int32),
            pltpu.VMEM(near.shape, jnp.int32),
            pltpu.VMEM(far.shape, jnp.int32),
            pltpu.VMEM((2, 3, groups, LOW), F32),
            pltpu.VMEM((LANES, LANES), BF),
            pltpu.VMEM((LANES, LOW), BF),
            pltpu.VMEM((LANES, LOW), BF),
            pltpu.SemaphoreType.DMA((3,)),
        ],
        compiler_params=params(12),
        cost_estimate=pl.CostEstimate(
            flops=2 * steps * groups * LOW**3,
            bytes_accessed=4 * steps * LANES * table_rows,
            transcendentals=0,
        ),
        name="build_rows",
    )(place, seeds, near, far)


def pick_kernel(
    first_block,
    start,
    blocks,
    per_slot,
    fans,
    rows_ref,
    own_ref,
    peer_ref,
    self_own_ref,
    self_peer_ref,
    neigh_own_ref,
    neigh_peer_ref,
    across_ref,
    pre_ref,
    column_ref,
    peer,
    sem,
):
    width = own_ref.shape[1]
    step = pl.program_id(0)
    fetch = pltpu.make_async_copy(peer_ref, peer, sem)

    @pl.when(step == 0)
    def _():
        fetch.start()

    total = None
    columns = []
    for i, (table, weight_self, weight_neigh) in enumerate(
        ((own_ref, self_own_ref, neigh_own_ref), (peer, self_peer_ref, neigh_peer_ref))
    ):
        if i == 1:

            @pl.when(step == 0)
            def _():
                fetch.wait()

        self_parts, neigh_parts = [], []
        for b in range(blocks):
            block = first_block + step * blocks + b
            share = jnp.where(block < per_slot, F32(1.0 / fans[0]), F32(1.0 / fans[1]))
            at = start + 2 * b * LANES
            picked = dot(rows_ref[at : at + 2 * LANES, :], table[...])
            neigh_parts.append((picked[:LANES] * share).astype(BF))
            self_parts.append(picked[LANES:].astype(BF))
        for j, parts in enumerate((self_parts, neigh_parts)):
            features = jnp.concatenate(parts, axis=0)
            part = dot(features, (weight_self, weight_neigh)[j][...])
            total = part if total is None else total + part
            columns.append(dot(jnp.ones((8, features.shape[0]), BF), features))
            for b in range(blocks):
                across_ref[
                    (2 * i + j) * width : (2 * i + j + 1) * width, b * LANES : (b + 1) * LANES
                ] = parts[b].T
    pre_ref[...] = total.astype(BF)
    columns = jnp.concatenate(columns, axis=1)

    @pl.when(step == 0)
    def _():
        column_ref[...] = columns

    @pl.when(step > 0)
    def _():
        column_ref[...] += columns


def pick_rows(first_block, count, rows, own, peer, weights, per_slot, fans):
    table_rows, width = own.shape
    hidden_width = weights[0].shape[1]
    total = count * LANES
    resident = rows.size * 2 <= 32 * MIB
    if resident:
        blocks, start, rows_spec = count, first_block * 2 * LANES, VMEM
    else:
        blocks, start = per_slot, 0
        skip = first_block // blocks
        rows_spec = pl.BlockSpec((blocks * 2 * LANES, table_rows), lambda i: (i + skip, 0))
    return pl.pallas_call(
        functools.partial(pick_kernel, first_block, start, blocks, per_slot, fans),
        grid=(count // blocks,),
        in_specs=[rows_spec, VMEM, HBM] + [VMEM] * 4,
        out_specs=[
            pl.BlockSpec((4 * width, blocks * LANES), lambda i: (0, i)),
            pl.BlockSpec((blocks * LANES, hidden_width), lambda i: (i, 0)),
            pl.BlockSpec((8, 4 * width), lambda i: (0, 0)),
        ],
        out_shape=[
            jax.ShapeDtypeStruct((4 * width, total), BF),
            jax.ShapeDtypeStruct((total, hidden_width), BF),
            jax.ShapeDtypeStruct((8, 4 * width), F32),
        ],
        scratch_shapes=[
            pltpu.VMEM(peer.shape, BF),
            pltpu.SemaphoreType.DMA,
        ],
        compiler_params=params(16 if resident else 24),
        cost_estimate=pl.CostEstimate(
            flops=8 * total * table_rows * width,
            bytes_accessed=2 * total * table_rows + 4 * table_rows * width,
            transcendentals=0,
        ),
        name="pick_rows",
    )(rows, own, peer, *weights)


def stats_kernel(chunks, *refs):
    pairs, columns = refs[: 2 * chunks], refs[2 * chunks : 3 * chunks]
    keep_ref, send_ref, total = refs[3 * chunks :]
    width = columns[0].shape[1] // 4
    rows = total.shape[0]
    mean = 0.0
    first = 0
    for i in range(chunks):
        value = pairs[2 * i][...].astype(F32) + pairs[2 * i + 1][...].astype(F32)
        total[first : first + value.shape[0], :] = value
        mean = mean + jnp.sum(value, axis=0, keepdims=True)
        first += value.shape[0]
    mean = mean / rows
    gap = total[...] - mean
    square = jnp.sum(gap * gap, axis=0, keepdims=True)
    column = sum(c[0:1, :] for c in columns)
    pad = jnp.zeros((4, mean.shape[1]), F32)
    lanes = mean.shape[1] - width
    for ref, first in ((keep_ref, 0), (send_ref, 2)):
        parts = [column[:, (first + j) * width : (first + j + 1) * width] for j in range(2)]
        if lanes:
            parts = [jnp.concatenate([p, jnp.zeros((1, lanes), F32)], axis=1) for p in parts]
        ref[...] = jnp.concatenate([mean, square, *parts, pad], axis=0)


def join_kernel(count, mine_ref, other_ref, out_ref):
    mine, other = mine_ref[...], other_ref[...]
    gap = mine[0:1] - other[0:1]
    out_ref[...] = jnp.concatenate(
        [
            (mine[0:1] + other[0:1]) * 0.5,
            mine[1:2] + other[1:2] + gap * gap * (count * 0.5),
            mine[2:] + other[2:],
        ],
        axis=0,
    )


def joined(mine, other, count):
    return pl.pallas_call(
        functools.partial(join_kernel, count),
        in_specs=[VMEM, VMEM],
        out_specs=VMEM,
        out_shape=jax.ShapeDtypeStruct(mine.shape, mine.dtype),
        compiler_params=params(1),
        name="join",
    )(mine, other)


def middle_kernel(
    chunks,
    slots,
    row_total,
    batches,
    place_ref,
    *refs,
):
    pairs, acrosses = refs[: 2 * chunks], refs[2 * chunks : 3 * chunks]
    chips = len(refs) - 3 * chunks - 12
    grad_parts = refs[3 * chunks : 3 * chunks + chips]
    (
        stats_ref,
        gain_ref,
        shift_ref,
        upper_self_ref,
        upper_neigh_ref,
        embed_ref,
        keep_ref,
        send_ref,
        sums_ref,
        both,
        embed_all,
        grad_all,
    ) = refs[3 * chunks + chips :]
    own_seeds, hidden_width = grad_parts[0].shape
    seeds = own_seeds * chips
    width = acrosses[0].shape[0] // 4
    for mask, part in enumerate(grad_parts):
        at = pl.multiple_of((place_ref[0] ^ mask) * own_seeds, own_seeds)
        grad_all[pl.ds(at, own_seeds), :] = part[...].astype(F32)
    fan_one = slots - 1
    mean = stats_ref[0:1, :]
    inv_std = lax.rsqrt(stats_ref[1:2, :] / row_total + 1e-05)
    gain, shift = gain_ref[...], shift_ref[...]
    grad = grad_all[...].astype(BF)
    d_self = dot(grad, upper_self_ref[...], ((1,), (1,)))
    d_mean = dot(grad, upper_neigh_ref[...], ((1,), (1,))) / fan_one
    gain_sum = shift_sum = hidden_sum = own_rows = None
    places = [(i, k) for i in range(chunks) for k in range(pairs[2 * i].shape[0] // seeds)]
    for slot, (i, k) in enumerate(places):
        span = slice(k * seeds, (k + 1) * seeds)
        pre_act = pairs[2 * i][span, :].astype(F32) + pairs[2 * i + 1][span, :].astype(F32)
        span = slice(slot * seeds, (slot + 1) * seeds)
        normed = (pre_act - mean) * inv_std
        shifted = gain * normed + shift
        sigmoid_v = 1.0 / (1.0 + jnp.exp(-shifted))
        hidden = (shifted * sigmoid_v).astype(BF)
        if slot == 0:
            own_rows = hidden
        else:
            hidden_sum = hidden.astype(F32) + (0.0 if hidden_sum is None else hidden_sum)
        grad_hidden = d_self if slot == 0 else d_mean
        grad_shifted = grad_hidden * sigmoid_v * (1.0 + shifted * (1.0 - sigmoid_v))
        gain_part = grad_shifted * normed
        gain_sum = gain_part if gain_sum is None else gain_sum + gain_part
        shift_sum = grad_shifted if shift_sum is None else shift_sum + grad_shifted
        both[span, :hidden_width] = grad_shifted.astype(BF)
        both[span, hidden_width:] = normed.astype(BF)
    hidden_mean = (hidden_sum / fan_one).astype(BF)
    embed_all[...] = dot(own_rows, upper_self_ref[...]) + dot(hidden_mean, upper_neigh_ref[...])
    start = pl.multiple_of(place_ref[0] * own_seeds, own_seeds)
    embed_ref[...] = embed_all[pl.ds(start, own_seeds), :].astype(BF)
    upper_self_part = dot(own_rows, grad, ((0,), (0,)))
    upper_neigh_part = dot(hidden_mean, grad, ((0,), (0,)))
    first_core = place_ref[1] == 0
    upper_keep = jnp.where(first_core, upper_self_part, upper_neigh_part)
    upper_send = jnp.where(first_core, upper_neigh_part, upper_self_part)
    gain_high, gain_low = halves(jnp.sum(gain_sum, axis=0, keepdims=True))
    shift_high, shift_low = halves(jnp.sum(shift_sum, axis=0, keepdims=True))
    sums = [gain_high, gain_low, shift_high, shift_low]
    sums_ref[...] = jnp.concatenate(
        [s.astype(F32) for s in sums] + [jnp.zeros((12, hidden_width), F32)], axis=0
    ).astype(BF)
    lower = None
    first = 0
    for a in acrosses:
        part = dot(a[...], both[first : first + a.shape[1], :])
        lower = part if lower is None else lower + part
        first += a.shape[1]
    piece, upper_piece = width // batches, hidden_width // batches
    for block, upper, ref in ((0, upper_keep, keep_ref), (2, upper_send, send_ref)):
        for d in range(batches):
            parts = []
            for lane in (0, hidden_width):
                for j in (0, 1):
                    row = (block + j) * width + d * piece
                    parts.append(lower[row : row + piece, lane : lane + hidden_width])
            parts.append(upper[d * upper_piece : (d + 1) * upper_piece, :])
            ref[d, :, :] = jnp.concatenate(parts, axis=0).astype(ref.dtype)


def merge_kernel(keep_ref, got_ref, sums_ref, got_sums_ref, out_ref):
    batches, rows, _ = keep_ref.shape
    mine, theirs = sums_ref[...].astype(F32), got_sums_ref[...].astype(F32)
    sums = []
    for j in (0, 2):
        sums += halves(
            (mine[j : j + 1] + mine[j + 1 : j + 2]) + (theirs[j : j + 1] + theirs[j + 1 : j + 2])
        )
    tail = jnp.concatenate(
        [s.astype(F32) for s in sums] + [jnp.zeros((12, mine.shape[1]), F32)], axis=0
    ).astype(BF)
    for d in range(batches):
        out_ref[d, :rows, :] = (keep_ref[d, :, :] + got_ref[d, :, :].astype(F32)).astype(BF)
        out_ref[d, rows:, :] = tail


def finish_kernel(row_total, parts_ref, stats_ref, gain_ref, column_ref, out_ref, gain_out, shift_out):
    batches, all_rows, _ = parts_ref.shape
    total = parts_ref[0, :, :].astype(F32)
    for d in range(1, batches):
        total = total + parts_ref[d, :, :].astype(F32)
    rows = all_rows - 16
    pieces = column_ref.shape[1]
    grad_gain = total[rows : rows + 1] + total[rows + 1 : rows + 2]
    grad_shift = total[rows + 2 : rows + 3] + total[rows + 3 : rows + 4]
    inv_std = lax.rsqrt(stats_ref[1:2, :] / row_total + 1e-05)
    outer = dot(
        column_ref[...],
        jnp.broadcast_to(grad_shift / row_total, (8, grad_shift.shape[1])),
        ((0,), (0,)),
        lax.Precision.HIGHEST,
    )
    lower = (gain_ref[...] * inv_std) * (
        total[:pieces] - outer - total[pieces : 2 * pieces] * (grad_gain / row_total)
    )
    out_ref[...] = jnp.concatenate([lower, total[2 * pieces : rows]], axis=0).astype(BF)
    gain_out[...] = grad_gain
    shift_out[...] = grad_shift


def place_kernel(masks, group_ref, parts_ref, self_ref, neigh_ref, upper_ref):
    piece = self_ref.shape[0] // len(masks)
    upper_piece = upper_ref.shape[0] // len(masks)
    for i, mask in enumerate(masks):
        d = group_ref[0] ^ mask
        rows = parts_ref[i, :, :].astype(F32)
        self_ref[pl.ds(pl.multiple_of(d * piece, piece), piece), :] = rows[:piece]
        neigh_ref[pl.ds(pl.multiple_of(d * piece, piece), piece), :] = rows[piece : 2 * piece]
        upper_ref[pl.ds(pl.multiple_of(d * upper_piece, upper_piece), upper_piece), :] = rows[
            2 * piece :
        ]


def swap(value, axis, mask):
    return lax.ppermute(value, axis, [(i, i ^ mask) for i in range(lax.axis_size(axis))])


def on_device(
    node_feats,
    seed_ids,
    first_hop,
    second_hop,
    lower_self,
    lower_neighbour,
    norm_gain,
    norm_shift,
    upper_self,
    upper_neighbour,
    embed_grad,
):
    feats, batches = lax.axis_size("feat"), lax.axis_size("batch")
    chips = feats // 2
    feat, batch = lax.axis_index("feat"), lax.axis_index("batch")
    core, chip = feat % 2, feat // 2
    table_rows, width = node_feats.shape
    hidden_width = lower_self.shape[1]
    fan_one, fan_two = first_hop.shape[1], second_hop.shape[2]
    slots = fan_one + 1
    own_seeds = embed_grad.shape[0]
    seeds = own_seeds * chips
    row_total = own_seeds * slots * feats * batches
    rows = seeds * slots

    peer_feats = swap(node_feats, "feat", 1)
    peer_self = swap(lower_self, "feat", 1)
    peer_neigh = swap(lower_neighbour, "feat", 1)
    grads = [embed_grad] + [swap(embed_grad, "feat", 2 * mask) for mask in range(1, chips)]

    place = jnp.stack([chip, core]).astype(jnp.int32)
    picks = build_rows(
        place, seed_ids[None, :], first_hop.T, second_hop.transpose(1, 2, 0), table_rows
    )

    weights = (lower_self, peer_self, lower_neighbour, peer_neigh)
    per_slot = seeds // LANES
    pairs, acrosses, columns = [], [], []
    first = 0
    for share in CHUNKS:
        across, pre_act, column = pick_rows(
            first * per_slot,
            share * per_slot,
            picks,
            node_feats,
            peer_feats,
            weights,
            per_slot,
            (fan_one, fan_two),
        )
        acrosses.append(across)
        columns.append(column)
        mask = 2
        other = swap(pre_act, "feat", mask)
        while 2 * mask < feats:
            mask *= 2
            pre_act = (pre_act.astype(F32) + other.astype(F32)).astype(BF)
            other = swap(pre_act, "feat", mask)
        pairs += [pre_act, other]
        first += share

    tile = jax.ShapeDtypeStruct((8, hidden_width), F32)
    keep, send = pl.pallas_call(
        functools.partial(stats_kernel, len(CHUNKS)),
        out_shape=[tile, tile],
        scratch_shapes=[pltpu.VMEM((rows, hidden_width), F32)],
        compiler_params=params(16),
        name="stats",
    )(*pairs, *columns)

    count = float(rows)
    stats = joined(keep, swap(send, "feat", 1), count)
    mask = 1
    while mask < batches:
        count *= 2
        stats = joined(stats, swap(stats, "batch", mask), count)
        mask *= 2

    gain_row, shift_row = norm_gain[None, :], norm_shift[None, :]
    per_group = 4 * width // batches + hidden_width // batches
    operands = [
        *pairs,
        *acrosses,
        *grads,
        stats,
        gain_row,
        shift_row,
        upper_self,
        upper_neighbour,
    ]
    embedding, keep, send, sums = pl.pallas_call(
        functools.partial(middle_kernel, len(CHUNKS), slots, row_total, batches),
        in_specs=[SMEM] + [VMEM] * len(operands),
        out_shape=[
            jax.ShapeDtypeStruct((own_seeds, hidden_width), BF),
            jax.ShapeDtypeStruct((batches, per_group, hidden_width), F32),
            jax.ShapeDtypeStruct((batches, per_group, hidden_width), BF),
            jax.ShapeDtypeStruct((16, hidden_width), BF),
        ],
        scratch_shapes=[
            pltpu.VMEM((rows, 2 * hidden_width), BF),
            pltpu.VMEM((seeds, hidden_width), F32),
            pltpu.VMEM((seeds, hidden_width), F32),
        ],
        compiler_params=params(24),
        name="middle",
    )(place, *operands)

    parts = pl.pallas_call(
        merge_kernel,
        out_shape=jax.ShapeDtypeStruct((batches, per_group + 16, hidden_width), BF),
        compiler_params=params(16),
        name="merge",
    )(keep, swap(send, "feat", 1), sums, swap(sums, "feat", 1))
    parts = lax.all_to_all(parts, "batch", 0, 0)

    piece = width // batches
    column = lax.dynamic_slice(stats[2:4], (0, batch * piece), (2, piece)).reshape(1, 2 * piece)
    column = jnp.pad(column, ((0, 7), (0, 0)))
    out_rows = 2 * piece + hidden_width // batches
    line = jax.ShapeDtypeStruct((1, hidden_width), F32)
    done, grad_gain, grad_shift = pl.pallas_call(
        functools.partial(finish_kernel, row_total),
        out_shape=[jax.ShapeDtypeStruct((out_rows, hidden_width), BF), line, line],
        compiler_params=params(16),
        name="finish",
    )(parts, stats, gain_row, column)

    gathered, masks = done[None], [0]
    mask = batches // 2
    while mask:
        gathered = jnp.concatenate([gathered, swap(gathered, "batch", mask)], axis=0)
        masks += [m ^ mask for m in masks]
        mask //= 2
    grad_self, grad_neigh, upper = pl.pallas_call(
        functools.partial(place_kernel, tuple(masks)),
        in_specs=[SMEM, VMEM],
        out_shape=[
            jax.ShapeDtypeStruct((width, hidden_width), F32),
            jax.ShapeDtypeStruct((width, hidden_width), F32),
            jax.ShapeDtypeStruct((hidden_width, hidden_width), F32),
        ],
        compiler_params=params(16),
        name="place",
    )(batch.astype(jnp.int32)[None], gathered)
    upper_other = swap(upper, "feat", 1)
    return (
        embedding,
        grad_self,
        grad_neigh,
        jnp.where(core == 0, upper, upper_other),
        jnp.where(core == 0, upper_other, upper),
        grad_gain[0],
        grad_shift[0],
    )


CHUNKS = (3, 2, 2, 2, 2)


def solution(mesh):
    return jax.shard_map(
        on_device,
        mesh=mesh,
        in_specs=(
            P("batch", "feat"),
            P("batch"),
            P("batch", None),
            P("batch", None, None),
            P("feat", None),
            P("feat", None),
            P(),
            P(),
            P(),
            P(),
            P(("batch", "feat"), None),
        ),
        out_specs=(
            P(("batch", "feat"), None),
            P("feat", None),
            P("feat", None),
            P(),
            P(),
            P(),
            P(),
        ),
        check_vma=False,
    )
```

```python
import functools

import jax
import jax.numpy as jnp
from jax import lax
from jax.experimental import pallas as pl
from jax.experimental.pallas import tpu as pltpu
from jax.sharding import PartitionSpec as P

BF = jnp.bfloat16
F32 = jnp.float32
LANES = 128
LOW = 256
SLOT = 16
GROUP = LOW // SLOT
MIB = 2**20


def dot(left, right, dims=((1,), (0,)), precision=None):
    return lax.dot_general(
        left, right, (dims, ((), ())), preferred_element_type=F32, precision=precision
    )


def params(mib):
    return pltpu.CompilerParams(vmem_limit_bytes=mib * MIB)


VMEM = pl.BlockSpec(memory_space=pltpu.VMEM)
SMEM = pl.BlockSpec(memory_space=pltpu.SMEM)
HBM = pl.BlockSpec(memory_space=pltpu.HBM)


def halves(value):
    high = value.astype(BF)
    return high, (value - high.astype(F32)).astype(BF)


def build_kernel(
    place_ref,
    seed_in,
    near_in,
    far_in,
    out_ref,
    seed_ref,
    near_ref,
    far_ref,
    keys,
    own_group,
    spread,
    own_slot,
    sems,
):
    groups = LANES // GROUP
    per_slot = seed_ref.shape[1] // (2 * LANES)
    step, steps = pl.program_id(0), pl.num_programs(0)
    first_core = place_ref[1] == 0

    def mine(ids, p):
        parts = []
        for q in range(per_slot):
            left = ids[:, 2 * q * LANES : (2 * q + 1) * LANES]
            right = ids[:, (2 * q + 1) * LANES : (2 * q + 2) * LANES]
            low_half = lax.broadcasted_iota(jnp.int32, left.shape, 1) < LANES // 2
            even = jnp.where(low_half, left, pltpu.roll(right, LANES // 2, 1))
            odd = jnp.where(low_half, pltpu.roll(left, LANES // 2, 1), right)
            parts.append(jnp.where(first_core, even, odd))
        part = parts[0]
        for q in range(1, per_slot):
            part = jnp.where(p == q, parts[q], part)
        return part

    def flag(shape, test):
        row = lax.broadcasted_iota(jnp.int32, shape, 0)
        lane = lax.broadcasted_iota(jnp.int32, shape, 1)
        return jnp.where(test(row, lane), 1.0, 0.0).astype(BF)

    def widen(part):
        tiled = jnp.concatenate([part.astype(F32).astype(BF)] * groups, axis=0) * own_group[...]
        return dot(tiled, spread[...]).astype(BF) * own_slot[...]

    def wide_of(ids, self_row, p):
        part = mine(ids, p)
        gap = SLOT - part.shape[0]
        part = jnp.concatenate([part, jnp.full((gap, LANES), -1, jnp.int32)], axis=0)
        own = mine(jnp.broadcast_to(self_row, (8, self_row.shape[1])), p).astype(F32)
        high = widen(lax.shift_right_arithmetic(part, 8))
        return high, widen(jnp.bitwise_and(part, LOW - 1)), jnp.concatenate([own, own], axis=1)

    def keys_of(high, low, own):
        gather = flag((groups, LANES), lambda r, c: r == c // SLOT)
        in_group = (lax.broadcasted_iota(jnp.int32, (groups, LOW), 1) % GROUP).astype(F32)
        return dot(gather, high) * GROUP + in_group, dot(gather, low), own

    def keep(values, at):
        for j, value in enumerate(values):
            keys[at, j, :, :] = value

    @pl.when(step == 0)
    def _():
        copies = [
            pltpu.make_async_copy(a, b, sems.at[i])
            for i, (a, b) in enumerate(((seed_in, seed_ref), (near_in, near_ref), (far_in, far_ref)))
        ]
        for copy in copies:
            copy.start()
        own_group[...] = flag((LANES, LANES), lambda r, c: r // SLOT == c // GROUP)
        spread[...] = flag((LANES, LOW), lambda r, c: r % GROUP == c % GROUP)
        own_slot[...] = flag((LANES, LOW), lambda r, c: r % SLOT == c // GROUP)
        for copy in copies:
            copy.wait()
        keep(keys_of(*wide_of(near_ref[...], seed_ref[...], 0)), 0)

    now = step % 2
    later = jnp.minimum(step + 1, steps - 1)
    slot = later // per_slot
    back = jnp.maximum(slot - 1, 0)
    ids = far_ref[back, :, :]
    self_row = near_ref[pl.ds(back, 1), :]
    if per_slot > 1:
        padded = jnp.concatenate(
            [near_ref[...], jnp.full((ids.shape[0] - near_ref.shape[0], ids.shape[1]), -1, jnp.int32)]
        )
        ids = jnp.where(slot == 0, padded, ids)
        self_row = jnp.where(slot == 0, seed_ref[...], self_row)
    later_wide = wide_of(ids, self_row, later % per_slot)

    index = lax.broadcasted_iota(jnp.int32, (LOW, LOW), 0).astype(BF)
    one = jnp.ones((LOW, LOW), BF)
    zero = jnp.zeros((LOW, LOW), BF)
    def store(g, counts):
        counts = counts.astype(BF)
        for h in range(LOW // GROUP):
            out_ref[g * GROUP : (g + 1) * GROUP, h * LOW : (h + 1) * LOW] = counts[
                h * GROUP : (h + 1) * GROUP, :
            ]

    lanes = lax.broadcasted_iota(jnp.int32, (LANES, LANES), 1)
    ids = jnp.broadcast_to(keys[now, 2, 0:1, :LANES], (LANES, LANES)).T.astype(jnp.int32)
    low = jnp.bitwise_and(ids, LOW - 1)
    high = lax.shift_right_logical(ids, 8).astype(BF)
    bases = [
        jnp.where(lanes + LANES * part == low, 1.0, 0.0).astype(BF) for part in range(LOW // LANES)
    ]
    tiles = [(h, part) for h in range(out_ref.shape[1] // LOW) for part in range(LOW // LANES)]
    share = -(-len(tiles) // groups)
    waiting = []
    later_keys = None
    for g in range(groups):
        left = jnp.where(index == keys[now, 0, g : g + 1, :].astype(BF), one, zero)
        right = jnp.where(index == keys[now, 1, g : g + 1, :].astype(BF), one, zero)
        waiting.append((g, dot(left, right, ((1,), (1,)))))
        if g == 6:
            later_keys = keys_of(*later_wide)
        for h, part in tiles[g * share : (g + 1) * share]:
            at = h * LOW + part * LANES
            out_ref[LANES:, at : at + LANES] = jnp.where(
                high == BF(h), bases[part], jnp.zeros_like(bases[part])
            )
        if len(waiting) > 1:
            store(*waiting.pop(0))
    for item in waiting:
        store(*item)
    keep(later_keys, 1 - now)


def build_rows(place, seeds, near, far, table_rows):
    steps = (near.shape[0] + 1) * seeds.shape[1] // (2 * LANES)
    groups = LANES // GROUP
    return pl.pallas_call(
        build_kernel,
        grid=(steps,),
        in_specs=[SMEM, HBM, HBM, HBM],
        out_specs=pl.BlockSpec((2 * LANES, table_rows), lambda i: (i, 0)),
        out_shape=jax.ShapeDtypeStruct((steps * 2 * LANES, table_rows), BF),
        scratch_shapes=[
            pltpu.VMEM(seeds.shape, jnp.int32),
            pltpu.VMEM(near.shape, jnp.int32),
            pltpu.VMEM(far.shape, jnp.int32),
            pltpu.VMEM((2, 3, groups, LOW), F32),
            pltpu.VMEM((LANES, LANES), BF),
            pltpu.VMEM((LANES, LOW), BF),
            pltpu.VMEM((LANES, LOW), BF),
            pltpu.SemaphoreType.DMA((3,)),
        ],
        compiler_params=params(12),
        cost_estimate=pl.CostEstimate(
            flops=2 * steps * groups * LOW**3,
            bytes_accessed=4 * steps * LANES * table_rows,
            transcendentals=0,
        ),
        name="build_rows",
    )(place, seeds, near, far)


def pick_kernel(
    first_block,
    start,
    blocks,
    per_slot,
    fans,
    rows_ref,
    own_ref,
    peer_ref,
    self_own_ref,
    self_peer_ref,
    neigh_own_ref,
    neigh_peer_ref,
    across_ref,
    pre_ref,
    column_ref,
):
    width = own_ref.shape[1]
    step = pl.program_id(0)
    tables = (own_ref, peer_ref)
    picked = [
        [dot(rows_ref[at : at + 2 * LANES, :], table[...]) for table in tables]
        for at in range(start, start + 2 * blocks * LANES, 2 * LANES)
    ]
    total = None
    columns = []
    for i in range(2):
        self_parts, neigh_parts = [], []
        for b in range(blocks):
            block = first_block + step * blocks + b
            share = jnp.where(block < per_slot, F32(1.0 / fans[0]), F32(1.0 / fans[1]))
            neigh_parts.append((picked[b][i][:LANES] * share).astype(BF))
            self_parts.append(picked[b][i][LANES:].astype(BF))
        weights = ((self_own_ref, neigh_own_ref), (self_peer_ref, neigh_peer_ref))[i]
        for j, parts in enumerate((self_parts, neigh_parts)):
            part = dot(jnp.concatenate(parts, axis=0), weights[j][...])
            total = part if total is None else total + part
            columns.append(
                sum(jnp.sum(p.astype(F32).reshape(-1, 8, width), axis=0) for p in parts)
            )
            for b in range(blocks):
                across_ref[
                    (2 * i + j) * width : (2 * i + j + 1) * width, b * LANES : (b + 1) * LANES
                ] = parts[b].T
    pre_ref[...] = total.astype(BF)
    columns = jnp.concatenate(columns, axis=1)

    @pl.when(step == 0)
    def _():
        column_ref[...] = columns

    @pl.when(step > 0)
    def _():
        column_ref[...] += columns


def pick_rows(first_block, count, rows, own, peer, weights, per_slot, fans):
    table_rows, width = own.shape
    hidden_width = weights[0].shape[1]
    total = count * LANES
    resident = rows.size * 2 <= 32 * MIB
    if resident:
        blocks, start, rows_spec = count, first_block * 2 * LANES, VMEM
    else:
        blocks, start = per_slot, 0
        skip = first_block // blocks
        rows_spec = pl.BlockSpec((blocks * 2 * LANES, table_rows), lambda i: (i + skip, 0))
    return pl.pallas_call(
        functools.partial(pick_kernel, first_block, start, blocks, per_slot, fans),
        grid=(count // blocks,),
        in_specs=[rows_spec] + [VMEM] * 6,
        out_specs=[
            pl.BlockSpec((4 * width, blocks * LANES), lambda i: (0, i)),
            pl.BlockSpec((blocks * LANES, hidden_width), lambda i: (i, 0)),
            pl.BlockSpec((8, 4 * width), lambda i: (0, 0)),
        ],
        out_shape=[
            jax.ShapeDtypeStruct((4 * width, total), BF),
            jax.ShapeDtypeStruct((total, hidden_width), BF),
            jax.ShapeDtypeStruct((8, 4 * width), F32),
        ],
        compiler_params=params(12 if resident else 22),
        cost_estimate=pl.CostEstimate(
            flops=8 * total * table_rows * width,
            bytes_accessed=2 * total * table_rows + 4 * table_rows * width,
            transcendentals=0,
        ),
        name="pick_rows",
    )(rows, own, peer, *weights)


def stats_kernel(chunks, *refs):
    pairs, columns = refs[: 2 * chunks], refs[2 * chunks : 3 * chunks]
    keep_ref, send_ref, total = refs[3 * chunks :]
    width = columns[0].shape[1] // 4
    rows = total.shape[0]
    mean = 0.0
    first = 0
    for i in range(chunks):
        value = pairs[2 * i][...].astype(F32) + pairs[2 * i + 1][...].astype(F32)
        total[first : first + value.shape[0], :] = value
        mean = mean + jnp.sum(value, axis=0, keepdims=True)
        first += value.shape[0]
    mean = mean / rows
    gap = total[...] - mean
    square = jnp.sum(gap * gap, axis=0, keepdims=True)
    column = jnp.sum(sum(c[...] for c in columns), axis=0, keepdims=True)
    pad = jnp.zeros((4, mean.shape[1]), F32)
    lanes = mean.shape[1] - width
    for ref, first in ((keep_ref, 0), (send_ref, 2)):
        parts = [column[:, (first + j) * width : (first + j + 1) * width] for j in range(2)]
        if lanes:
            parts = [jnp.concatenate([p, jnp.zeros((1, lanes), F32)], axis=1) for p in parts]
        ref[...] = jnp.concatenate([mean, square, *parts, pad], axis=0)


def join_kernel(count, mine_ref, other_ref, out_ref):
    mine, other = mine_ref[...], other_ref[...]
    gap = mine[0:1] - other[0:1]
    out_ref[...] = jnp.concatenate(
        [
            (mine[0:1] + other[0:1]) * 0.5,
            mine[1:2] + other[1:2] + gap * gap * (count * 0.5),
            mine[2:] + other[2:],
        ],
        axis=0,
    )


def joined(mine, other, count):
    return pl.pallas_call(
        functools.partial(join_kernel, count),
        in_specs=[VMEM, VMEM],
        out_specs=VMEM,
        out_shape=jax.ShapeDtypeStruct(mine.shape, mine.dtype),
        compiler_params=params(1),
        name="join",
    )(mine, other)


def middle_kernel(
    chunks,
    slots,
    row_total,
    batches,
    place_ref,
    *refs,
):
    pairs, acrosses = refs[: 2 * chunks], refs[2 * chunks : 3 * chunks]
    chips = len(refs) - 3 * chunks - 12
    grad_parts = refs[3 * chunks : 3 * chunks + chips]
    (
        stats_ref,
        gain_ref,
        shift_ref,
        upper_self_ref,
        upper_neigh_ref,
        embed_ref,
        keep_ref,
        send_ref,
        sums_ref,
        both,
        embed_all,
        grad_all,
    ) = refs[3 * chunks + chips :]
    own_seeds, hidden_width = grad_parts[0].shape
    seeds = own_seeds * chips
    width = acrosses[0].shape[0] // 4
    for mask, part in enumerate(grad_parts):
        at = pl.multiple_of((place_ref[0] ^ mask) * own_seeds, own_seeds)
        grad_all[pl.ds(at, own_seeds), :] = part[...].astype(F32)
    fan_one = slots - 1
    mean = stats_ref[0:1, :]
    inv_std = lax.rsqrt(stats_ref[1:2, :] / row_total + 1e-05)
    gain, shift = gain_ref[...], shift_ref[...]
    grad = grad_all[...].astype(BF)
    d_self = dot(grad, upper_self_ref[...], ((1,), (1,)))
    d_mean = dot(grad, upper_neigh_ref[...], ((1,), (1,))) / fan_one
    gain_sum = shift_sum = hidden_sum = own_rows = None
    places = [(i, k) for i in range(chunks) for k in range(pairs[2 * i].shape[0] // seeds)]
    for slot, (i, k) in enumerate(places):
        span = slice(k * seeds, (k + 1) * seeds)
        pre_act = pairs[2 * i][span, :].astype(F32) + pairs[2 * i + 1][span, :].astype(F32)
        span = slice(slot * seeds, (slot + 1) * seeds)
        normed = (pre_act - mean) * inv_std
        shifted = gain * normed + shift
        sigmoid_v = 1.0 / (1.0 + jnp.exp(-shifted))
        hidden = (shifted * sigmoid_v).astype(BF)
        if slot == 0:
            own_rows = hidden
        else:
            hidden_sum = hidden.astype(F32) + (0.0 if hidden_sum is None else hidden_sum)
        grad_hidden = d_self if slot == 0 else d_mean
        grad_shifted = grad_hidden * sigmoid_v * (1.0 + shifted * (1.0 - sigmoid_v))
        gain_part = grad_shifted * normed
        gain_sum = gain_part if gain_sum is None else gain_sum + gain_part
        shift_sum = grad_shifted if shift_sum is None else shift_sum + grad_shifted
        both[span, :hidden_width] = grad_shifted.astype(BF)
        both[span, hidden_width:] = normed.astype(BF)
    hidden_mean = (hidden_sum / fan_one).astype(BF)
    embed_all[...] = dot(own_rows, upper_self_ref[...]) + dot(hidden_mean, upper_neigh_ref[...])
    start = pl.multiple_of(place_ref[0] * own_seeds, own_seeds)
    embed_ref[...] = embed_all[pl.ds(start, own_seeds), :].astype(BF)
    upper_self_part = dot(own_rows, grad, ((0,), (0,)))
    upper_neigh_part = dot(hidden_mean, grad, ((0,), (0,)))
    first_core = place_ref[1] == 0
    upper_keep = jnp.where(first_core, upper_self_part, upper_neigh_part)
    upper_send = jnp.where(first_core, upper_neigh_part, upper_self_part)
    gain_high, gain_low = halves(jnp.sum(gain_sum, axis=0, keepdims=True))
    shift_high, shift_low = halves(jnp.sum(shift_sum, axis=0, keepdims=True))
    sums = [gain_high, gain_low, shift_high, shift_low]
    sums_ref[...] = jnp.concatenate(
        [s.astype(F32) for s in sums] + [jnp.zeros((12, hidden_width), F32)], axis=0
    ).astype(BF)
    lower = None
    first = 0
    for a in acrosses:
        part = dot(a[...], both[first : first + a.shape[1], :])
        lower = part if lower is None else lower + part
        first += a.shape[1]
    piece, upper_piece = width // batches, hidden_width // batches
    for block, upper, ref in ((0, upper_keep, keep_ref), (2, upper_send, send_ref)):
        for d in range(batches):
            parts = []
            for lane in (0, hidden_width):
                for j in (0, 1):
                    row = (block + j) * width + d * piece
                    parts.append(lower[row : row + piece, lane : lane + hidden_width])
            parts.append(upper[d * upper_piece : (d + 1) * upper_piece, :])
            ref[d, :, :] = jnp.concatenate(parts, axis=0).astype(ref.dtype)


def merge_kernel(keep_ref, got_ref, sums_ref, got_sums_ref, out_ref):
    batches, rows, _ = keep_ref.shape
    mine, theirs = sums_ref[...].astype(F32), got_sums_ref[...].astype(F32)
    sums = []
    for j in (0, 2):
        sums += halves(
            (mine[j : j + 1] + mine[j + 1 : j + 2]) + (theirs[j : j + 1] + theirs[j + 1 : j + 2])
        )
    tail = jnp.concatenate(
        [s.astype(F32) for s in sums] + [jnp.zeros((12, mine.shape[1]), F32)], axis=0
    ).astype(BF)
    for d in range(batches):
        out_ref[d, :rows, :] = (keep_ref[d, :, :] + got_ref[d, :, :].astype(F32)).astype(BF)
        out_ref[d, rows:, :] = tail


def finish_kernel(row_total, parts_ref, stats_ref, gain_ref, column_ref, out_ref, gain_out, shift_out):
    batches, all_rows, _ = parts_ref.shape
    total = parts_ref[0, :, :].astype(F32)
    for d in range(1, batches):
        total = total + parts_ref[d, :, :].astype(F32)
    rows = all_rows - 16
    pieces = column_ref.shape[1]
    grad_gain = total[rows : rows + 1] + total[rows + 1 : rows + 2]
    grad_shift = total[rows + 2 : rows + 3] + total[rows + 3 : rows + 4]
    inv_std = lax.rsqrt(stats_ref[1:2, :] / row_total + 1e-05)
    outer = dot(
        column_ref[...],
        jnp.broadcast_to(grad_shift / row_total, (8, grad_shift.shape[1])),
        ((0,), (0,)),
        lax.Precision.HIGHEST,
    )
    lower = (gain_ref[...] * inv_std) * (
        total[:pieces] - outer - total[pieces : 2 * pieces] * (grad_gain / row_total)
    )
    out_ref[...] = jnp.concatenate([lower, total[2 * pieces : rows]], axis=0).astype(BF)
    gain_out[...] = grad_gain
    shift_out[...] = grad_shift


def place_kernel(masks, group_ref, parts_ref, self_ref, neigh_ref, upper_ref):
    piece = self_ref.shape[0] // len(masks)
    upper_piece = upper_ref.shape[0] // len(masks)
    for i, mask in enumerate(masks):
        d = group_ref[0] ^ mask
        rows = parts_ref[i, :, :].astype(F32)
        self_ref[pl.ds(pl.multiple_of(d * piece, piece), piece), :] = rows[:piece]
        neigh_ref[pl.ds(pl.multiple_of(d * piece, piece), piece), :] = rows[piece : 2 * piece]
        upper_ref[pl.ds(pl.multiple_of(d * upper_piece, upper_piece), upper_piece), :] = rows[
            2 * piece :
        ]


def swap(value, axis, mask):
    return lax.ppermute(value, axis, [(i, i ^ mask) for i in range(lax.axis_size(axis))])


def on_device(
    node_feats,
    seed_ids,
    first_hop,
    second_hop,
    lower_self,
    lower_neighbour,
    norm_gain,
    norm_shift,
    upper_self,
    upper_neighbour,
    embed_grad,
):
    feats, batches = lax.axis_size("feat"), lax.axis_size("batch")
    chips = feats // 2
    feat, batch = lax.axis_index("feat"), lax.axis_index("batch")
    core, chip = feat % 2, feat // 2
    table_rows, width = node_feats.shape
    hidden_width = lower_self.shape[1]
    fan_one, fan_two = first_hop.shape[1], second_hop.shape[2]
    slots = fan_one + 1
    own_seeds = embed_grad.shape[0]
    seeds = own_seeds * chips
    row_total = own_seeds * slots * feats * batches
    rows = seeds * slots

    peer_feats = swap(node_feats, "feat", 1)
    peer_self = swap(lower_self, "feat", 1)
    peer_neigh = swap(lower_neighbour, "feat", 1)
    grads = [embed_grad] + [swap(embed_grad, "feat", 2 * mask) for mask in range(1, chips)]

    place = jnp.stack([chip, core]).astype(jnp.int32)
    picks = build_rows(
        place, seed_ids[None, :], first_hop.T, second_hop.transpose(1, 2, 0), table_rows
    )

    weights = (lower_self, peer_self, lower_neighbour, peer_neigh)
    per_slot = seeds // LANES
    pairs, acrosses, columns = [], [], []
    first = 0
    for share in CHUNKS:
        across, pre_act, column = pick_rows(
            first * per_slot,
            share * per_slot,
            picks,
            node_feats,
            peer_feats,
            weights,
            per_slot,
            (fan_one, fan_two),
        )
        acrosses.append(across)
        columns.append(column)
        mask = 2
        other = swap(pre_act, "feat", mask)
        while 2 * mask < feats:
            mask *= 2
            pre_act = (pre_act.astype(F32) + other.astype(F32)).astype(BF)
            other = swap(pre_act, "feat", mask)
        pairs += [pre_act, other]
        first += share

    tile = jax.ShapeDtypeStruct((8, hidden_width), F32)
    keep, send = pl.pallas_call(
        functools.partial(stats_kernel, len(CHUNKS)),
        out_shape=[tile, tile],
        scratch_shapes=[pltpu.VMEM((rows, hidden_width), F32)],
        compiler_params=params(16),
        name="stats",
    )(*pairs, *columns)

    count = float(rows)
    stats = joined(keep, swap(send, "feat", 1), count)
    mask = 1
    while mask < batches:
        count *= 2
        stats = joined(stats, swap(stats, "batch", mask), count)
        mask *= 2

    gain_row, shift_row = norm_gain[None, :], norm_shift[None, :]
    per_group = 4 * width // batches + hidden_width // batches
    operands = [
        *pairs,
        *acrosses,
        *grads,
        stats,
        gain_row,
        shift_row,
        upper_self,
        upper_neighbour,
    ]
    embedding, keep, send, sums = pl.pallas_call(
        functools.partial(middle_kernel, len(CHUNKS), slots, row_total, batches),
        in_specs=[SMEM] + [VMEM] * len(operands),
        out_shape=[
            jax.ShapeDtypeStruct((own_seeds, hidden_width), BF),
            jax.ShapeDtypeStruct((batches, per_group, hidden_width), F32),
            jax.ShapeDtypeStruct((batches, per_group, hidden_width), BF),
            jax.ShapeDtypeStruct((16, hidden_width), BF),
        ],
        scratch_shapes=[
            pltpu.VMEM((rows, 2 * hidden_width), BF),
            pltpu.VMEM((seeds, hidden_width), F32),
            pltpu.VMEM((seeds, hidden_width), F32),
        ],
        compiler_params=params(24),
        name="middle",
    )(place, *operands)

    parts = pl.pallas_call(
        merge_kernel,
        out_shape=jax.ShapeDtypeStruct((batches, per_group + 16, hidden_width), BF),
        compiler_params=params(16),
        name="merge",
    )(keep, swap(send, "feat", 1), sums, swap(sums, "feat", 1))
    parts = lax.all_to_all(parts, "batch", 0, 0)

    piece = width // batches
    column = lax.dynamic_slice(stats[2:4], (0, batch * piece), (2, piece)).reshape(1, 2 * piece)
    column = jnp.pad(column, ((0, 7), (0, 0)))
    out_rows = 2 * piece + hidden_width // batches
    line = jax.ShapeDtypeStruct((1, hidden_width), F32)
    done, grad_gain, grad_shift = pl.pallas_call(
        functools.partial(finish_kernel, row_total),
        out_shape=[jax.ShapeDtypeStruct((out_rows, hidden_width), BF), line, line],
        compiler_params=params(16),
        name="finish",
    )(parts, stats, gain_row, column)

    gathered, masks = done[None], [0]
    mask = batches // 2
    while mask:
        gathered = jnp.concatenate([gathered, swap(gathered, "batch", mask)], axis=0)
        masks += [m ^ mask for m in masks]
        mask //= 2
    grad_self, grad_neigh, upper = pl.pallas_call(
        functools.partial(place_kernel, tuple(masks)),
        in_specs=[SMEM, VMEM],
        out_shape=[
            jax.ShapeDtypeStruct((width, hidden_width), F32),
            jax.ShapeDtypeStruct((width, hidden_width), F32),
            jax.ShapeDtypeStruct((hidden_width, hidden_width), F32),
        ],
        compiler_params=params(16),
        name="place",
    )(batch.astype(jnp.int32)[None], gathered)
    upper_other = swap(upper, "feat", 1)
    return (
        embedding,
        grad_self,
        grad_neigh,
        jnp.where(core == 0, upper, upper_other),
        jnp.where(core == 0, upper_other, upper),
        grad_gain[0],
        grad_shift[0],
    )


CHUNKS = (2, 3, 3, 3)


def solution(mesh):
    return jax.shard_map(
        on_device,
        mesh=mesh,
        in_specs=(
            P("batch", "feat"),
            P("batch"),
            P("batch", None),
            P("batch", None, None),
            P("feat", None),
            P("feat", None),
            P(),
            P(),
            P(),
            P(),
            P(("batch", "feat"), None),
        ),
        out_specs=(
            P(("batch", "feat"), None),
            P("feat", None),
            P("feat", None),
            P(),
            P(),
            P(),
            P(),
        ),
        check_vma=False,
    )
```

```python
import functools

import jax
import jax.numpy as jnp
from jax import lax
from jax.experimental import pallas as pl
from jax.experimental.pallas import tpu as pltpu
from jax.sharding import PartitionSpec as P

BF = jnp.bfloat16
F32 = jnp.float32
LANES = 128
LOW = 256
SLOT = 16
GROUP = LOW // SLOT
MIB = 2**20


def dot(left, right, dims=((1,), (0,)), precision=None):
    return lax.dot_general(
        left, right, (dims, ((), ())), preferred_element_type=F32, precision=precision
    )


def params(mib):
    return pltpu.CompilerParams(vmem_limit_bytes=mib * MIB)


VMEM = pl.BlockSpec(memory_space=pltpu.VMEM)
SMEM = pl.BlockSpec(memory_space=pltpu.SMEM)


def halves(value):
    high = value.astype(BF)
    return high, (value - high.astype(F32)).astype(BF)


def build_kernel(
    place_ref,
    own_ref,
    far_ref,
    out_ref,
    keys,
    own_group,
    spread,
    own_slot,
):
    groups = LANES // GROUP
    per_slot = own_ref.shape[1] // (2 * LANES)
    step, steps = pl.program_id(0), pl.num_programs(0)
    first_core = place_ref[1] == 0

    def mine(ids, p):
        parts = []
        for q in range(per_slot):
            left = ids[:, 2 * q * LANES : (2 * q + 1) * LANES]
            right = ids[:, (2 * q + 1) * LANES : (2 * q + 2) * LANES]
            low_half = lax.broadcasted_iota(jnp.int32, left.shape, 1) < LANES // 2
            even = jnp.where(low_half, left, pltpu.roll(right, LANES // 2, 1))
            odd = jnp.where(low_half, pltpu.roll(left, LANES // 2, 1), right)
            parts.append(jnp.where(first_core, even, odd))
        part = parts[0]
        for q in range(1, per_slot):
            part = jnp.where(p == q, parts[q], part)
        return part

    def flag(shape, test):
        row = lax.broadcasted_iota(jnp.int32, shape, 0)
        lane = lax.broadcasted_iota(jnp.int32, shape, 1)
        return jnp.where(test(row, lane), 1.0, 0.0).astype(BF)

    def widen(part):
        tiled = jnp.concatenate([part.astype(F32).astype(BF)] * groups, axis=0) * own_group[...]
        return dot(tiled, spread[...]).astype(BF) * own_slot[...]

    def wide_of(ids, self_row, p):
        part = mine(ids, p)
        gap = SLOT - part.shape[0]
        part = jnp.concatenate([part, jnp.full((gap, LANES), -1, jnp.int32)], axis=0)
        own = mine(jnp.broadcast_to(self_row, (8, self_row.shape[1])), p).astype(F32)
        high = widen(lax.shift_right_arithmetic(part, 8))
        return high, widen(jnp.bitwise_and(part, LOW - 1)), jnp.concatenate([own, own], axis=1)

    def keys_of(high, low, own):
        gather = flag((groups, LANES), lambda r, c: r == c // SLOT)
        in_group = (lax.broadcasted_iota(jnp.int32, (groups, LOW), 1) % GROUP).astype(F32)
        return dot(gather, high) * GROUP + in_group, dot(gather, low), own

    def keep(values, at):
        for j, value in enumerate(values):
            keys[at, j, :, :] = value

    @pl.when(step == 0)
    def _():
        own_group[...] = flag((LANES, LANES), lambda r, c: r // SLOT == c // GROUP)
        spread[...] = flag((LANES, LOW), lambda r, c: r % GROUP == c % GROUP)
        own_slot[...] = flag((LANES, LOW), lambda r, c: r % SLOT == c // GROUP)
        keep(keys_of(*wide_of(own_ref[1:, :], own_ref[0:1, :], 0)), 0)

    now = step % 2
    later = jnp.minimum(step + 1, steps - 1)
    slot = later // per_slot
    back = jnp.maximum(slot - 1, 0)
    ids = far_ref[back, :, :]
    self_row = own_ref[pl.ds(back + 1, 1), :]
    if per_slot > 1:
        padded = jnp.concatenate(
            [own_ref[1:, :], jnp.full((ids.shape[0] + 1 - own_ref.shape[0], ids.shape[1]), -1, jnp.int32)]
        )
        ids = jnp.where(slot == 0, padded, ids)
        self_row = jnp.where(slot == 0, own_ref[0:1, :], self_row)
    later_wide = wide_of(ids, self_row, later % per_slot)

    index = lax.broadcasted_iota(jnp.int32, (LOW, LOW), 0).astype(BF)
    one = jnp.ones((LOW, LOW), BF)
    zero = jnp.zeros((LOW, LOW), BF)
    def store(g, counts):
        counts = counts.astype(BF)
        for h in range(LOW // GROUP):
            out_ref[g * GROUP : (g + 1) * GROUP, h * LOW : (h + 1) * LOW] = counts[
                h * GROUP : (h + 1) * GROUP, :
            ]

    lanes = lax.broadcasted_iota(jnp.int32, (LANES, LANES), 1)
    ids = jnp.broadcast_to(keys[now, 2, 0:1, :LANES], (LANES, LANES)).T.astype(jnp.int32)
    low = jnp.bitwise_and(ids, LOW - 1)
    high = lax.shift_right_logical(ids, 8).astype(BF)
    bases = [
        jnp.where(lanes + LANES * part == low, 1.0, 0.0).astype(BF) for part in range(LOW // LANES)
    ]
    tiles = [(h, part) for h in range(out_ref.shape[1] // LOW) for part in range(LOW // LANES)]
    share = -(-len(tiles) // groups)
    waiting = []
    later_keys = None
    for g in range(groups):
        left = jnp.where(index == keys[now, 0, g : g + 1, :].astype(BF), one, zero)
        right = jnp.where(index == keys[now, 1, g : g + 1, :].astype(BF), one, zero)
        waiting.append((g, dot(left, right, ((1,), (1,)))))
        if g == 6:
            later_keys = keys_of(*later_wide)
        for h, part in tiles[g * share : (g + 1) * share]:
            at = h * LOW + part * LANES
            out_ref[LANES:, at : at + LANES] = jnp.where(
                high == BF(h), bases[part], jnp.zeros_like(bases[part])
            )
        if len(waiting) > 1:
            store(*waiting.pop(0))
    for item in waiting:
        store(*item)
    keep(later_keys, 1 - now)


def build_rows(place, own, far, table_rows):
    steps = own.shape[0] * own.shape[1] // (2 * LANES)
    groups = LANES // GROUP
    return pl.pallas_call(
        build_kernel,
        grid=(steps,),
        in_specs=[SMEM, VMEM, VMEM],
        out_specs=pl.BlockSpec((2 * LANES, table_rows), lambda i: (i, 0)),
        out_shape=jax.ShapeDtypeStruct((steps * 2 * LANES, table_rows), BF),
        scratch_shapes=[
            pltpu.VMEM((2, 3, groups, LOW), F32),
            pltpu.VMEM((LANES, LANES), BF),
            pltpu.VMEM((LANES, LOW), BF),
            pltpu.VMEM((LANES, LOW), BF),
        ],
        compiler_params=params(12),
        cost_estimate=pl.CostEstimate(
            flops=2 * steps * groups * LOW**3,
            bytes_accessed=4 * steps * LANES * table_rows,
            transcendentals=0,
        ),
        name="build_rows",
    )(place, own, far)


def pick_kernel(
    first_block,
    start,
    blocks,
    per_slot,
    fans,
    rows_ref,
    own_ref,
    peer_ref,
    self_own_ref,
    self_peer_ref,
    neigh_own_ref,
    neigh_peer_ref,
    across_ref,
    pre_ref,
    column_ref,
):
    width = own_ref.shape[1]
    step = pl.program_id(0)
    tables = (own_ref, peer_ref)
    picked = [
        [dot(rows_ref[at : at + 2 * LANES, :], table[...]) for table in tables]
        for at in range(start, start + 2 * blocks * LANES, 2 * LANES)
    ]
    total = None
    columns = []
    for i in range(2):
        self_parts, neigh_parts = [], []
        for b in range(blocks):
            block = first_block + step * blocks + b
            share = jnp.where(block < per_slot, F32(1.0 / fans[0]), F32(1.0 / fans[1]))
            neigh_parts.append((picked[b][i][:LANES] * share).astype(BF))
            self_parts.append(picked[b][i][LANES:].astype(BF))
        weights = ((self_own_ref, neigh_own_ref), (self_peer_ref, neigh_peer_ref))[i]
        for j, parts in enumerate((self_parts, neigh_parts)):
            part = dot(jnp.concatenate(parts, axis=0), weights[j][...])
            total = part if total is None else total + part
            columns.append(
                sum(jnp.sum(p.astype(F32).reshape(-1, 8, width), axis=0) for p in parts)
            )
            for b in range(blocks):
                across_ref[
                    (2 * i + j) * width : (2 * i + j + 1) * width, b * LANES : (b + 1) * LANES
                ] = parts[b].T
    pre_ref[...] = total.astype(BF)
    columns = jnp.concatenate(columns, axis=1)

    @pl.when(step == 0)
    def _():
        column_ref[...] = columns

    @pl.when(step > 0)
    def _():
        column_ref[...] += columns


def pick_rows(first_block, count, rows, own, peer, weights, per_slot, fans):
    table_rows, width = own.shape
    hidden_width = weights[0].shape[1]
    total = count * LANES
    resident = rows.size * 2 <= 32 * MIB
    if resident:
        blocks, start, rows_spec = count, first_block * 2 * LANES, VMEM
    else:
        blocks, start = per_slot, 0
        skip = first_block // blocks
        rows_spec = pl.BlockSpec((blocks * 2 * LANES, table_rows), lambda i: (i + skip, 0))
    return pl.pallas_call(
        functools.partial(pick_kernel, first_block, start, blocks, per_slot, fans),
        grid=(count // blocks,),
        in_specs=[rows_spec] + [VMEM] * 6,
        out_specs=[
            pl.BlockSpec((4 * width, blocks * LANES), lambda i: (0, i)),
            pl.BlockSpec((blocks * LANES, hidden_width), lambda i: (i, 0)),
            pl.BlockSpec((8, 4 * width), lambda i: (0, 0)),
        ],
        out_shape=[
            jax.ShapeDtypeStruct((4 * width, total), BF),
            jax.ShapeDtypeStruct((total, hidden_width), BF),
            jax.ShapeDtypeStruct((8, 4 * width), F32),
        ],
        compiler_params=params(12 if resident else 22),
        cost_estimate=pl.CostEstimate(
            flops=8 * total * table_rows * width,
            bytes_accessed=2 * total * table_rows + 4 * table_rows * width,
            transcendentals=0,
        ),
        name="pick_rows",
    )(rows, own, peer, *weights)


def stats_kernel(chunks, *refs):
    pairs, columns = refs[: 2 * chunks], refs[2 * chunks : 3 * chunks]
    keep_ref, send_ref, total = refs[3 * chunks :]
    width = columns[0].shape[1] // 4
    rows = total.shape[0]
    mean = 0.0
    first = 0
    for i in range(chunks):
        value = pairs[2 * i][...].astype(F32) + pairs[2 * i + 1][...].astype(F32)
        total[first : first + value.shape[0], :] = value
        mean = mean + jnp.sum(value, axis=0, keepdims=True)
        first += value.shape[0]
    mean = mean / rows
    gap = total[...] - mean
    square = jnp.sum(gap * gap, axis=0, keepdims=True)
    column = jnp.sum(sum(c[...] for c in columns), axis=0, keepdims=True)
    pad = jnp.zeros((4, mean.shape[1]), F32)
    lanes = mean.shape[1] - width
    for ref, first in ((keep_ref, 0), (send_ref, 2)):
        parts = [column[:, (first + j) * width : (first + j + 1) * width] for j in range(2)]
        if lanes:
            parts = [jnp.concatenate([p, jnp.zeros((1, lanes), F32)], axis=1) for p in parts]
        ref[...] = jnp.concatenate([mean, square, *parts, pad], axis=0)


def join_kernel(count, mine_ref, other_ref, out_ref):
    mine, other = mine_ref[...], other_ref[...]
    gap = mine[0:1] - other[0:1]
    out_ref[...] = jnp.concatenate(
        [
            (mine[0:1] + other[0:1]) * 0.5,
            mine[1:2] + other[1:2] + gap * gap * (count * 0.5),
            mine[2:] + other[2:],
        ],
        axis=0,
    )


def joined(mine, other, count):
    return pl.pallas_call(
        functools.partial(join_kernel, count),
        in_specs=[VMEM, VMEM],
        out_specs=VMEM,
        out_shape=jax.ShapeDtypeStruct(mine.shape, mine.dtype),
        compiler_params=params(1),
        name="join",
    )(mine, other)


def middle_kernel(
    chunks,
    slots,
    row_total,
    batches,
    place_ref,
    *refs,
):
    pairs, acrosses = refs[: 2 * chunks], refs[2 * chunks : 3 * chunks]
    chips = len(refs) - 3 * chunks - 12
    grad_parts = refs[3 * chunks : 3 * chunks + chips]
    (
        stats_ref,
        gain_ref,
        shift_ref,
        upper_self_ref,
        upper_neigh_ref,
        embed_ref,
        keep_ref,
        send_ref,
        sums_ref,
        both,
        embed_all,
        grad_all,
    ) = refs[3 * chunks + chips :]
    own_seeds, hidden_width = grad_parts[0].shape
    seeds = own_seeds * chips
    width = acrosses[0].shape[0] // 4
    for mask, part in enumerate(grad_parts):
        at = pl.multiple_of((place_ref[0] ^ mask) * own_seeds, own_seeds)
        grad_all[pl.ds(at, own_seeds), :] = part[...].astype(F32)
    fan_one = slots - 1
    mean = stats_ref[0:1, :]
    inv_std = lax.rsqrt(stats_ref[1:2, :] / row_total + 1e-05)
    gain, shift = gain_ref[...], shift_ref[...]
    grad = grad_all[...].astype(BF)
    d_self = dot(grad, upper_self_ref[...], ((1,), (1,)))
    d_mean = dot(grad, upper_neigh_ref[...], ((1,), (1,))) / fan_one
    gain_sum = shift_sum = hidden_sum = own_rows = None
    places = [(i, k) for i in range(chunks) for k in range(pairs[2 * i].shape[0] // seeds)]
    for slot, (i, k) in enumerate(places):
        span = slice(k * seeds, (k + 1) * seeds)
        pre_act = pairs[2 * i][span, :].astype(F32) + pairs[2 * i + 1][span, :].astype(F32)
        span = slice(slot * seeds, (slot + 1) * seeds)
        normed = (pre_act - mean) * inv_std
        shifted = gain * normed + shift
        sigmoid_v = 1.0 / (1.0 + jnp.exp(-shifted))
        hidden = (shifted * sigmoid_v).astype(BF)
        if slot == 0:
            own_rows = hidden
        else:
            hidden_sum = hidden.astype(F32) + (0.0 if hidden_sum is None else hidden_sum)
        grad_hidden = d_self if slot == 0 else d_mean
        grad_shifted = grad_hidden * sigmoid_v * (1.0 + shifted * (1.0 - sigmoid_v))
        gain_part = grad_shifted * normed
        gain_sum = gain_part if gain_sum is None else gain_sum + gain_part
        shift_sum = grad_shifted if shift_sum is None else shift_sum + grad_shifted
        both[span, :hidden_width] = grad_shifted.astype(BF)
        both[span, hidden_width:] = normed.astype(BF)
    hidden_mean = (hidden_sum / fan_one).astype(BF)
    embed_all[...] = dot(own_rows, upper_self_ref[...]) + dot(hidden_mean, upper_neigh_ref[...])
    start = pl.multiple_of(place_ref[0] * own_seeds, own_seeds)
    embed_ref[...] = embed_all[pl.ds(start, own_seeds), :].astype(BF)
    upper_self_part = dot(own_rows, grad, ((0,), (0,)))
    upper_neigh_part = dot(hidden_mean, grad, ((0,), (0,)))
    first_core = place_ref[1] == 0
    upper_keep = jnp.where(first_core, upper_self_part, upper_neigh_part)
    upper_send = jnp.where(first_core, upper_neigh_part, upper_self_part)
    gain_high, gain_low = halves(jnp.sum(gain_sum, axis=0, keepdims=True))
    shift_high, shift_low = halves(jnp.sum(shift_sum, axis=0, keepdims=True))
    sums = [gain_high, gain_low, shift_high, shift_low]
    sums_ref[...] = jnp.concatenate(
        [s.astype(F32) for s in sums] + [jnp.zeros((12, hidden_width), F32)], axis=0
    ).astype(BF)
    lower = None
    first = 0
    for a in acrosses:
        part = dot(a[...], both[first : first + a.shape[1], :])
        lower = part if lower is None else lower + part
        first += a.shape[1]
    piece, upper_piece = width // batches, hidden_width // batches
    for block, upper, ref in ((0, upper_keep, keep_ref), (2, upper_send, send_ref)):
        for d in range(batches):
            parts = []
            for lane in (0, hidden_width):
                for j in (0, 1):
                    row = (block + j) * width + d * piece
                    parts.append(lower[row : row + piece, lane : lane + hidden_width])
            parts.append(upper[d * upper_piece : (d + 1) * upper_piece, :])
            ref[d, :, :] = jnp.concatenate(parts, axis=0).astype(ref.dtype)


def joined_sums(mine, theirs):
    sums = []
    for j in (0, 2):
        sums += halves((mine[j : j + 1] + mine[j + 1 : j + 2]) + (theirs[j : j + 1] + theirs[j + 1 : j + 2]))
    fill = jnp.zeros((12, mine.shape[1]), F32)
    return jnp.concatenate([s.astype(F32) for s in sums] + [fill], axis=0)


def merge_kernel(
    orders, place_ref, keep_ref, got_ref, sums_ref, got_sums_ref, kept_ref, sent_ref, tail_ref
):
    batches, rows, _ = keep_ref.shape
    tail = joined_sums(sums_ref[...].astype(F32), got_sums_ref[...].astype(F32)).astype(BF)
    half = batches // 2
    for i in range(batches):
        d = place_ref[2] ^ jnp.where(place_ref[1] == 0, orders[0][i], orders[1][i])
        value = keep_ref[d, :, :] + got_ref[d, :, :].astype(F32)
        if i < half:
            kept_ref[i, :, :] = value
        else:
            sent_ref[(i - half) * rows : (i - half + 1) * rows, :] = value.astype(BF)
    sent_ref[half * rows :, :] = tail
    tail_ref[...] = tail


def halve_kernel(keep_ref, got_ref, tail_ref, kept_ref, sent_ref, new_tail_ref):
    pieces, rows, _ = keep_ref.shape
    half = pieces // 2
    got_tail = got_ref[pieces * rows :, :].astype(F32)
    tail = joined_sums(tail_ref[...].astype(F32), got_tail).astype(BF)
    for i in range(pieces):
        value = keep_ref[i, :, :] + got_ref[i * rows : (i + 1) * rows, :].astype(F32)
        if i < half:
            kept_ref[i, :, :] = value
        else:
            sent_ref[(i - half) * rows : (i - half + 1) * rows, :] = value.astype(BF)
    sent_ref[half * rows :, :] = tail
    new_tail_ref[...] = tail


def finish_kernel(
    row_total,
    keep_ref,
    got_ref,
    tail_ref,
    stats_ref,
    gain_ref,
    column_ref,
    out_ref,
    gain_out,
    shift_out,
):
    rows = keep_ref.shape[1]
    total = keep_ref[0, :, :] + got_ref[:rows, :].astype(F32)
    sums = joined_sums(tail_ref[...].astype(F32), got_ref[rows:, :].astype(F32))
    pieces = column_ref.shape[1]
    grad_gain = sums[0:1] + sums[1:2]
    grad_shift = sums[2:3] + sums[3:4]
    inv_std = lax.rsqrt(stats_ref[1:2, :] / row_total + 1e-05)
    outer = dot(
        column_ref[...],
        jnp.broadcast_to(grad_shift / row_total, (8, grad_shift.shape[1])),
        ((0,), (0,)),
        lax.Precision.HIGHEST,
    )
    lower = (gain_ref[...] * inv_std) * (
        total[:pieces] - outer - total[pieces : 2 * pieces] * (grad_gain / row_total)
    )
    out_ref[...] = jnp.concatenate([lower, total[2 * pieces : rows]], axis=0).astype(BF)
    gain_out[...] = grad_gain
    shift_out[...] = grad_shift


def place_kernel(
    masks, group_ref, parts_ref, gain_ref, shift_ref, self_ref, neigh_ref, upper_ref
):
    piece = self_ref.shape[0] // len(masks)
    upper_piece = (upper_ref.shape[0] - 8) // len(masks)
    hidden_width = upper_ref.shape[1]
    upper_ref[upper_ref.shape[0] - 8 :, :] = jnp.concatenate(
        [gain_ref[...], shift_ref[...], jnp.zeros((6, hidden_width), F32)], axis=0
    )
    for i, mask in enumerate(masks):
        d = group_ref[0] ^ mask
        rows = parts_ref[i, :, :].astype(F32)
        self_ref[pl.ds(pl.multiple_of(d * piece, piece), piece), :] = rows[:piece]
        neigh_ref[pl.ds(pl.multiple_of(d * piece, piece), piece), :] = rows[piece : 2 * piece]
        upper_ref[pl.ds(pl.multiple_of(d * upper_piece, upper_piece), upper_piece), :] = rows[
            2 * piece :
        ]


def swap(value, axis, mask):
    return lax.ppermute(value, axis, [(i, i ^ mask) for i in range(lax.axis_size(axis))])


def on_device(
    node_feats,
    seed_ids,
    first_hop,
    second_hop,
    lower_self,
    lower_neighbour,
    norm_gain,
    norm_shift,
    upper_self,
    upper_neighbour,
    embed_grad,
):
    feats, batches = lax.axis_size("feat"), lax.axis_size("batch")
    chips = feats // 2
    feat, batch = lax.axis_index("feat"), lax.axis_index("batch")
    core, chip = feat % 2, feat // 2
    table_rows, width = node_feats.shape
    hidden_width = lower_self.shape[1]
    fan_one, fan_two = first_hop.shape[1], second_hop.shape[2]
    slots = fan_one + 1
    own_seeds = embed_grad.shape[0]
    seeds = own_seeds * chips
    row_total = own_seeds * slots * feats * batches
    rows = seeds * slots

    peer_feats = swap(node_feats, "feat", 1)
    peer_self = swap(lower_self, "feat", 1)
    peer_neigh = swap(lower_neighbour, "feat", 1)
    grads = [embed_grad] + [swap(embed_grad, "feat", 2 * mask) for mask in range(1, chips)]

    place = jnp.stack([chip, core, batch]).astype(jnp.int32)
    own_ids = jnp.concatenate([seed_ids[None, :], first_hop.T], axis=0)
    picks = build_rows(place, own_ids, second_hop.transpose(1, 2, 0), table_rows)

    weights = (lower_self, peer_self, lower_neighbour, peer_neigh)
    per_slot = seeds // LANES
    pairs, acrosses, columns = [], [], []
    first = 0
    for share in CHUNKS:
        across, pre_act, column = pick_rows(
            first * per_slot,
            share * per_slot,
            picks,
            node_feats,
            peer_feats,
            weights,
            per_slot,
            (fan_one, fan_two),
        )
        acrosses.append(across)
        columns.append(column)
        mask = 2
        other = swap(pre_act, "feat", mask)
        while 2 * mask < feats:
            mask *= 2
            pre_act = (pre_act.astype(F32) + other.astype(F32)).astype(BF)
            other = swap(pre_act, "feat", mask)
        pairs += [pre_act, other]
        first += share

    tile = jax.ShapeDtypeStruct((8, hidden_width), F32)
    keep, send = pl.pallas_call(
        functools.partial(stats_kernel, len(CHUNKS)),
        out_shape=[tile, tile],
        scratch_shapes=[pltpu.VMEM((rows, hidden_width), F32)],
        compiler_params=params(16),
        name="stats",
    )(*pairs, *columns)

    count = float(rows)
    stats = joined(keep, swap(send, "feat", 1), count)
    mask = 1
    while mask < batches:
        count *= 2
        stats = joined(stats, swap(stats, "batch", mask), count)
        mask *= 2

    gain_row, shift_row = norm_gain[None, :], norm_shift[None, :]
    per_group = 4 * width // batches + hidden_width // batches
    operands = [
        *pairs,
        *acrosses,
        *grads,
        stats,
        gain_row,
        shift_row,
        upper_self,
        upper_neighbour,
    ]
    embedding, keep, send, sums = pl.pallas_call(
        functools.partial(middle_kernel, len(CHUNKS), slots, row_total, batches),
        in_specs=[SMEM] + [VMEM] * len(operands),
        out_shape=[
            jax.ShapeDtypeStruct((own_seeds, hidden_width), BF),
            jax.ShapeDtypeStruct((batches, per_group, hidden_width), F32),
            jax.ShapeDtypeStruct((batches, per_group, hidden_width), BF),
            jax.ShapeDtypeStruct((16, hidden_width), BF),
        ],
        scratch_shapes=[
            pltpu.VMEM((rows, 2 * hidden_width), BF),
            pltpu.VMEM((seeds, hidden_width), F32),
            pltpu.VMEM((seeds, hidden_width), F32),
        ],
        compiler_params=params(24),
        name="middle",
    )(place, *operands)

    bits = [1 << i for i in range(batches.bit_length() - 1)]
    rounds = (bits, bits[1::-1] + bits[2:])

    def order_of(masks):
        order = [0]
        for mask in reversed(masks):
            order = order + [i ^ mask for i in order]
        return order

    def kept_and_sent(pieces):
        return [
            jax.ShapeDtypeStruct((pieces, per_group, hidden_width), F32),
            jax.ShapeDtypeStruct((pieces * per_group + 16, hidden_width), BF),
            jax.ShapeDtypeStruct((16, hidden_width), BF),
        ]

    def exchange(value, step):
        pairs = [
            (f * batches + b, f * batches + (b ^ rounds[f % 2][step]))
            for f in range(feats)
            for b in range(batches)
        ]
        return lax.ppermute(value, ("feat", "batch"), pairs)

    pieces = batches // 2
    kept, sent, tail = pl.pallas_call(
        functools.partial(merge_kernel, [order_of(masks) for masks in rounds]),
        in_specs=[SMEM] + [VMEM] * 4,
        out_shape=kept_and_sent(pieces),
        compiler_params=params(16),
        name="merge",
    )(place, keep, swap(send, "feat", 1), sums, swap(sums, "feat", 1))
    got = exchange(sent, 0)
    for step in range(1, len(bits)):
        pieces //= 2
        kept, sent, tail = pl.pallas_call(
            halve_kernel,
            out_shape=kept_and_sent(pieces),
            compiler_params=params(16),
            name="halve",
        )(kept, got, tail)
        got = exchange(sent, step)

    piece = width // batches
    column = lax.dynamic_slice(stats[2:4], (0, batch * piece), (2, piece)).reshape(1, 2 * piece)
    column = jnp.pad(column, ((0, 7), (0, 0)))
    out_rows = 2 * piece + hidden_width // batches
    line = jax.ShapeDtypeStruct((1, hidden_width), F32)
    done, grad_gain, grad_shift = pl.pallas_call(
        functools.partial(finish_kernel, row_total),
        out_shape=[jax.ShapeDtypeStruct((out_rows, hidden_width), BF), line, line],
        compiler_params=params(16),
        name="finish",
    )(kept, got, tail, stats, gain_row, column)

    gathered, masks = done[None], [0]
    mask = batches // 2
    while mask:
        gathered = jnp.concatenate([gathered, swap(gathered, "batch", mask)], axis=0)
        masks += [m ^ mask for m in masks]
        mask //= 2
    grad_self, grad_neigh, upper = pl.pallas_call(
        functools.partial(place_kernel, tuple(masks)),
        in_specs=[SMEM] + [VMEM] * 3,
        out_shape=[
            jax.ShapeDtypeStruct((width, hidden_width), F32),
            jax.ShapeDtypeStruct((width, hidden_width), F32),
            jax.ShapeDtypeStruct((hidden_width + 8, hidden_width), F32),
        ],
        compiler_params=params(16),
        name="place",
    )(batch.astype(jnp.int32)[None], gathered, grad_gain, grad_shift)
    upper_other = swap(upper, "feat", 1)
    first = jnp.where(core == 0, upper, upper_other)
    second = jnp.where(core == 0, upper_other, upper)
    return (
        embedding,
        grad_self,
        grad_neigh,
        first[:hidden_width],
        second[:hidden_width],
        first[hidden_width],
        first[hidden_width + 1],
    )


CHUNKS = (2, 3, 3, 3)


def solution(mesh):
    return jax.shard_map(
        on_device,
        mesh=mesh,
        in_specs=(
            P("batch", "feat"),
            P("batch"),
            P("batch", None),
            P("batch", None, None),
            P("feat", None),
            P("feat", None),
            P(),
            P(),
            P(),
            P(),
            P(("batch", "feat"), None),
        ),
        out_specs=(
            P(("batch", "feat"), None),
            P("feat", None),
            P("feat", None),
            P(),
            P(),
            P(),
            P(),
        ),
        check_vma=False,
    )
```

```python
import functools

import jax
import jax.numpy as jnp
from jax import lax
from jax.experimental import pallas as pl
from jax.experimental.pallas import tpu as pltpu
from jax.sharding import PartitionSpec as P

BF = jnp.bfloat16
F32 = jnp.float32
LANES = 128
LOW = 256
SLOT = 16
GROUP = LOW // SLOT
MIB = 2**20


def dot(left, right, dims=((1,), (0,)), precision=None):
    return lax.dot_general(
        left, right, (dims, ((), ())), preferred_element_type=F32, precision=precision
    )


def params(mib):
    return pltpu.CompilerParams(vmem_limit_bytes=mib * MIB)


VMEM = pl.BlockSpec(memory_space=pltpu.VMEM)
SMEM = pl.BlockSpec(memory_space=pltpu.SMEM)


def halves(value):
    high = value.astype(BF)
    return high, (value - high.astype(F32)).astype(BF)


def build_kernel(
    place_ref,
    own_ref,
    far_ref,
    out_ref,
    keys,
    own_group,
    spread,
    own_slot,
):
    groups = LANES // GROUP
    per_slot = own_ref.shape[1] // (2 * LANES)
    step, steps = pl.program_id(0), pl.num_programs(0)
    first_core = place_ref[1] == 0

    def mine(ids, p):
        parts = []
        for q in range(per_slot):
            left = ids[:, 2 * q * LANES : (2 * q + 1) * LANES]
            right = ids[:, (2 * q + 1) * LANES : (2 * q + 2) * LANES]
            low_half = lax.broadcasted_iota(jnp.int32, left.shape, 1) < LANES // 2
            even = jnp.where(low_half, left, pltpu.roll(right, LANES // 2, 1))
            odd = jnp.where(low_half, pltpu.roll(left, LANES // 2, 1), right)
            parts.append(jnp.where(first_core, even, odd))
        part = parts[0]
        for q in range(1, per_slot):
            part = jnp.where(p == q, parts[q], part)
        return part

    def flag(shape, test):
        row = lax.broadcasted_iota(jnp.int32, shape, 0)
        lane = lax.broadcasted_iota(jnp.int32, shape, 1)
        return jnp.where(test(row, lane), 1.0, 0.0).astype(BF)

    def widen(part):
        tiled = jnp.concatenate([part.astype(F32).astype(BF)] * groups, axis=0) * own_group[...]
        return dot(tiled, spread[...]).astype(BF) * own_slot[...]

    def wide_of(ids, self_row, p):
        part = mine(ids, p)
        gap = SLOT - part.shape[0]
        part = jnp.concatenate([part, jnp.full((gap, LANES), -1, jnp.int32)], axis=0)
        own = mine(jnp.broadcast_to(self_row, (8, self_row.shape[1])), p).astype(F32)
        high = widen(lax.shift_right_arithmetic(part, 8))
        return high, widen(jnp.bitwise_and(part, LOW - 1)), jnp.concatenate([own, own], axis=1)

    def keys_of(high, low, own):
        gather = flag((groups, LANES), lambda r, c: r == c // SLOT)
        in_group = (lax.broadcasted_iota(jnp.int32, (groups, LOW), 1) % GROUP).astype(F32)
        return dot(gather, high) * GROUP + in_group, dot(gather, low), own

    def keep(values, at):
        for j, value in enumerate(values):
            keys[at, j, :, :] = value

    @pl.when(step == 0)
    def _():
        own_group[...] = flag((LANES, LANES), lambda r, c: r // SLOT == c // GROUP)
        spread[...] = flag((LANES, LOW), lambda r, c: r % GROUP == c % GROUP)
        own_slot[...] = flag((LANES, LOW), lambda r, c: r % SLOT == c // GROUP)
        keep(keys_of(*wide_of(own_ref[1:, :], own_ref[0:1, :], 0)), 0)

    now = step % 2
    later = jnp.minimum(step + 1, steps - 1)
    slot = later // per_slot
    back = jnp.maximum(slot - 1, 0)
    ids = far_ref[back, :, :]
    self_row = own_ref[pl.ds(back + 1, 1), :]
    if per_slot > 1:
        padded = jnp.concatenate(
            [own_ref[1:, :], jnp.full((ids.shape[0] + 1 - own_ref.shape[0], ids.shape[1]), -1, jnp.int32)]
        )
        ids = jnp.where(slot == 0, padded, ids)
        self_row = jnp.where(slot == 0, own_ref[0:1, :], self_row)
    later_wide = wide_of(ids, self_row, later % per_slot)

    index = lax.broadcasted_iota(jnp.int32, (LOW, LOW), 0).astype(BF)
    one = jnp.ones((LOW, LOW), BF)
    zero = jnp.zeros((LOW, LOW), BF)
    def store(g, counts):
        counts = counts.astype(BF)
        for h in range(LOW // GROUP):
            out_ref[g * GROUP : (g + 1) * GROUP, h * LOW : (h + 1) * LOW] = counts[
                h * GROUP : (h + 1) * GROUP, :
            ]

    lanes = lax.broadcasted_iota(jnp.int32, (LANES, LANES), 1)
    ids = jnp.broadcast_to(keys[now, 2, 0:1, :LANES], (LANES, LANES)).T.astype(jnp.int32)
    low = jnp.bitwise_and(ids, LOW - 1)
    high = lax.shift_right_logical(ids, 8).astype(BF)
    bases = [
        jnp.where(lanes + LANES * part == low, 1.0, 0.0).astype(BF) for part in range(LOW // LANES)
    ]
    tiles = [(h, part) for h in range(out_ref.shape[1] // LOW) for part in range(LOW // LANES)]
    share = -(-len(tiles) // groups)
    waiting = []
    later_keys = None
    for g in range(groups):
        left = jnp.where(index == keys[now, 0, g : g + 1, :].astype(BF), one, zero)
        right = jnp.where(index == keys[now, 1, g : g + 1, :].astype(BF), one, zero)
        waiting.append((g, dot(left, right, ((1,), (1,)))))
        if g == 6:
            later_keys = keys_of(*later_wide)
        for h, part in tiles[g * share : (g + 1) * share]:
            at = h * LOW + part * LANES
            out_ref[LANES:, at : at + LANES] = jnp.where(
                high == BF(h), bases[part], jnp.zeros_like(bases[part])
            )
        if len(waiting) > 1:
            store(*waiting.pop(0))
    for item in waiting:
        store(*item)
    keep(later_keys, 1 - now)


def build_rows(place, own, far, table_rows):
    steps = own.shape[0] * own.shape[1] // (2 * LANES)
    groups = LANES // GROUP
    return pl.pallas_call(
        build_kernel,
        grid=(steps,),
        in_specs=[SMEM, VMEM, VMEM],
        out_specs=pl.BlockSpec((2 * LANES, table_rows), lambda i: (i, 0)),
        out_shape=jax.ShapeDtypeStruct((steps * 2 * LANES, table_rows), BF),
        scratch_shapes=[
            pltpu.VMEM((2, 3, groups, LOW), F32),
            pltpu.VMEM((LANES, LANES), BF),
            pltpu.VMEM((LANES, LOW), BF),
            pltpu.VMEM((LANES, LOW), BF),
        ],
        compiler_params=params(12),
        cost_estimate=pl.CostEstimate(
            flops=2 * steps * groups * LOW**3,
            bytes_accessed=4 * steps * LANES * table_rows,
            transcendentals=0,
        ),
        name="build_rows",
    )(place, own, far)


def pick_kernel(
    first_block,
    start,
    blocks,
    per_slot,
    fans,
    rows_ref,
    own_ref,
    peer_ref,
    self_own_ref,
    self_peer_ref,
    neigh_own_ref,
    neigh_peer_ref,
    across_ref,
    pre_ref,
    column_ref,
):
    width = own_ref.shape[1]
    step = pl.program_id(0)
    tables = (own_ref, peer_ref)
    picked = [
        [dot(rows_ref[at : at + 2 * LANES, :], table[...]) for table in tables]
        for at in range(start, start + 2 * blocks * LANES, 2 * LANES)
    ]
    total = None
    columns = []
    for i in range(2):
        self_parts, neigh_parts = [], []
        for b in range(blocks):
            block = first_block + step * blocks + b
            share = jnp.where(block < per_slot, F32(1.0 / fans[0]), F32(1.0 / fans[1]))
            neigh_parts.append((picked[b][i][:LANES] * share).astype(BF))
            self_parts.append(picked[b][i][LANES:].astype(BF))
        weights = ((self_own_ref, neigh_own_ref), (self_peer_ref, neigh_peer_ref))[i]
        for j, parts in enumerate((self_parts, neigh_parts)):
            part = dot(jnp.concatenate(parts, axis=0), weights[j][...])
            total = part if total is None else total + part
            columns.append(
                sum(jnp.sum(p.astype(F32).reshape(-1, 8, width), axis=0) for p in parts)
            )
            for b in range(blocks):
                across_ref[
                    (2 * i + j) * width : (2 * i + j + 1) * width, b * LANES : (b + 1) * LANES
                ] = parts[b].T
    pre_ref[...] = total.astype(BF)
    columns = jnp.concatenate(columns, axis=1)

    @pl.when(step == 0)
    def _():
        column_ref[...] = columns

    @pl.when(step > 0)
    def _():
        column_ref[...] += columns


def pick_rows(first_block, count, rows, own, peer, weights, per_slot, fans):
    table_rows, width = own.shape
    hidden_width = weights[0].shape[1]
    total = count * LANES
    resident = rows.size * 2 <= 32 * MIB
    if resident:
        blocks, start, rows_spec = count, first_block * 2 * LANES, VMEM
    else:
        blocks, start = per_slot, 0
        skip = first_block // blocks
        rows_spec = pl.BlockSpec((blocks * 2 * LANES, table_rows), lambda i: (i + skip, 0))
    return pl.pallas_call(
        functools.partial(pick_kernel, first_block, start, blocks, per_slot, fans),
        grid=(count // blocks,),
        in_specs=[rows_spec] + [VMEM] * 6,
        out_specs=[
            pl.BlockSpec((4 * width, blocks * LANES), lambda i: (0, i)),
            pl.BlockSpec((blocks * LANES, hidden_width), lambda i: (i, 0)),
            pl.BlockSpec((8, 4 * width), lambda i: (0, 0)),
        ],
        out_shape=[
            jax.ShapeDtypeStruct((4 * width, total), BF),
            jax.ShapeDtypeStruct((total, hidden_width), BF),
            jax.ShapeDtypeStruct((8, 4 * width), F32),
        ],
        compiler_params=params(12 if resident else 22),
        cost_estimate=pl.CostEstimate(
            flops=8 * total * table_rows * width,
            bytes_accessed=2 * total * table_rows + 4 * table_rows * width,
            transcendentals=0,
        ),
        name="pick_rows",
    )(rows, own, peer, *weights)


def stats_kernel(chunks, *refs):
    pairs, columns = refs[: 2 * chunks], refs[2 * chunks : 3 * chunks]
    keep_ref, send_ref, total = refs[3 * chunks :]
    width = columns[0].shape[1] // 4
    rows = total.shape[0]
    mean = 0.0
    first = 0
    for i in range(chunks):
        value = pairs[2 * i][...].astype(F32) + pairs[2 * i + 1][...].astype(F32)
        total[first : first + value.shape[0], :] = value
        mean = mean + jnp.sum(value, axis=0, keepdims=True)
        first += value.shape[0]
    mean = mean / rows
    gap = total[...] - mean
    square = jnp.sum(gap * gap, axis=0, keepdims=True)
    column = jnp.sum(sum(c[...] for c in columns), axis=0, keepdims=True)
    pad = jnp.zeros((4, mean.shape[1]), F32)
    lanes = mean.shape[1] - width
    for ref, first in ((keep_ref, 0), (send_ref, 2)):
        parts = [column[:, (first + j) * width : (first + j + 1) * width] for j in range(2)]
        if lanes:
            parts = [jnp.concatenate([p, jnp.zeros((1, lanes), F32)], axis=1) for p in parts]
        ref[...] = jnp.concatenate([mean, square, *parts, pad], axis=0)


def join_kernel(count, mine_ref, other_ref, out_ref):
    mine, other = mine_ref[...], other_ref[...]
    gap = mine[0:1] - other[0:1]
    out_ref[...] = jnp.concatenate(
        [
            (mine[0:1] + other[0:1]) * 0.5,
            mine[1:2] + other[1:2] + gap * gap * (count * 0.5),
            mine[2:] + other[2:],
        ],
        axis=0,
    )


def joined(mine, other, count):
    return pl.pallas_call(
        functools.partial(join_kernel, count),
        in_specs=[VMEM, VMEM],
        out_specs=VMEM,
        out_shape=jax.ShapeDtypeStruct(mine.shape, mine.dtype),
        compiler_params=params(1),
        name="join",
    )(mine, other)


def middle_kernel(
    chunks,
    slots,
    row_total,
    batches,
    place_ref,
    *refs,
):
    pairs, acrosses = refs[: 2 * chunks], refs[2 * chunks : 3 * chunks]
    chips = len(refs) - 3 * chunks - 12
    grad_parts = refs[3 * chunks : 3 * chunks + chips]
    (
        stats_ref,
        gain_ref,
        shift_ref,
        upper_self_ref,
        upper_neigh_ref,
        embed_ref,
        keep_ref,
        send_ref,
        sums_ref,
        both,
        embed_all,
        grad_all,
    ) = refs[3 * chunks + chips :]
    own_seeds, hidden_width = grad_parts[0].shape
    seeds = own_seeds * chips
    width = acrosses[0].shape[0] // 4
    for mask, part in enumerate(grad_parts):
        at = pl.multiple_of((place_ref[0] ^ mask) * own_seeds, own_seeds)
        grad_all[pl.ds(at, own_seeds), :] = part[...].astype(F32)
    fan_one = slots - 1
    mean = stats_ref[0:1, :]
    inv_std = lax.rsqrt(stats_ref[1:2, :] / row_total + 1e-05)
    gain, shift = gain_ref[...], shift_ref[...]
    grad = grad_all[...].astype(BF)
    d_self = dot(grad, upper_self_ref[...], ((1,), (1,)))
    d_mean = dot(grad, upper_neigh_ref[...], ((1,), (1,))) / fan_one
    gain_sum = shift_sum = hidden_sum = own_rows = None
    places = [(i, k) for i in range(chunks) for k in range(pairs[2 * i].shape[0] // seeds)]
    for slot, (i, k) in enumerate(places):
        span = slice(k * seeds, (k + 1) * seeds)
        pre_act = pairs[2 * i][span, :].astype(F32) + pairs[2 * i + 1][span, :].astype(F32)
        span = slice(slot * seeds, (slot + 1) * seeds)
        normed = (pre_act - mean) * inv_std
        shifted = gain * normed + shift
        sigmoid_v = 1.0 / (1.0 + jnp.exp(-shifted))
        hidden = (shifted * sigmoid_v).astype(BF)
        if slot == 0:
            own_rows = hidden
        else:
            hidden_sum = hidden.astype(F32) + (0.0 if hidden_sum is None else hidden_sum)
        grad_hidden = d_self if slot == 0 else d_mean
        grad_shifted = grad_hidden * sigmoid_v * (1.0 + shifted * (1.0 - sigmoid_v))
        gain_part = grad_shifted * normed
        gain_sum = gain_part if gain_sum is None else gain_sum + gain_part
        shift_sum = grad_shifted if shift_sum is None else shift_sum + grad_shifted
        both[span, :hidden_width] = grad_shifted.astype(BF)
        both[span, hidden_width:] = normed.astype(BF)
    hidden_mean = (hidden_sum / fan_one).astype(BF)
    embed_all[...] = dot(own_rows, upper_self_ref[...]) + dot(hidden_mean, upper_neigh_ref[...])
    start = pl.multiple_of(place_ref[0] * own_seeds, own_seeds)
    embed_ref[...] = embed_all[pl.ds(start, own_seeds), :].astype(BF)
    upper_self_part = dot(own_rows, grad, ((0,), (0,)))
    upper_neigh_part = dot(hidden_mean, grad, ((0,), (0,)))
    first_core = place_ref[1] == 0
    upper_keep = jnp.where(first_core, upper_self_part, upper_neigh_part)
    upper_send = jnp.where(first_core, upper_neigh_part, upper_self_part)
    gain_high, gain_low = halves(jnp.sum(gain_sum, axis=0, keepdims=True))
    shift_high, shift_low = halves(jnp.sum(shift_sum, axis=0, keepdims=True))
    sums = [gain_high, gain_low, shift_high, shift_low]
    sums = jnp.concatenate(
        [s.astype(F32) for s in sums] + [jnp.zeros((12, hidden_width), F32)], axis=0
    ).astype(BF)
    sums_ref[...] = sums
    per_group = keep_ref.shape[1]
    send_ref[batches * per_group :, :] = sums
    lower = None
    first = 0
    for a in acrosses:
        part = dot(a[...], both[first : first + a.shape[1], :])
        lower = part if lower is None else lower + part
        first += a.shape[1]
    piece, upper_piece = width // batches, hidden_width // batches
    for block, upper in ((0, upper_keep), (2, upper_send)):
        for d in range(batches):
            parts = []
            for lane in (0, hidden_width):
                for j in (0, 1):
                    row = (block + j) * width + d * piece
                    parts.append(lower[row : row + piece, lane : lane + hidden_width])
            parts.append(upper[d * upper_piece : (d + 1) * upper_piece, :])
            value = jnp.concatenate(parts, axis=0)
            if block == 0:
                keep_ref[d, :, :] = value
            else:
                send_ref[d * per_group : (d + 1) * per_group, :] = value.astype(BF)


def joined_sums(mine, theirs):
    sums = []
    for j in (0, 2):
        sums += halves((mine[j : j + 1] + mine[j + 1 : j + 2]) + (theirs[j : j + 1] + theirs[j + 1 : j + 2]))
    fill = jnp.zeros((12, mine.shape[1]), F32)
    return jnp.concatenate([s.astype(F32) for s in sums] + [fill], axis=0)


def merge_kernel(
    orders, place_ref, keep_ref, got_ref, sums_ref, kept_ref, sent_ref, tail_ref
):
    batches, rows, _ = keep_ref.shape
    got_sums = got_ref[batches * rows :, :].astype(F32)
    tail = joined_sums(sums_ref[...].astype(F32), got_sums).astype(BF)
    half = batches // 2
    for i in range(batches):
        d = place_ref[2] ^ jnp.where(place_ref[1] == 0, orders[0][i], orders[1][i])
        at = pl.multiple_of(d * rows, rows)
        value = keep_ref[d, :, :] + got_ref[pl.ds(at, rows), :].astype(F32)
        if i < half:
            kept_ref[i, :, :] = value
        else:
            sent_ref[(i - half) * rows : (i - half + 1) * rows, :] = value.astype(BF)
    sent_ref[half * rows :, :] = tail
    tail_ref[...] = tail


def halve_kernel(keep_ref, got_ref, tail_ref, kept_ref, sent_ref, new_tail_ref):
    pieces, rows, _ = keep_ref.shape
    half = pieces // 2
    got_tail = got_ref[pieces * rows :, :].astype(F32)
    tail = joined_sums(tail_ref[...].astype(F32), got_tail).astype(BF)
    for i in range(pieces):
        value = keep_ref[i, :, :] + got_ref[i * rows : (i + 1) * rows, :].astype(F32)
        if i < half:
            kept_ref[i, :, :] = value
        else:
            sent_ref[(i - half) * rows : (i - half + 1) * rows, :] = value.astype(BF)
    sent_ref[half * rows :, :] = tail
    new_tail_ref[...] = tail


def both_kernel(keep_ref, got_ref, tail_ref, sent_ref, new_tail_ref):
    pieces, rows, _ = keep_ref.shape
    got_tail = got_ref[pieces * rows :, :].astype(F32)
    tail = joined_sums(tail_ref[...].astype(F32), got_tail).astype(BF)
    for i in range(pieces):
        value = keep_ref[i, :, :] + got_ref[i * rows : (i + 1) * rows, :].astype(F32)
        sent_ref[i * rows : (i + 1) * rows, :] = value.astype(BF)
    sent_ref[pieces * rows :, :] = tail
    new_tail_ref[...] = tail


def finish_kernel(
    row_total, sent_ref, got_ref, tail_ref, stats_ref, gain_ref, column_ref, out_ref, sums_ref
):
    rows = (sent_ref.shape[0] - 16) // 2
    sums = joined_sums(tail_ref[...].astype(F32), got_ref[2 * rows :, :].astype(F32))
    pieces = column_ref.shape[2]
    grad_gain = sums[0:1] + sums[1:2]
    grad_shift = sums[2:3] + sums[3:4]
    scale = gain_ref[...] * lax.rsqrt(stats_ref[1:2, :] / row_total + 1e-05)
    shift_part = jnp.broadcast_to(grad_shift / row_total, (8, grad_shift.shape[1]))
    for i in range(2):
        mine = sent_ref[i * rows : (i + 1) * rows, :].astype(F32)
        total = mine + got_ref[(1 - i) * rows : (2 - i) * rows, :].astype(F32)
        outer = dot(column_ref[i, :, :], shift_part, ((0,), (0,)), lax.Precision.HIGHEST)
        lower = scale * (
            total[:pieces] - outer - total[pieces : 2 * pieces] * (grad_gain / row_total)
        )
        out_ref[i, :, :] = jnp.concatenate([lower, total[2 * pieces : rows]], axis=0).astype(BF)
    sums_ref[...] = sums.astype(BF)


def upper_kernel(masks, place_ref, parts_ref, sums_ref, upper_ref):
    rows = upper_ref.shape[0] - 16
    piece = rows // len(masks)
    for i, mask in enumerate(masks):
        at = pl.multiple_of((place_ref[2] ^ mask) * piece, piece)
        upper_ref[pl.ds(at, piece), :] = parts_ref[i, parts_ref.shape[1] - piece :, :].astype(F32)
    upper_ref[rows:, :] = sums_ref[...].astype(F32)


def lower_kernel(masks, place_ref, parts_ref, self_ref, neigh_ref):
    piece = self_ref.shape[0] // len(masks)
    for i, mask in enumerate(masks):
        at = pl.ds(pl.multiple_of((place_ref[2] ^ mask) * piece, piece), piece)
        rows = parts_ref[i, :, :].astype(F32)
        self_ref[at, :] = rows[:piece]
        neigh_ref[at, :] = rows[piece : 2 * piece]


def last_kernel(place_ref, mine_ref, other_ref, self_ref, neigh_ref, gain_ref, shift_ref):
    rows = self_ref.shape[0]
    first_core = place_ref[1] == 0
    first = jnp.where(first_core, mine_ref[...], other_ref[...])
    self_ref[...] = first[:rows]
    neigh_ref[...] = jnp.where(first_core, other_ref[:rows, :], mine_ref[:rows, :])
    gain_ref[...] = first[rows : rows + 1] + first[rows + 1 : rows + 2]
    shift_ref[...] = first[rows + 2 : rows + 3] + first[rows + 3 : rows + 4]


def swap(value, axis, mask):
    return lax.ppermute(value, axis, [(i, i ^ mask) for i in range(lax.axis_size(axis))])


def on_device(
    node_feats,
    seed_ids,
    first_hop,
    second_hop,
    lower_self,
    lower_neighbour,
    norm_gain,
    norm_shift,
    upper_self,
    upper_neighbour,
    embed_grad,
):
    feats, batches = lax.axis_size("feat"), lax.axis_size("batch")
    chips = feats // 2
    feat, batch = lax.axis_index("feat"), lax.axis_index("batch")
    core, chip = feat % 2, feat // 2
    table_rows, width = node_feats.shape
    hidden_width = lower_self.shape[1]
    fan_one, fan_two = first_hop.shape[1], second_hop.shape[2]
    slots = fan_one + 1
    own_seeds = embed_grad.shape[0]
    seeds = own_seeds * chips
    row_total = own_seeds * slots * feats * batches
    rows = seeds * slots

    peer_feats = swap(node_feats, "feat", 1)
    peer_self = swap(lower_self, "feat", 1)
    peer_neigh = swap(lower_neighbour, "feat", 1)
    grads = [embed_grad] + [swap(embed_grad, "feat", 2 * mask) for mask in range(1, chips)]

    place = jnp.stack([chip, core, batch]).astype(jnp.int32)
    own_ids = jnp.concatenate([seed_ids[None, :], first_hop.T], axis=0)
    picks = build_rows(place, own_ids, second_hop.transpose(1, 2, 0), table_rows)

    weights = (lower_self, peer_self, lower_neighbour, peer_neigh)
    per_slot = seeds // LANES
    pairs, acrosses, columns = [], [], []
    first = 0
    for share in CHUNKS:
        across, pre_act, column = pick_rows(
            first * per_slot,
            share * per_slot,
            picks,
            node_feats,
            peer_feats,
            weights,
            per_slot,
            (fan_one, fan_two),
        )
        acrosses.append(across)
        columns.append(column)
        mask = 2
        other = swap(pre_act, "feat", mask)
        while 2 * mask < feats:
            mask *= 2
            pre_act = (pre_act.astype(F32) + other.astype(F32)).astype(BF)
            other = swap(pre_act, "feat", mask)
        pairs += [pre_act, other]
        first += share

    tile = jax.ShapeDtypeStruct((8, hidden_width), F32)
    keep, send = pl.pallas_call(
        functools.partial(stats_kernel, len(CHUNKS)),
        out_shape=[tile, tile],
        scratch_shapes=[pltpu.VMEM((rows, hidden_width), F32)],
        compiler_params=params(16),
        name="stats",
    )(*pairs, *columns)

    count = float(rows)
    stats = joined(keep, swap(send, "feat", 1), count)
    mask = 1
    while mask < batches:
        count *= 2
        stats = joined(stats, swap(stats, "batch", mask), count)
        mask *= 2

    gain_row, shift_row = norm_gain[None, :], norm_shift[None, :]
    per_group = 4 * width // batches + hidden_width // batches
    operands = [
        *pairs,
        *acrosses,
        *grads,
        stats,
        gain_row,
        shift_row,
        upper_self,
        upper_neighbour,
    ]
    embedding, keep, send, sums = pl.pallas_call(
        functools.partial(middle_kernel, len(CHUNKS), slots, row_total, batches),
        in_specs=[SMEM] + [VMEM] * len(operands),
        out_shape=[
            jax.ShapeDtypeStruct((own_seeds, hidden_width), BF),
            jax.ShapeDtypeStruct((batches, per_group, hidden_width), F32),
            jax.ShapeDtypeStruct((batches * per_group + 16, hidden_width), BF),
            jax.ShapeDtypeStruct((16, hidden_width), BF),
        ],
        scratch_shapes=[
            pltpu.VMEM((rows, 2 * hidden_width), BF),
            pltpu.VMEM((seeds, hidden_width), F32),
            pltpu.VMEM((seeds, hidden_width), F32),
        ],
        compiler_params=params(24),
        name="middle",
    )(place, *operands)

    bits = [1 << i for i in range(batches.bit_length() - 1)]
    rounds = (bits, bits[1::-1] + bits[2:])

    def order_of(masks):
        order = [0]
        for mask in reversed(masks):
            order = order + [i ^ mask for i in order]
        return order

    def kept_and_sent(pieces):
        return [
            jax.ShapeDtypeStruct((pieces, per_group, hidden_width), F32),
            jax.ShapeDtypeStruct((pieces * per_group + 16, hidden_width), BF),
            jax.ShapeDtypeStruct((16, hidden_width), BF),
        ]

    def exchange(value, step):
        pairs = [
            (f * batches + b, f * batches + (b ^ rounds[f % 2][step]))
            for f in range(feats)
            for b in range(batches)
        ]
        return lax.ppermute(value, ("feat", "batch"), pairs)

    pieces = batches // 2
    kept, sent, tail = pl.pallas_call(
        functools.partial(merge_kernel, [order_of(masks) for masks in rounds]),
        in_specs=[SMEM] + [VMEM] * 3,
        out_shape=kept_and_sent(pieces),
        compiler_params=params(16),
        name="merge",
    )(place, keep, swap(send, "feat", 1), sums)
    got = exchange(sent, 0)
    for step in range(1, len(bits) - 1):
        pieces //= 2
        kept, sent, tail = pl.pallas_call(
            halve_kernel,
            out_shape=kept_and_sent(pieces),
            compiler_params=params(16),
            name="halve",
        )(kept, got, tail)
        got = exchange(sent, step)
    sent, tail = pl.pallas_call(
        both_kernel,
        out_shape=kept_and_sent(pieces)[1:],
        compiler_params=params(16),
        name="both",
    )(kept, got, tail)
    got = exchange(sent, len(bits) - 1)

    piece = width // batches
    columns = []
    for mask in (0, batches // 2):
        at = (0, (batch ^ mask) * piece)
        columns.append(lax.dynamic_slice(stats[2:4], at, (2, piece)).reshape(1, 1, 2 * piece))
    column = jnp.pad(jnp.concatenate(columns, axis=0), ((0, 0), (0, 7), (0, 0)))
    out_rows = 2 * piece + hidden_width // batches
    done, sums = pl.pallas_call(
        functools.partial(finish_kernel, row_total),
        out_shape=[
            jax.ShapeDtypeStruct((2, out_rows, hidden_width), BF),
            jax.ShapeDtypeStruct((16, hidden_width), BF),
        ],
        compiler_params=params(16),
        name="finish",
    )(sent, got, tail, stats, gain_row, column)

    gathered, masks = done, [0, batches // 2]
    mask = batches // 4
    while mask:
        gathered = jnp.concatenate([gathered, swap(gathered, "batch", mask)], axis=0)
        masks += [m ^ mask for m in masks]
        mask //= 2
    square = jax.ShapeDtypeStruct((hidden_width, hidden_width), F32)
    tall = jax.ShapeDtypeStruct((width, hidden_width), F32)
    line = jax.ShapeDtypeStruct((1, hidden_width), F32)
    upper = pl.pallas_call(
        functools.partial(upper_kernel, tuple(masks)),
        in_specs=[SMEM, VMEM, VMEM],
        out_shape=jax.ShapeDtypeStruct((hidden_width + 16, hidden_width), F32),
        compiler_params=params(4),
        name="upper",
    )(place, gathered, sums)
    upper_other = swap(upper, "feat", 1)
    grad_self, grad_neigh = pl.pallas_call(
        functools.partial(lower_kernel, tuple(masks)),
        in_specs=[SMEM, VMEM],
        out_shape=[tall, tall],
        compiler_params=params(4),
        cost_estimate=pl.CostEstimate(
            flops=0, bytes_accessed=12 * width * hidden_width, transcendentals=0
        ),
        name="lower",
    )(place, gathered)
    grad_upper_self, grad_upper_neigh, grad_gain, grad_shift = pl.pallas_call(
        last_kernel,
        in_specs=[SMEM, VMEM, VMEM],
        out_shape=[square, square, line, line],
        compiler_params=params(4),
        name="last",
    )(place, upper, upper_other)
    return (
        embedding,
        grad_self,
        grad_neigh,
        grad_upper_self,
        grad_upper_neigh,
        grad_gain[0],
        grad_shift[0],
    )


CHUNKS = (2, 3, 3, 3)


def solution(mesh):
    return jax.shard_map(
        on_device,
        mesh=mesh,
        in_specs=(
            P("batch", "feat"),
            P("batch"),
            P("batch", None),
            P("batch", None, None),
            P("feat", None),
            P("feat", None),
            P(),
            P(),
            P(),
            P(),
            P(("batch", "feat"), None),
        ),
        out_specs=(
            P(("batch", "feat"), None),
            P("feat", None),
            P("feat", None),
            P(),
            P(),
            P(),
            P(),
        ),
        check_vma=False,
    )
```

```python
import functools

import jax
import jax.numpy as jnp
from jax import lax
from jax.experimental import pallas as pl
from jax.experimental.pallas import tpu as pltpu
from jax.sharding import PartitionSpec as P

BF = jnp.bfloat16
F32 = jnp.float32
LANES = 128
LOW = 256
SLOT = 16
GROUP = LOW // SLOT
MIB = 2**20


def dot(left, right, dims=((1,), (0,)), precision=None):
    return lax.dot_general(
        left, right, (dims, ((), ())), preferred_element_type=F32, precision=precision
    )


def params(mib):
    return pltpu.CompilerParams(vmem_limit_bytes=mib * MIB)


VMEM = pl.BlockSpec(memory_space=pltpu.VMEM)


def here():
    feat = lax.axis_index("feat")
    return lax.shift_right_logical(feat, 1), jnp.bitwise_and(feat, 1), lax.axis_index("batch")


def halves(value):
    high = value.astype(BF)
    return high, (value - high.astype(F32)).astype(BF)


def build_kernel(
    own_ref,
    far_ref,
    out_ref,
    keys,
    own_group,
    spread,
    own_slot,
):
    place = here()
    groups = LANES // GROUP
    per_slot = own_ref.shape[1] // (2 * LANES)
    step, steps = pl.program_id(0), pl.num_programs(0)
    first_core = place[1] == 0

    def mine(ids, p):
        parts = []
        for q in range(per_slot):
            left = ids[:, 2 * q * LANES : (2 * q + 1) * LANES]
            right = ids[:, (2 * q + 1) * LANES : (2 * q + 2) * LANES]
            low_half = lax.broadcasted_iota(jnp.int32, left.shape, 1) < LANES // 2
            even = jnp.where(low_half, left, pltpu.roll(right, LANES // 2, 1))
            odd = jnp.where(low_half, pltpu.roll(left, LANES // 2, 1), right)
            parts.append(jnp.where(first_core, even, odd))
        part = parts[0]
        for q in range(1, per_slot):
            part = jnp.where(p == q, parts[q], part)
        return part

    def flag(shape, test):
        row = lax.broadcasted_iota(jnp.int32, shape, 0)
        lane = lax.broadcasted_iota(jnp.int32, shape, 1)
        return jnp.where(test(row, lane), 1.0, 0.0).astype(BF)

    def widen(part):
        tiled = jnp.concatenate([part.astype(F32).astype(BF)] * groups, axis=0) * own_group[...]
        return dot(tiled, spread[...]).astype(BF) * own_slot[...]

    def wide_of(ids, self_row, p):
        part = mine(ids, p)
        gap = SLOT - part.shape[0]
        part = jnp.concatenate([part, jnp.full((gap, LANES), -1, jnp.int32)], axis=0)
        own = mine(jnp.broadcast_to(self_row, (8, self_row.shape[1])), p).astype(F32)
        high = widen(lax.shift_right_arithmetic(part, 8))
        return high, widen(jnp.bitwise_and(part, LOW - 1)), jnp.concatenate([own, own], axis=1)

    def keys_of(high, low, own):
        gather = flag((groups, LANES), lambda r, c: r == c // SLOT)
        in_group = (lax.broadcasted_iota(jnp.int32, (groups, LOW), 1) % GROUP).astype(F32)
        return dot(gather, high) * GROUP + in_group, dot(gather, low), own

    def keep(values, at):
        for j, value in enumerate(values):
            keys[at, j, :, :] = value

    @pl.when(step == 0)
    def _():
        own_group[...] = flag((LANES, LANES), lambda r, c: r // SLOT == c // GROUP)
        spread[...] = flag((LANES, LOW), lambda r, c: r % GROUP == c % GROUP)
        own_slot[...] = flag((LANES, LOW), lambda r, c: r % SLOT == c // GROUP)
        keep(keys_of(*wide_of(own_ref[1:, :], own_ref[0:1, :], 0)), 0)

    now = step % 2
    later = jnp.minimum(step + 1, steps - 1)
    slot = later // per_slot
    back = jnp.maximum(slot - 1, 0)
    ids = far_ref[back, :, :]
    self_row = own_ref[pl.ds(back + 1, 1), :]
    if per_slot > 1:
        padded = jnp.concatenate(
            [own_ref[1:, :], jnp.full((ids.shape[0] + 1 - own_ref.shape[0], ids.shape[1]), -1, jnp.int32)]
        )
        ids = jnp.where(slot == 0, padded, ids)
        self_row = jnp.where(slot == 0, own_ref[0:1, :], self_row)
    later_wide = wide_of(ids, self_row, later % per_slot)

    index = lax.broadcasted_iota(jnp.int32, (LOW, LOW), 0).astype(BF)
    one = jnp.ones((LOW, LOW), BF)
    zero = jnp.zeros((LOW, LOW), BF)
    def store(g, counts):
        counts = counts.astype(BF)
        for h in range(LOW // GROUP):
            out_ref[g * GROUP : (g + 1) * GROUP, h * LOW : (h + 1) * LOW] = counts[
                h * GROUP : (h + 1) * GROUP, :
            ]

    lanes = lax.broadcasted_iota(jnp.int32, (LANES, LANES), 1)
    ids = jnp.broadcast_to(keys[now, 2, 0:1, :LANES], (LANES, LANES)).T.astype(jnp.int32)
    low = jnp.bitwise_and(ids, LOW - 1)
    high = lax.shift_right_logical(ids, 8).astype(BF)
    bases = [
        jnp.where(lanes + LANES * part == low, 1.0, 0.0).astype(BF) for part in range(LOW // LANES)
    ]
    tiles = [(h, part) for h in range(out_ref.shape[1] // LOW) for part in range(LOW // LANES)]
    share = -(-len(tiles) // groups)
    waiting = []
    later_keys = None
    for g in range(groups):
        left = jnp.where(index == keys[now, 0, g : g + 1, :].astype(BF), one, zero)
        right = jnp.where(index == keys[now, 1, g : g + 1, :].astype(BF), one, zero)
        waiting.append((g, dot(left, right, ((1,), (1,)))))
        if g == 6:
            later_keys = keys_of(*later_wide)
        for h, part in tiles[g * share : (g + 1) * share]:
            at = h * LOW + part * LANES
            out_ref[LANES:, at : at + LANES] = jnp.where(
                high == BF(h), bases[part], jnp.zeros_like(bases[part])
            )
        if len(waiting) > 1:
            store(*waiting.pop(0))
    for item in waiting:
        store(*item)
    keep(later_keys, 1 - now)


def build_rows(own, far, table_rows):
    steps = own.shape[0] * own.shape[1] // (2 * LANES)
    groups = LANES // GROUP
    return pl.pallas_call(
        build_kernel,
        grid=(steps,),
        in_specs=[VMEM, VMEM],
        out_specs=pl.BlockSpec((2 * LANES, table_rows), lambda i: (i, 0)),
        out_shape=jax.ShapeDtypeStruct((steps * 2 * LANES, table_rows), BF),
        scratch_shapes=[
            pltpu.VMEM((2, 3, groups, LOW), F32),
            pltpu.VMEM((LANES, LANES), BF),
            pltpu.VMEM((LANES, LOW), BF),
            pltpu.VMEM((LANES, LOW), BF),
        ],
        compiler_params=params(12),
        cost_estimate=pl.CostEstimate(
            flops=2 * steps * groups * LOW**3,
            bytes_accessed=4 * steps * LANES * table_rows,
            transcendentals=0,
        ),
        name="build_rows",
    )(own, far)


def pick_kernel(
    first_block,
    start,
    blocks,
    per_slot,
    fans,
    rows_ref,
    own_ref,
    peer_ref,
    self_own_ref,
    self_peer_ref,
    neigh_own_ref,
    neigh_peer_ref,
    across_ref,
    pre_ref,
    column_ref,
):
    width = own_ref.shape[1]
    step = pl.program_id(0)
    tables = (own_ref, peer_ref)
    picked = [
        [dot(rows_ref[at : at + 2 * LANES, :], table[...]) for table in tables]
        for at in range(start, start + 2 * blocks * LANES, 2 * LANES)
    ]
    total = None
    columns = []
    for i in range(2):
        self_parts, neigh_parts = [], []
        for b in range(blocks):
            block = first_block + step * blocks + b
            share = jnp.where(block < per_slot, F32(1.0 / fans[0]), F32(1.0 / fans[1]))
            neigh_parts.append((picked[b][i][:LANES] * share).astype(BF))
            self_parts.append(picked[b][i][LANES:].astype(BF))
        weights = ((self_own_ref, neigh_own_ref), (self_peer_ref, neigh_peer_ref))[i]
        for j, parts in enumerate((self_parts, neigh_parts)):
            part = dot(jnp.concatenate(parts, axis=0), weights[j][...])
            total = part if total is None else total + part
            columns.append(
                sum(jnp.sum(p.astype(F32).reshape(-1, 8, width), axis=0) for p in parts)
            )
            for b in range(blocks):
                across_ref[
                    (2 * i + j) * width : (2 * i + j + 1) * width, b * LANES : (b + 1) * LANES
                ] = parts[b].T
    pre_ref[...] = total.astype(BF)
    columns = jnp.concatenate(columns, axis=1)

    @pl.when(step == 0)
    def _():
        column_ref[...] = columns

    @pl.when(step > 0)
    def _():
        column_ref[...] += columns


def pick_rows(first_block, count, rows, own, peer, weights, per_slot, fans):
    table_rows, width = own.shape
    hidden_width = weights[0].shape[1]
    total = count * LANES
    resident = rows.size * 2 <= 32 * MIB
    if resident:
        blocks, start, rows_spec = count, first_block * 2 * LANES, VMEM
    else:
        blocks, start = per_slot, 0
        skip = first_block // blocks
        rows_spec = pl.BlockSpec((blocks * 2 * LANES, table_rows), lambda i: (i + skip, 0))
    return pl.pallas_call(
        functools.partial(pick_kernel, first_block, start, blocks, per_slot, fans),
        grid=(count // blocks,),
        in_specs=[rows_spec] + [VMEM] * 6,
        out_specs=[
            pl.BlockSpec((4 * width, blocks * LANES), lambda i: (0, i)),
            pl.BlockSpec((blocks * LANES, hidden_width), lambda i: (i, 0)),
            pl.BlockSpec((8, 4 * width), lambda i: (0, 0)),
        ],
        out_shape=[
            jax.ShapeDtypeStruct((4 * width, total), BF),
            jax.ShapeDtypeStruct((total, hidden_width), BF),
            jax.ShapeDtypeStruct((8, 4 * width), F32),
        ],
        compiler_params=params(12 if resident else 22),
        cost_estimate=pl.CostEstimate(
            flops=8 * total * table_rows * width,
            bytes_accessed=2 * total * table_rows + 4 * table_rows * width,
            transcendentals=0,
        ),
        name="pick_rows",
    )(rows, own, peer, *weights)


def stats_kernel(chunks, *refs):
    pairs, columns = refs[: 2 * chunks], refs[2 * chunks : 3 * chunks]
    keep_ref, send_ref, total = refs[3 * chunks :]
    width = columns[0].shape[1] // 4
    rows = total.shape[0]
    mean = 0.0
    first = 0
    for i in range(chunks):
        value = pairs[2 * i][...].astype(F32) + pairs[2 * i + 1][...].astype(F32)
        total[first : first + value.shape[0], :] = value
        mean = mean + jnp.sum(value, axis=0, keepdims=True)
        first += value.shape[0]
    mean = mean / rows
    gap = total[...] - mean
    square = jnp.sum(gap * gap, axis=0, keepdims=True)
    column = jnp.sum(sum(c[...] for c in columns), axis=0, keepdims=True)
    pad = jnp.zeros((4, mean.shape[1]), F32)
    lanes = mean.shape[1] - width
    for ref, first in ((keep_ref, 0), (send_ref, 2)):
        parts = [column[:, (first + j) * width : (first + j + 1) * width] for j in range(2)]
        if lanes:
            parts = [jnp.concatenate([p, jnp.zeros((1, lanes), F32)], axis=1) for p in parts]
        ref[...] = jnp.concatenate([mean, square, *parts, pad], axis=0)


def join_kernel(count, mine_ref, other_ref, out_ref):
    mine, other = mine_ref[...], other_ref[...]
    gap = mine[0:1] - other[0:1]
    out_ref[...] = jnp.concatenate(
        [
            (mine[0:1] + other[0:1]) * 0.5,
            mine[1:2] + other[1:2] + gap * gap * (count * 0.5),
            mine[2:] + other[2:],
        ],
        axis=0,
    )


def joined(mine, other, count):
    return pl.pallas_call(
        functools.partial(join_kernel, count),
        in_specs=[VMEM, VMEM],
        out_specs=VMEM,
        out_shape=jax.ShapeDtypeStruct(mine.shape, mine.dtype),
        compiler_params=params(1),
        name="join",
    )(mine, other)


def middle_kernel(
    chunks,
    slots,
    row_total,
    batches,
    *refs,
):
    place = here()
    pairs, acrosses = refs[: 2 * chunks], refs[2 * chunks : 3 * chunks]
    chips = len(refs) - 3 * chunks - 12
    grad_parts = refs[3 * chunks : 3 * chunks + chips]
    (
        stats_ref,
        gain_ref,
        shift_ref,
        upper_self_ref,
        upper_neigh_ref,
        embed_ref,
        keep_ref,
        send_ref,
        sums_ref,
        both,
        embed_all,
        grad_all,
    ) = refs[3 * chunks + chips :]
    own_seeds, hidden_width = grad_parts[0].shape
    seeds = own_seeds * chips
    width = acrosses[0].shape[0] // 4
    for mask, part in enumerate(grad_parts):
        at = pl.multiple_of((place[0] ^ mask) * own_seeds, own_seeds)
        grad_all[pl.ds(at, own_seeds), :] = part[...].astype(F32)
    fan_one = slots - 1
    mean = stats_ref[0:1, :]
    inv_std = lax.rsqrt(stats_ref[1:2, :] / row_total + 1e-05)
    gain, shift = gain_ref[...], shift_ref[...]
    grad = grad_all[...].astype(BF)
    d_self = dot(grad, upper_self_ref[...], ((1,), (1,)))
    d_mean = dot(grad, upper_neigh_ref[...], ((1,), (1,))) / fan_one
    gain_sum = shift_sum = hidden_sum = own_rows = None
    places = [(i, k) for i in range(chunks) for k in range(pairs[2 * i].shape[0] // seeds)]
    for slot, (i, k) in enumerate(places):
        span = slice(k * seeds, (k + 1) * seeds)
        pre_act = pairs[2 * i][span, :].astype(F32) + pairs[2 * i + 1][span, :].astype(F32)
        span = slice(slot * seeds, (slot + 1) * seeds)
        normed = (pre_act - mean) * inv_std
        shifted = gain * normed + shift
        sigmoid_v = 1.0 / (1.0 + jnp.exp(-shifted))
        hidden = (shifted * sigmoid_v).astype(BF)
        if slot == 0:
            own_rows = hidden
        else:
            hidden_sum = hidden.astype(F32) + (0.0 if hidden_sum is None else hidden_sum)
        grad_hidden = d_self if slot == 0 else d_mean
        grad_shifted = grad_hidden * sigmoid_v * (1.0 + shifted * (1.0 - sigmoid_v))
        gain_part = grad_shifted * normed
        gain_sum = gain_part if gain_sum is None else gain_sum + gain_part
        shift_sum = grad_shifted if shift_sum is None else shift_sum + grad_shifted
        both[span, :hidden_width] = grad_shifted.astype(BF)
        both[span, hidden_width:] = normed.astype(BF)
    hidden_mean = (hidden_sum / fan_one).astype(BF)
    embed_all[...] = dot(own_rows, upper_self_ref[...]) + dot(hidden_mean, upper_neigh_ref[...])
    start = pl.multiple_of(place[0] * own_seeds, own_seeds)
    embed_ref[...] = embed_all[pl.ds(start, own_seeds), :].astype(BF)
    upper_self_part = dot(own_rows, grad, ((0,), (0,)))
    upper_neigh_part = dot(hidden_mean, grad, ((0,), (0,)))
    first_core = place[1] == 0
    upper_keep = jnp.where(first_core, upper_self_part, upper_neigh_part)
    upper_send = jnp.where(first_core, upper_neigh_part, upper_self_part)
    gain_high, gain_low = halves(jnp.sum(gain_sum, axis=0, keepdims=True))
    shift_high, shift_low = halves(jnp.sum(shift_sum, axis=0, keepdims=True))
    sums = [gain_high, gain_low, shift_high, shift_low]
    sums = jnp.concatenate(
        [s.astype(F32) for s in sums] + [jnp.zeros((12, hidden_width), F32)], axis=0
    ).astype(BF)
    sums_ref[...] = sums
    per_group = keep_ref.shape[1]
    send_ref[batches * per_group :, :] = sums
    lower = None
    first = 0
    for a in acrosses:
        part = dot(a[...], both[first : first + a.shape[1], :])
        lower = part if lower is None else lower + part
        first += a.shape[1]
    piece, upper_piece = width // batches, hidden_width // batches
    for block, upper in ((0, upper_keep), (2, upper_send)):
        for d in range(batches):
            parts = []
            for lane in (0, hidden_width):
                for j in (0, 1):
                    row = (block + j) * width + d * piece
                    parts.append(lower[row : row + piece, lane : lane + hidden_width])
            parts.append(upper[d * upper_piece : (d + 1) * upper_piece, :])
            value = jnp.concatenate(parts, axis=0)
            if block == 0:
                keep_ref[d, :, :] = value
            else:
                send_ref[d * per_group : (d + 1) * per_group, :] = value.astype(BF)


def joined_sums(mine, theirs):
    sums = []
    for j in (0, 2):
        sums += halves((mine[j : j + 1] + mine[j + 1 : j + 2]) + (theirs[j : j + 1] + theirs[j + 1 : j + 2]))
    fill = jnp.zeros((12, mine.shape[1]), F32)
    return jnp.concatenate([s.astype(F32) for s in sums] + [fill], axis=0)


def merge_kernel(
    orders, keep_ref, got_ref, sums_ref, kept_ref, sent_ref, tail_ref
):
    place = here()
    batches, rows, _ = keep_ref.shape
    got_sums = got_ref[batches * rows :, :].astype(F32)
    tail = joined_sums(sums_ref[...].astype(F32), got_sums).astype(BF)
    half = batches // 2
    for i in range(batches):
        d = place[2] ^ jnp.where(place[1] == 0, orders[0][i], orders[1][i])
        at = pl.multiple_of(d * rows, rows)
        value = keep_ref[d, :, :] + got_ref[pl.ds(at, rows), :].astype(F32)
        if i < half:
            kept_ref[i, :, :] = value
        else:
            sent_ref[(i - half) * rows : (i - half + 1) * rows, :] = value.astype(BF)
    sent_ref[half * rows :, :] = tail
    tail_ref[...] = tail


def halve_kernel(keep_ref, got_ref, tail_ref, kept_ref, sent_ref, new_tail_ref):
    pieces, rows, _ = keep_ref.shape
    half = pieces // 2
    got_tail = got_ref[pieces * rows :, :].astype(F32)
    tail = joined_sums(tail_ref[...].astype(F32), got_tail).astype(BF)
    for i in range(pieces):
        value = keep_ref[i, :, :] + got_ref[i * rows : (i + 1) * rows, :].astype(F32)
        if i < half:
            kept_ref[i, :, :] = value
        else:
            sent_ref[(i - half) * rows : (i - half + 1) * rows, :] = value.astype(BF)
    sent_ref[half * rows :, :] = tail
    new_tail_ref[...] = tail


def both_kernel(keep_ref, got_ref, tail_ref, sent_ref, new_tail_ref):
    pieces, rows, _ = keep_ref.shape
    got_tail = got_ref[pieces * rows :, :].astype(F32)
    tail = joined_sums(tail_ref[...].astype(F32), got_tail).astype(BF)
    for i in range(pieces):
        value = keep_ref[i, :, :] + got_ref[i * rows : (i + 1) * rows, :].astype(F32)
        sent_ref[i * rows : (i + 1) * rows, :] = value.astype(BF)
    sent_ref[pieces * rows :, :] = tail
    new_tail_ref[...] = tail


def finish_kernel(
    row_total, sent_ref, got_ref, tail_ref, stats_ref, gain_ref, column_ref, out_ref, sums_ref
):
    rows = (sent_ref.shape[0] - 16) // 2
    sums = joined_sums(tail_ref[...].astype(F32), got_ref[2 * rows :, :].astype(F32))
    pieces = column_ref.shape[2]
    grad_gain = sums[0:1] + sums[1:2]
    grad_shift = sums[2:3] + sums[3:4]
    scale = gain_ref[...] * lax.rsqrt(stats_ref[1:2, :] / row_total + 1e-05)
    shift_part = jnp.broadcast_to(grad_shift / row_total, (8, grad_shift.shape[1]))
    for i in range(2):
        mine = sent_ref[i * rows : (i + 1) * rows, :].astype(F32)
        total = mine + got_ref[(1 - i) * rows : (2 - i) * rows, :].astype(F32)
        outer = dot(column_ref[i, :, :], shift_part, ((0,), (0,)), lax.Precision.HIGHEST)
        lower = scale * (
            total[:pieces] - outer - total[pieces : 2 * pieces] * (grad_gain / row_total)
        )
        out_ref[i, :, :] = jnp.concatenate([lower, total[2 * pieces : rows]], axis=0).astype(BF)
    sums_ref[...] = sums.astype(BF)


def upper_kernel(masks, parts_ref, sums_ref, upper_ref):
    place = here()
    rows = upper_ref.shape[0] - 16
    piece = rows // len(masks)
    for i, mask in enumerate(masks):
        at = pl.multiple_of((place[2] ^ mask) * piece, piece)
        upper_ref[pl.ds(at, piece), :] = parts_ref[i, parts_ref.shape[1] - piece :, :].astype(F32)
    upper_ref[rows:, :] = sums_ref[...].astype(F32)


def lower_kernel(masks, parts_ref, self_ref, neigh_ref):
    place = here()
    piece = self_ref.shape[0] // len(masks)
    for i, mask in enumerate(masks):
        at = pl.ds(pl.multiple_of((place[2] ^ mask) * piece, piece), piece)
        rows = parts_ref[i, :, :].astype(F32)
        self_ref[at, :] = rows[:piece]
        neigh_ref[at, :] = rows[piece : 2 * piece]


def last_kernel(mine_ref, other_ref, self_ref, neigh_ref, gain_ref, shift_ref):
    place = here()
    rows = self_ref.shape[0]
    first_core = place[1] == 0
    first = jnp.where(first_core, mine_ref[...], other_ref[...])
    self_ref[...] = first[:rows]
    neigh_ref[...] = jnp.where(first_core, other_ref[:rows, :], mine_ref[:rows, :])
    gain_ref[...] = first[rows : rows + 1] + first[rows + 1 : rows + 2]
    shift_ref[...] = first[rows + 2 : rows + 3] + first[rows + 3 : rows + 4]


def swap(value, axis, mask):
    return lax.ppermute(value, axis, [(i, i ^ mask) for i in range(lax.axis_size(axis))])


def on_device(
    node_feats,
    seed_ids,
    first_hop,
    second_hop,
    lower_self,
    lower_neighbour,
    norm_gain,
    norm_shift,
    upper_self,
    upper_neighbour,
    embed_grad,
):
    feats, batches = lax.axis_size("feat"), lax.axis_size("batch")
    chips = feats // 2
    feat, batch = lax.axis_index("feat"), lax.axis_index("batch")
    core, chip = feat % 2, feat // 2
    table_rows, width = node_feats.shape
    hidden_width = lower_self.shape[1]
    fan_one, fan_two = first_hop.shape[1], second_hop.shape[2]
    slots = fan_one + 1
    own_seeds = embed_grad.shape[0]
    seeds = own_seeds * chips
    row_total = own_seeds * slots * feats * batches
    rows = seeds * slots

    peer_feats = swap(node_feats, "feat", 1)
    peer_self = swap(lower_self, "feat", 1)
    peer_neigh = swap(lower_neighbour, "feat", 1)
    grads = [embed_grad] + [swap(embed_grad, "feat", 2 * mask) for mask in range(1, chips)]

    own_ids = jnp.concatenate([seed_ids[None, :], first_hop.T], axis=0)
    picks = build_rows(own_ids, second_hop.transpose(1, 2, 0), table_rows)

    weights = (lower_self, peer_self, lower_neighbour, peer_neigh)
    per_slot = seeds // LANES
    pairs, acrosses, columns = [], [], []
    first = 0
    for share in CHUNKS:
        across, pre_act, column = pick_rows(
            first * per_slot,
            share * per_slot,
            picks,
            node_feats,
            peer_feats,
            weights,
            per_slot,
            (fan_one, fan_two),
        )
        acrosses.append(across)
        columns.append(column)
        mask = 2
        other = swap(pre_act, "feat", mask)
        while 2 * mask < feats:
            mask *= 2
            pre_act = (pre_act.astype(F32) + other.astype(F32)).astype(BF)
            other = swap(pre_act, "feat", mask)
        pairs += [pre_act, other]
        first += share

    tile = jax.ShapeDtypeStruct((8, hidden_width), F32)
    keep, send = pl.pallas_call(
        functools.partial(stats_kernel, len(CHUNKS)),
        out_shape=[tile, tile],
        scratch_shapes=[pltpu.VMEM((rows, hidden_width), F32)],
        compiler_params=params(16),
        name="stats",
    )(*pairs, *columns)

    count = float(rows)
    stats = joined(keep, swap(send, "feat", 1), count)
    mask = 1
    while mask < batches:
        count *= 2
        stats = joined(stats, swap(stats, "batch", mask), count)
        mask *= 2

    gain_row, shift_row = norm_gain[None, :], norm_shift[None, :]
    per_group = 4 * width // batches + hidden_width // batches
    operands = [
        *pairs,
        *acrosses,
        *grads,
        stats,
        gain_row,
        shift_row,
        upper_self,
        upper_neighbour,
    ]
    embedding, keep, send, sums = pl.pallas_call(
        functools.partial(middle_kernel, len(CHUNKS), slots, row_total, batches),
        in_specs=[VMEM] * len(operands),
        out_shape=[
            jax.ShapeDtypeStruct((own_seeds, hidden_width), BF),
            jax.ShapeDtypeStruct((batches, per_group, hidden_width), F32),
            jax.ShapeDtypeStruct((batches * per_group + 16, hidden_width), BF),
            jax.ShapeDtypeStruct((16, hidden_width), BF),
        ],
        scratch_shapes=[
            pltpu.VMEM((rows, 2 * hidden_width), BF),
            pltpu.VMEM((seeds, hidden_width), F32),
            pltpu.VMEM((seeds, hidden_width), F32),
        ],
        compiler_params=params(24),
        name="middle",
    )(*operands)

    bits = [1 << i for i in range(batches.bit_length() - 1)]
    rounds = (bits, bits[1::-1] + bits[2:])

    def order_of(masks):
        order = [0]
        for mask in reversed(masks):
            order = order + [i ^ mask for i in order]
        return order

    def kept_and_sent(pieces):
        return [
            jax.ShapeDtypeStruct((pieces, per_group, hidden_width), F32),
            jax.ShapeDtypeStruct((pieces * per_group + 16, hidden_width), BF),
            jax.ShapeDtypeStruct((16, hidden_width), BF),
        ]

    def exchange(value, step):
        pairs = [
            (f * batches + b, f * batches + (b ^ rounds[f % 2][step]))
            for f in range(feats)
            for b in range(batches)
        ]
        return lax.ppermute(value, ("feat", "batch"), pairs)

    pieces = batches // 2
    kept, sent, tail = pl.pallas_call(
        functools.partial(merge_kernel, [order_of(masks) for masks in rounds]),
        in_specs=[VMEM] * 3,
        out_shape=kept_and_sent(pieces),
        compiler_params=params(16),
        name="merge",
    )(keep, swap(send, "feat", 1), sums)
    got = exchange(sent, 0)
    for step in range(1, len(bits) - 1):
        pieces //= 2
        kept, sent, tail = pl.pallas_call(
            halve_kernel,
            out_shape=kept_and_sent(pieces),
            compiler_params=params(16),
            name="halve",
        )(kept, got, tail)
        got = exchange(sent, step)
    sent, tail = pl.pallas_call(
        both_kernel,
        out_shape=kept_and_sent(pieces)[1:],
        compiler_params=params(16),
        name="both",
    )(kept, got, tail)
    got = exchange(sent, len(bits) - 1)

    piece = width // batches
    columns = []
    for mask in (0, batches // 2):
        at = (0, (batch ^ mask) * piece)
        columns.append(lax.dynamic_slice(stats[2:4], at, (2, piece)).reshape(1, 1, 2 * piece))
    column = jnp.pad(jnp.concatenate(columns, axis=0), ((0, 0), (0, 7), (0, 0)))
    out_rows = 2 * piece + hidden_width // batches
    done, sums = pl.pallas_call(
        functools.partial(finish_kernel, row_total),
        out_shape=[
            jax.ShapeDtypeStruct((2, out_rows, hidden_width), BF),
            jax.ShapeDtypeStruct((16, hidden_width), BF),
        ],
        compiler_params=params(16),
        name="finish",
    )(sent, got, tail, stats, gain_row, column)

    gathered, masks = done, [0, batches // 2]
    mask = batches // 4
    while mask:
        gathered = jnp.concatenate([gathered, swap(gathered, "batch", mask)], axis=0)
        masks += [m ^ mask for m in masks]
        mask //= 2
    square = jax.ShapeDtypeStruct((hidden_width, hidden_width), F32)
    tall = jax.ShapeDtypeStruct((width, hidden_width), F32)
    line = jax.ShapeDtypeStruct((1, hidden_width), F32)
    upper = pl.pallas_call(
        functools.partial(upper_kernel, tuple(masks)),
        in_specs=[VMEM, VMEM],
        out_shape=jax.ShapeDtypeStruct((hidden_width + 16, hidden_width), F32),
        compiler_params=params(4),
        name="upper",
    )(gathered, sums)
    upper_other = swap(upper, "feat", 1)
    grad_self, grad_neigh = pl.pallas_call(
        functools.partial(lower_kernel, tuple(masks)),
        in_specs=[VMEM],
        out_shape=[tall, tall],
        compiler_params=params(4),
        cost_estimate=pl.CostEstimate(
            flops=0, bytes_accessed=12 * width * hidden_width, transcendentals=0
        ),
        name="lower",
    )(gathered)
    grad_upper_self, grad_upper_neigh, grad_gain, grad_shift = pl.pallas_call(
        last_kernel,
        in_specs=[VMEM, VMEM],
        out_shape=[square, square, line, line],
        compiler_params=params(4),
        name="last",
    )(upper, upper_other)
    return (
        embedding,
        grad_self,
        grad_neigh,
        grad_upper_self,
        grad_upper_neigh,
        grad_gain[0],
        grad_shift[0],
    )


CHUNKS = (2, 3, 3, 3)


def solution(mesh):
    return jax.shard_map(
        on_device,
        mesh=mesh,
        in_specs=(
            P("batch", "feat"),
            P("batch"),
            P("batch", None),
            P("batch", None, None),
            P("feat", None),
            P("feat", None),
            P(),
            P(),
            P(),
            P(),
            P(("batch", "feat"), None),
        ),
        out_specs=(
            P(("batch", "feat"), None),
            P("feat", None),
            P("feat", None),
            P(),
            P(),
            P(),
            P(),
        ),
        check_vma=False,
    )
```

```python
import functools

import jax
import jax.numpy as jnp
from jax import lax
from jax.experimental import pallas as pl
from jax.experimental.pallas import tpu as pltpu
from jax.sharding import PartitionSpec as P

BF = jnp.bfloat16
F32 = jnp.float32
LANES = 128
LOW = 256
SLOT = 16
GROUP = LOW // SLOT
MIB = 2**20


def dot(left, right, dims=((1,), (0,)), precision=None):
    return lax.dot_general(
        left, right, (dims, ((), ())), preferred_element_type=F32, precision=precision
    )


def params(mib):
    return pltpu.CompilerParams(vmem_limit_bytes=mib * MIB)


VMEM = pl.BlockSpec(memory_space=pltpu.VMEM)


def here():
    feat = lax.axis_index("feat")
    return lax.shift_right_logical(feat, 1), jnp.bitwise_and(feat, 1), lax.axis_index("batch")


def halves(value):
    high = value.astype(BF)
    return high, (value - high.astype(F32)).astype(BF)


def build_kernel(
    own_ref,
    far_ref,
    out_ref,
    keys,
    own_group,
    spread,
    own_slot,
):
    place = here()
    groups = LANES // GROUP
    per_slot = own_ref.shape[1] // (2 * LANES)
    step, steps = pl.program_id(0), pl.num_programs(0)
    first_core = place[1] == 0

    def mine(ids, p):
        parts = []
        for q in range(per_slot):
            left = ids[:, 2 * q * LANES : (2 * q + 1) * LANES]
            right = ids[:, (2 * q + 1) * LANES : (2 * q + 2) * LANES]
            low_half = lax.broadcasted_iota(jnp.int32, left.shape, 1) < LANES // 2
            even = jnp.where(low_half, left, pltpu.roll(right, LANES // 2, 1))
            odd = jnp.where(low_half, pltpu.roll(left, LANES // 2, 1), right)
            parts.append(jnp.where(first_core, even, odd))
        part = parts[0]
        for q in range(1, per_slot):
            part = jnp.where(p == q, parts[q], part)
        return part

    def flag(shape, test):
        row = lax.broadcasted_iota(jnp.int32, shape, 0)
        lane = lax.broadcasted_iota(jnp.int32, shape, 1)
        return jnp.where(test(row, lane), 1.0, 0.0).astype(BF)

    def widen(part):
        tiled = jnp.concatenate([part.astype(F32).astype(BF)] * groups, axis=0) * own_group[...]
        return dot(tiled, spread[...]).astype(BF) * own_slot[...]

    def wide_of(ids, self_row, p):
        part = mine(ids, p)
        gap = SLOT - part.shape[0]
        part = jnp.concatenate([part, jnp.full((gap, LANES), -1, jnp.int32)], axis=0)
        own = mine(jnp.broadcast_to(self_row, (8, self_row.shape[1])), p).astype(F32)
        high = widen(lax.shift_right_arithmetic(part, 8))
        return high, widen(jnp.bitwise_and(part, LOW - 1)), jnp.concatenate([own, own], axis=1)

    def keys_of(high, low, own):
        gather = flag((groups, LANES), lambda r, c: r == c // SLOT)
        in_group = (lax.broadcasted_iota(jnp.int32, (groups, LOW), 1) % GROUP).astype(F32)
        return dot(gather, high) * GROUP + in_group, dot(gather, low), own

    def keep(values, at):
        for j, value in enumerate(values):
            keys[at, j, :, :] = value

    @pl.when(step == 0)
    def _():
        own_group[...] = flag((LANES, LANES), lambda r, c: r // SLOT == c // GROUP)
        spread[...] = flag((LANES, LOW), lambda r, c: r % GROUP == c % GROUP)
        own_slot[...] = flag((LANES, LOW), lambda r, c: r % SLOT == c // GROUP)
        keep(keys_of(*wide_of(own_ref[1:, :], own_ref[0:1, :], 0)), 0)

    now = step % 2
    later = jnp.minimum(step + 1, steps - 1)
    slot = later // per_slot
    back = jnp.maximum(slot - 1, 0)
    ids = far_ref[back, :, :]
    self_row = own_ref[pl.ds(back + 1, 1), :]
    if per_slot > 1:
        padded = jnp.concatenate(
            [own_ref[1:, :], jnp.full((ids.shape[0] + 1 - own_ref.shape[0], ids.shape[1]), -1, jnp.int32)]
        )
        ids = jnp.where(slot == 0, padded, ids)
        self_row = jnp.where(slot == 0, own_ref[0:1, :], self_row)
    later_wide = wide_of(ids, self_row, later % per_slot)

    index = lax.broadcasted_iota(jnp.int32, (LOW, LOW), 0).astype(BF)
    one = jnp.ones((LOW, LOW), BF)
    zero = jnp.zeros((LOW, LOW), BF)
    def store(g, counts):
        counts = counts.astype(BF)
        for h in range(LOW // GROUP):
            out_ref[g * GROUP : (g + 1) * GROUP, h * LOW : (h + 1) * LOW] = counts[
                h * GROUP : (h + 1) * GROUP, :
            ]

    lanes = lax.broadcasted_iota(jnp.int32, (LANES, LANES), 1)
    ids = jnp.broadcast_to(keys[now, 2, 0:1, :LANES], (LANES, LANES)).T.astype(jnp.int32)
    low = jnp.bitwise_and(ids, LOW - 1)
    high = lax.shift_right_logical(ids, 8).astype(BF)
    bases = [
        jnp.where(lanes + LANES * part == low, 1.0, 0.0).astype(BF) for part in range(LOW // LANES)
    ]
    tiles = [(h, part) for h in range(out_ref.shape[1] // LOW) for part in range(LOW // LANES)]
    share = -(-len(tiles) // groups)
    waiting = []
    later_keys = None
    for g in range(groups):
        left = jnp.where(index == keys[now, 0, g : g + 1, :].astype(BF), one, zero)
        right = jnp.where(index == keys[now, 1, g : g + 1, :].astype(BF), one, zero)
        waiting.append((g, dot(left, right, ((1,), (1,)))))
        if g == 6:
            later_keys = keys_of(*later_wide)
        for h, part in tiles[g * share : (g + 1) * share]:
            at = h * LOW + part * LANES
            out_ref[LANES:, at : at + LANES] = jnp.where(
                high == BF(h), bases[part], jnp.zeros_like(bases[part])
            )
        if len(waiting) > 1:
            store(*waiting.pop(0))
    for item in waiting:
        store(*item)
    keep(later_keys, 1 - now)


def build_rows(own, far, table_rows):
    steps = own.shape[0] * own.shape[1] // (2 * LANES)
    groups = LANES // GROUP
    return pl.pallas_call(
        build_kernel,
        grid=(steps,),
        in_specs=[VMEM, VMEM],
        out_specs=pl.BlockSpec((2 * LANES, table_rows), lambda i: (i, 0)),
        out_shape=jax.ShapeDtypeStruct((steps * 2 * LANES, table_rows), BF),
        scratch_shapes=[
            pltpu.VMEM((2, 3, groups, LOW), F32),
            pltpu.VMEM((LANES, LANES), BF),
            pltpu.VMEM((LANES, LOW), BF),
            pltpu.VMEM((LANES, LOW), BF),
        ],
        compiler_params=params(12),
        cost_estimate=pl.CostEstimate(
            flops=2 * steps * groups * LOW**3,
            bytes_accessed=4 * steps * LANES * table_rows,
            transcendentals=0,
        ),
        name="build_rows",
    )(own, far)


def pick_kernel(
    first_block,
    start,
    blocks,
    per_slot,
    fans,
    rows_ref,
    own_ref,
    peer_ref,
    self_own_ref,
    self_peer_ref,
    neigh_own_ref,
    neigh_peer_ref,
    across_ref,
    pre_ref,
    column_ref,
):
    width = own_ref.shape[1]
    step = pl.program_id(0)
    tables = (own_ref, peer_ref)
    picked = [
        [dot(rows_ref[at : at + 2 * LANES, :], table[...]) for table in tables]
        for at in range(start, start + 2 * blocks * LANES, 2 * LANES)
    ]
    total = None
    columns = []
    for i in range(2):
        self_parts, neigh_parts = [], []
        for b in range(blocks):
            block = first_block + step * blocks + b
            share = jnp.where(block < per_slot, F32(1.0 / fans[0]), F32(1.0 / fans[1]))
            neigh_parts.append((picked[b][i][:LANES] * share).astype(BF))
            self_parts.append(picked[b][i][LANES:].astype(BF))
        weights = ((self_own_ref, neigh_own_ref), (self_peer_ref, neigh_peer_ref))[i]
        for j, parts in enumerate((self_parts, neigh_parts)):
            part = dot(jnp.concatenate(parts, axis=0), weights[j][...])
            total = part if total is None else total + part
            columns.append(
                sum(jnp.sum(p.astype(F32).reshape(-1, 8, width), axis=0) for p in parts)
            )
            for b in range(blocks):
                across_ref[
                    (2 * i + j) * width : (2 * i + j + 1) * width, b * LANES : (b + 1) * LANES
                ] = parts[b].T
    pre_ref[...] = total.astype(BF)
    columns = jnp.concatenate(columns, axis=1)

    @pl.when(step == 0)
    def _():
        column_ref[...] = columns

    @pl.when(step > 0)
    def _():
        column_ref[...] += columns


def pick_rows(first_block, count, rows, own, peer, weights, per_slot, fans):
    table_rows, width = own.shape
    hidden_width = weights[0].shape[1]
    total = count * LANES
    resident = rows.size * 2 <= 32 * MIB
    if resident:
        blocks, start, rows_spec = count, first_block * 2 * LANES, VMEM
    else:
        blocks, start = per_slot, 0
        skip = first_block // blocks
        rows_spec = pl.BlockSpec((blocks * 2 * LANES, table_rows), lambda i: (i + skip, 0))
    return pl.pallas_call(
        functools.partial(pick_kernel, first_block, start, blocks, per_slot, fans),
        grid=(count // blocks,),
        in_specs=[rows_spec] + [VMEM] * 6,
        out_specs=[
            pl.BlockSpec((4 * width, blocks * LANES), lambda i: (0, i)),
            pl.BlockSpec((blocks * LANES, hidden_width), lambda i: (i, 0)),
            pl.BlockSpec((8, 4 * width), lambda i: (0, 0)),
        ],
        out_shape=[
            jax.ShapeDtypeStruct((4 * width, total), BF),
            jax.ShapeDtypeStruct((total, hidden_width), BF),
            jax.ShapeDtypeStruct((8, 4 * width), F32),
        ],
        compiler_params=params(12 if resident else 22),
        cost_estimate=pl.CostEstimate(
            flops=8 * total * table_rows * width,
            bytes_accessed=2 * total * table_rows + 4 * table_rows * width,
            transcendentals=0,
        ),
        name="pick_rows",
    )(rows, own, peer, *weights)


def stats_kernel(chunks, *refs):
    pairs, columns = refs[: 2 * chunks], refs[2 * chunks : 3 * chunks]
    keep_ref, send_ref, total = refs[3 * chunks :]
    width = columns[0].shape[1] // 4
    rows = total.shape[0]
    mean = 0.0
    first = 0
    for i in range(chunks):
        value = pairs[2 * i][...].astype(F32) + pairs[2 * i + 1][...].astype(F32)
        total[first : first + value.shape[0], :] = value
        mean = mean + jnp.sum(value, axis=0, keepdims=True)
        first += value.shape[0]
    mean = mean / rows
    gap = total[...] - mean
    square = jnp.sum(gap * gap, axis=0, keepdims=True)
    column = jnp.sum(sum(c[...] for c in columns), axis=0, keepdims=True)
    pad = jnp.zeros((4, mean.shape[1]), F32)
    lanes = mean.shape[1] - width
    for ref, first in ((keep_ref, 0), (send_ref, 2)):
        parts = [column[:, (first + j) * width : (first + j + 1) * width] for j in range(2)]
        if lanes:
            parts = [jnp.concatenate([p, jnp.zeros((1, lanes), F32)], axis=1) for p in parts]
        ref[...] = jnp.concatenate([mean, square, *parts, pad], axis=0)


def join_kernel(count, mine_ref, other_ref, out_ref):
    mine, other = mine_ref[...], other_ref[...]
    gap = mine[0:1] - other[0:1]
    out_ref[...] = jnp.concatenate(
        [
            (mine[0:1] + other[0:1]) * 0.5,
            mine[1:2] + other[1:2] + gap * gap * (count * 0.5),
            mine[2:] + other[2:],
        ],
        axis=0,
    )


def joined(mine, other, count):
    return pl.pallas_call(
        functools.partial(join_kernel, count),
        in_specs=[VMEM, VMEM],
        out_specs=VMEM,
        out_shape=jax.ShapeDtypeStruct(mine.shape, mine.dtype),
        compiler_params=params(1),
        name="join",
    )(mine, other)


def middle_kernel(
    chunks,
    slots,
    row_total,
    batches,
    *refs,
):
    place = here()
    pairs, acrosses = refs[: 2 * chunks], refs[2 * chunks : 3 * chunks]
    chips = len(refs) - 3 * chunks - 12
    grad_parts = refs[3 * chunks : 3 * chunks + chips]
    (
        stats_ref,
        gain_ref,
        shift_ref,
        upper_self_ref,
        upper_neigh_ref,
        embed_ref,
        keep_ref,
        send_ref,
        sums_ref,
        both,
        embed_all,
        grad_all,
    ) = refs[3 * chunks + chips :]
    own_seeds, hidden_width = grad_parts[0].shape
    seeds = own_seeds * chips
    width = acrosses[0].shape[0] // 4
    for mask, part in enumerate(grad_parts):
        at = pl.multiple_of((place[0] ^ mask) * own_seeds, own_seeds)
        grad_all[pl.ds(at, own_seeds), :] = part[...].astype(F32)
    fan_one = slots - 1
    mean = stats_ref[0:1, :]
    inv_std = lax.rsqrt(stats_ref[1:2, :] / row_total + 1e-05)
    gain, shift = gain_ref[...], shift_ref[...]
    grad = grad_all[...].astype(BF)
    d_self = dot(grad, upper_self_ref[...], ((1,), (1,)))
    d_mean = dot(grad, upper_neigh_ref[...], ((1,), (1,))) / fan_one
    gain_sum = shift_sum = hidden_sum = own_rows = None
    places = [(i, k) for i in range(chunks) for k in range(pairs[2 * i].shape[0] // seeds)]
    for slot, (i, k) in enumerate(places):
        span = slice(k * seeds, (k + 1) * seeds)
        pre_act = pairs[2 * i][span, :].astype(F32) + pairs[2 * i + 1][span, :].astype(F32)
        span = slice(slot * seeds, (slot + 1) * seeds)
        normed = (pre_act - mean) * inv_std
        shifted = gain * normed + shift
        sigmoid_v = 1.0 / (1.0 + jnp.exp(-shifted))
        hidden = (shifted * sigmoid_v).astype(BF)
        if slot == 0:
            own_rows = hidden
        else:
            hidden_sum = hidden.astype(F32) + (0.0 if hidden_sum is None else hidden_sum)
        grad_hidden = d_self if slot == 0 else d_mean
        grad_shifted = grad_hidden * sigmoid_v * (1.0 + shifted * (1.0 - sigmoid_v))
        gain_part = grad_shifted * normed
        gain_sum = gain_part if gain_sum is None else gain_sum + gain_part
        shift_sum = grad_shifted if shift_sum is None else shift_sum + grad_shifted
        both[span, :hidden_width] = grad_shifted.astype(BF)
        both[span, hidden_width:] = normed.astype(BF)
    hidden_mean = (hidden_sum / fan_one).astype(BF)
    embed_all[...] = dot(own_rows, upper_self_ref[...]) + dot(hidden_mean, upper_neigh_ref[...])
    start = pl.multiple_of(place[0] * own_seeds, own_seeds)
    embed_ref[...] = embed_all[pl.ds(start, own_seeds), :].astype(BF)
    upper_self_part = dot(own_rows, grad, ((0,), (0,)))
    upper_neigh_part = dot(hidden_mean, grad, ((0,), (0,)))
    first_core = place[1] == 0
    upper_keep = jnp.where(first_core, upper_self_part, upper_neigh_part)
    upper_send = jnp.where(first_core, upper_neigh_part, upper_self_part)
    gain_high, gain_low = halves(jnp.sum(gain_sum, axis=0, keepdims=True))
    shift_high, shift_low = halves(jnp.sum(shift_sum, axis=0, keepdims=True))
    sums = [gain_high, gain_low, shift_high, shift_low]
    sums = jnp.concatenate(
        [s.astype(F32) for s in sums] + [jnp.zeros((12, hidden_width), F32)], axis=0
    ).astype(BF)
    sums_ref[...] = sums
    per_group = keep_ref.shape[1]
    send_ref[batches * per_group :, :] = sums
    lower = None
    first = 0
    for a in acrosses:
        part = dot(a[...], both[first : first + a.shape[1], :])
        lower = part if lower is None else lower + part
        first += a.shape[1]
    piece, upper_piece = width // batches, hidden_width // batches
    for block, upper in ((0, upper_keep), (2, upper_send)):
        for d in range(batches):
            parts = []
            for lane in (0, hidden_width):
                for j in (0, 1):
                    row = (block + j) * width + d * piece
                    parts.append(lower[row : row + piece, lane : lane + hidden_width])
            parts.append(upper[d * upper_piece : (d + 1) * upper_piece, :])
            value = jnp.concatenate(parts, axis=0)
            if block == 0:
                keep_ref[d, :, :] = value
            else:
                send_ref[d * per_group : (d + 1) * per_group, :] = value.astype(BF)


def joined_sums(mine, theirs):
    sums = []
    for j in (0, 2):
        sums += halves((mine[j : j + 1] + mine[j + 1 : j + 2]) + (theirs[j : j + 1] + theirs[j + 1 : j + 2]))
    fill = jnp.zeros((12, mine.shape[1]), F32)
    return jnp.concatenate([s.astype(F32) for s in sums] + [fill], axis=0)


def merge_kernel(
    orders, keep_ref, got_ref, sums_ref, kept_ref, sent_ref, tail_ref
):
    place = here()
    batches, rows, _ = keep_ref.shape
    got_sums = got_ref[batches * rows :, :].astype(F32)
    tail = joined_sums(sums_ref[...].astype(F32), got_sums).astype(BF)
    half = batches // 2
    for i in range(batches):
        d = place[2] ^ jnp.where(place[1] == 0, orders[0][i], orders[1][i])
        at = pl.multiple_of(d * rows, rows)
        value = keep_ref[d, :, :] + got_ref[pl.ds(at, rows), :].astype(F32)
        if i < half:
            kept_ref[i, :, :] = value
        else:
            sent_ref[(i - half) * rows : (i - half + 1) * rows, :] = value.astype(BF)
    sent_ref[half * rows :, :] = tail
    tail_ref[...] = tail


def halve_kernel(keep_ref, got_ref, tail_ref, kept_ref, sent_ref, new_tail_ref):
    pieces, rows, _ = keep_ref.shape
    half = pieces // 2
    got_tail = got_ref[pieces * rows :, :].astype(F32)
    tail = joined_sums(tail_ref[...].astype(F32), got_tail).astype(BF)
    for i in range(pieces):
        value = keep_ref[i, :, :] + got_ref[i * rows : (i + 1) * rows, :].astype(F32)
        if i < half:
            kept_ref[i, :, :] = value
        else:
            sent_ref[(i - half) * rows : (i - half + 1) * rows, :] = value.astype(BF)
    sent_ref[half * rows :, :] = tail
    new_tail_ref[...] = tail


def both_kernel(keep_ref, got_ref, tail_ref, sent_ref, new_tail_ref):
    pieces, rows, _ = keep_ref.shape
    got_tail = got_ref[pieces * rows :, :].astype(F32)
    tail = joined_sums(tail_ref[...].astype(F32), got_tail).astype(BF)
    for i in range(pieces):
        value = keep_ref[i, :, :] + got_ref[i * rows : (i + 1) * rows, :].astype(F32)
        sent_ref[i * rows : (i + 1) * rows, :] = value.astype(BF)
    sent_ref[pieces * rows :, :] = tail
    new_tail_ref[...] = tail


def finish_kernel(
    row_total, sent_ref, got_ref, tail_ref, stats_ref, gain_ref, column_ref, out_ref, sums_ref
):
    rows = (sent_ref.shape[0] - 16) // 2
    sums = joined_sums(tail_ref[...].astype(F32), got_ref[2 * rows :, :].astype(F32))
    pieces = column_ref.shape[2]
    grad_gain = sums[0:1] + sums[1:2]
    grad_shift = sums[2:3] + sums[3:4]
    scale = gain_ref[...] * lax.rsqrt(stats_ref[1:2, :] / row_total + 1e-05)
    shift_part = jnp.broadcast_to(grad_shift / row_total, (8, grad_shift.shape[1]))
    for i in range(2):
        mine = sent_ref[i * rows : (i + 1) * rows, :].astype(F32)
        total = mine + got_ref[(1 - i) * rows : (2 - i) * rows, :].astype(F32)
        outer = dot(column_ref[i, :, :], shift_part, ((0,), (0,)), lax.Precision.HIGHEST)
        lower = scale * (
            total[:pieces] - outer - total[pieces : 2 * pieces] * (grad_gain / row_total)
        )
        out_ref[i, :, :] = jnp.concatenate([lower, total[2 * pieces : rows]], axis=0).astype(BF)
    sums_ref[...] = sums.astype(BF)


def upper_kernel(masks, parts_ref, sums_ref, upper_ref):
    place = here()
    rows = upper_ref.shape[0] - 16
    piece = rows // len(masks[0])
    for i in range(len(masks[0])):
        mask = jnp.where(place[1] == 0, masks[0][i], masks[1][i])
        at = pl.multiple_of((place[2] ^ mask) * piece, piece)
        upper_ref[pl.ds(at, piece), :] = parts_ref[i, parts_ref.shape[1] - piece :, :]
    upper_ref[rows:, :] = sums_ref[...]


def lower_kernel(masks, parts_ref, self_ref, neigh_ref):
    place = here()
    piece = self_ref.shape[0] // len(masks[0])
    for i in range(len(masks[0])):
        mask = jnp.where(place[1] == 0, masks[0][i], masks[1][i])
        at = pl.ds(pl.multiple_of((place[2] ^ mask) * piece, piece), piece)
        rows = parts_ref[i, :, :].astype(F32)
        self_ref[at, :] = rows[:piece]
        neigh_ref[at, :] = rows[piece : 2 * piece]


def last_kernel(mine_ref, other_ref, self_ref, neigh_ref, gain_ref, shift_ref):
    place = here()
    rows = self_ref.shape[0]
    first_core = place[1] == 0
    mine, other = mine_ref[...].astype(F32), other_ref[...].astype(F32)
    first = jnp.where(first_core, mine, other)
    self_ref[...] = first[:rows]
    neigh_ref[...] = jnp.where(first_core, other[:rows], mine[:rows])
    gain_ref[...] = first[rows : rows + 1] + first[rows + 1 : rows + 2]
    shift_ref[...] = first[rows + 2 : rows + 3] + first[rows + 3 : rows + 4]


def swap(value, axis, mask):
    return lax.ppermute(value, axis, [(i, i ^ mask) for i in range(lax.axis_size(axis))])


def on_device(
    node_feats,
    seed_ids,
    first_hop,
    second_hop,
    lower_self,
    lower_neighbour,
    norm_gain,
    norm_shift,
    upper_self,
    upper_neighbour,
    embed_grad,
):
    feats, batches = lax.axis_size("feat"), lax.axis_size("batch")
    chips = feats // 2
    feat, batch = lax.axis_index("feat"), lax.axis_index("batch")
    core, chip = feat % 2, feat // 2
    table_rows, width = node_feats.shape
    hidden_width = lower_self.shape[1]
    fan_one, fan_two = first_hop.shape[1], second_hop.shape[2]
    slots = fan_one + 1
    own_seeds = embed_grad.shape[0]
    seeds = own_seeds * chips
    row_total = own_seeds * slots * feats * batches
    rows = seeds * slots

    peer_feats = swap(node_feats, "feat", 1)
    peer_self = swap(lower_self, "feat", 1)
    peer_neigh = swap(lower_neighbour, "feat", 1)
    grads = [embed_grad] + [swap(embed_grad, "feat", 2 * mask) for mask in range(1, chips)]

    own_ids = jnp.concatenate([seed_ids[None, :], first_hop.T], axis=0)
    picks = build_rows(own_ids, second_hop.transpose(1, 2, 0), table_rows)

    weights = (lower_self, peer_self, lower_neighbour, peer_neigh)
    per_slot = seeds // LANES
    pairs, acrosses, columns = [], [], []
    first = 0
    for share in CHUNKS:
        across, pre_act, column = pick_rows(
            first * per_slot,
            share * per_slot,
            picks,
            node_feats,
            peer_feats,
            weights,
            per_slot,
            (fan_one, fan_two),
        )
        acrosses.append(across)
        columns.append(column)
        mask = 2
        other = swap(pre_act, "feat", mask)
        while 2 * mask < feats:
            mask *= 2
            pre_act = (pre_act.astype(F32) + other.astype(F32)).astype(BF)
            other = swap(pre_act, "feat", mask)
        pairs += [pre_act, other]
        first += share

    tile = jax.ShapeDtypeStruct((8, hidden_width), F32)
    keep, send = pl.pallas_call(
        functools.partial(stats_kernel, len(CHUNKS)),
        out_shape=[tile, tile],
        scratch_shapes=[pltpu.VMEM((rows, hidden_width), F32)],
        compiler_params=params(16),
        name="stats",
    )(*pairs, *columns)

    count = float(rows)
    stats = joined(keep, swap(send, "feat", 1), count)
    mask = 1
    while mask < batches:
        count *= 2
        stats = joined(stats, swap(stats, "batch", mask), count)
        mask *= 2

    gain_row, shift_row = norm_gain[None, :], norm_shift[None, :]
    per_group = 4 * width // batches + hidden_width // batches
    operands = [
        *pairs,
        *acrosses,
        *grads,
        stats,
        gain_row,
        shift_row,
        upper_self,
        upper_neighbour,
    ]
    embedding, keep, send, sums = pl.pallas_call(
        functools.partial(middle_kernel, len(CHUNKS), slots, row_total, batches),
        in_specs=[VMEM] * len(operands),
        out_shape=[
            jax.ShapeDtypeStruct((own_seeds, hidden_width), BF),
            jax.ShapeDtypeStruct((batches, per_group, hidden_width), F32),
            jax.ShapeDtypeStruct((batches * per_group + 16, hidden_width), BF),
            jax.ShapeDtypeStruct((16, hidden_width), BF),
        ],
        scratch_shapes=[
            pltpu.VMEM((rows, 2 * hidden_width), BF),
            pltpu.VMEM((seeds, hidden_width), F32),
            pltpu.VMEM((seeds, hidden_width), F32),
        ],
        compiler_params=params(24),
        name="middle",
    )(*operands)

    bits = [1 << i for i in range(batches.bit_length() - 1)]
    rounds = (bits, bits[1::-1] + bits[2:])

    def order_of(masks):
        order = [0]
        for mask in reversed(masks):
            order = order + [i ^ mask for i in order]
        return order

    def kept_and_sent(pieces):
        return [
            jax.ShapeDtypeStruct((pieces, per_group, hidden_width), F32),
            jax.ShapeDtypeStruct((pieces * per_group + 16, hidden_width), BF),
            jax.ShapeDtypeStruct((16, hidden_width), BF),
        ]

    def exchange(value, step):
        pairs = [
            (f * batches + b, f * batches + (b ^ rounds[f % 2][step]))
            for f in range(feats)
            for b in range(batches)
        ]
        return lax.ppermute(value, ("feat", "batch"), pairs)

    pieces = batches // 2
    kept, sent, tail = pl.pallas_call(
        functools.partial(merge_kernel, [order_of(masks) for masks in rounds]),
        in_specs=[VMEM] * 3,
        out_shape=kept_and_sent(pieces),
        compiler_params=params(16),
        name="merge",
    )(keep, swap(send, "feat", 1), sums)
    got = exchange(sent, 0)
    for step in range(1, len(bits) - 1):
        pieces //= 2
        kept, sent, tail = pl.pallas_call(
            halve_kernel,
            out_shape=kept_and_sent(pieces),
            compiler_params=params(16),
            name="halve",
        )(kept, got, tail)
        got = exchange(sent, step)
    sent, tail = pl.pallas_call(
        both_kernel,
        out_shape=kept_and_sent(pieces)[1:],
        compiler_params=params(16),
        name="both",
    )(kept, got, tail)
    got = exchange(sent, len(bits) - 1)

    piece = width // batches
    columns = []
    for mask in (0, batches // 2):
        at = (0, (batch ^ mask) * piece)
        columns.append(lax.dynamic_slice(stats[2:4], at, (2, piece)).reshape(1, 1, 2 * piece))
    column = jnp.pad(jnp.concatenate(columns, axis=0), ((0, 0), (0, 7), (0, 0)))
    out_rows = 2 * piece + hidden_width // batches
    done, sums = pl.pallas_call(
        functools.partial(finish_kernel, row_total),
        out_shape=[
            jax.ShapeDtypeStruct((2, out_rows, hidden_width), BF),
            jax.ShapeDtypeStruct((16, hidden_width), BF),
        ],
        compiler_params=params(16),
        name="finish",
    )(sent, got, tail, stats, gain_row, column)

    gathered, masks = done, [[0, batches // 2], [0, batches // 2]]
    for step in range(len(bits) - 2, -1, -1):
        other = exchange(gathered, step)
        gathered = jnp.concatenate([gathered, other], axis=0)
        masks = [m + [k ^ rounds[c][step] for k in m] for c, m in enumerate(masks)]
    square = jax.ShapeDtypeStruct((hidden_width, hidden_width), F32)
    tall = jax.ShapeDtypeStruct((width, hidden_width), F32)
    line = jax.ShapeDtypeStruct((1, hidden_width), F32)
    upper = pl.pallas_call(
        functools.partial(upper_kernel, masks),
        in_specs=[VMEM, VMEM],
        out_shape=jax.ShapeDtypeStruct((hidden_width + 16, hidden_width), BF),
        compiler_params=params(4),
        name="upper",
    )(gathered, sums)
    upper_other = swap(upper, "feat", 1)
    grad_self, grad_neigh = pl.pallas_call(
        functools.partial(lower_kernel, masks),
        in_specs=[VMEM],
        out_shape=[tall, tall],
        compiler_params=params(4),
        cost_estimate=pl.CostEstimate(
            flops=0, bytes_accessed=12 * width * hidden_width, transcendentals=0
        ),
        name="lower",
    )(gathered)
    grad_upper_self, grad_upper_neigh, grad_gain, grad_shift = pl.pallas_call(
        last_kernel,
        in_specs=[VMEM, VMEM],
        out_shape=[square, square, line, line],
        compiler_params=params(4),
        name="last",
    )(upper, upper_other)
    return (
        embedding,
        grad_self,
        grad_neigh,
        grad_upper_self,
        grad_upper_neigh,
        grad_gain[0],
        grad_shift[0],
    )


CHUNKS = (4, 4, 3)


def solution(mesh):
    return jax.shard_map(
        on_device,
        mesh=mesh,
        in_specs=(
            P("batch", "feat"),
            P("batch"),
            P("batch", None),
            P("batch", None, None),
            P("feat", None),
            P("feat", None),
            P(),
            P(),
            P(),
            P(),
            P(("batch", "feat"), None),
        ),
        out_specs=(
            P(("batch", "feat"), None),
            P("feat", None),
            P("feat", None),
            P(),
            P(),
            P(),
            P(),
        ),
        check_vma=False,
    )
```
